128 devices in a mesh: lon: 16 (over y, z_hi, core), lat: 8 (over z_lo, x).
Axes of the slice: x: 4, y: 4, z: 4 (z_hi: 2, z_lo: 2; z = z_hi * 2 + z_lo), core: 2. Of those that a mesh axis runs over, the one named last changes fastest.
Arguments:
- temp: float32 [16, 1024, 4096], P(None, 'lat', 'lon'), may hold values from -6 to 6
- salt: float32 [16, 1024, 4096], P(None, 'lat', 'lon'), may hold values from -6 to 6
- east_face_velocity: float32 [16, 1024, 4096], P(None, 'lat', 'lon'), may hold values from -0.1 to 0.1
- v_face: float32 [16, 1024, 4096], P(None, 'lat', 'lon'), may hold values from -0.1 to 0.1
- kappa: float32 [16, 1024, 4096], P(None, 'lat', 'lon'), may hold values from 0.01 to 0.1
- land_mask: int32 [1024, 4096], P('lat', 'lon'), may hold values 0 or 1
- margin_owner_device: int32 [8, 16, 256, 2], P('lat', 'lon'), may hold values from 0 to 127, all different within a row; in each aligned block of 256 rows (0 to 255, 256 to 511, ..., all dimensions but the last counted through in order) at most 8 rows name the same one
- margin_cell: int32 [8, 16, 256, 2], P('lat', 'lon'), may hold values from 0 to 255
- margin_weight: float32 [8, 16, 256, 2], P('lat', 'lon'), may hold values from 0.2 to 1
- air_temp: float32 [16, 8, 256, 128], P('lon', 'lat'), may hold values from -6 to 6
- wind_speed: float32 [16, 8, 256, 128], P('lon', 'lat'), may hold values from 0.3 to 3
Outputs:
- temp_out: float32 [16, 1024, 4096], P(None, 'lat', 'lon')
- salt_out: float32 [16, 1024, 4096], P(None, 'lat', 'lon')
- density: float32 [16, 1024, 4096], P(None, 'lat', 'lon')
The draws below stay inside these ranges and needn't reach their ends.
Inputs may be any that keep to these rules, and one draw needn't show every extreme that they name: `margin_owner_device`: each block's 2 owners differ; among one device's 256 blocks no owner is named more than 8 times, a bound that some device reaches.
All inputs are finite; a program needn't handle non-finite values. No bound on the sum of `land_mask` on one device may be relied on, other than what follows from the above.
Results may differ from the reference program's by a relative error of at most 0.00002.
Values sent between devices are 32-bit elements; how exact they have to be, the bound alone decides.
No kernel may reach another device: no remote copies, remote signals or barrier semaphores. Data moves between devices by JAX's collectives and lax.ppermute only.
A program may use at most 192 MiB of HBM per device.

```python
import math
import jax
import jax.numpy as jnp
import numpy as np
from jax import lax

K = 16
CLAT = 128
CLON = 256
NSTEP = 2
BW = 128
OV = 2
NLAT = 1024
NLON = 4096
NBLK = 256
ACELL = 256
CAP = 8
N_LON = 16
N_LAT = 8
DEVICES = 128


def with_ends(drawn, key, low, top_value):
    dims = drawn.shape
    spot = [jax.random.randint(jax.random.fold_in(key, axis), (), 0, dims[axis]) for axis in range(len(dims))]
    drawn = drawn.at[tuple(spot)].set(low)
    longest = dims.index(max(dims))
    spot[longest] = (spot[longest] + 1) % dims[longest]
    return drawn.at[tuple(spot)].set(top_value)


def shard_levels(key, shape, cuts, smallest, high):
    level, own = 1.0, jax.random.fold_in(key, 6)
    for dim, parts in cuts:
        heights = jnp.exp(jax.random.uniform(jax.random.fold_in(own, dim), (parts,), jnp.float32, smallest / len(cuts), high / len(cuts)))
        level = level * jnp.repeat(heights, shape[dim] // parts).reshape([-1 if axis == dim else 1 for axis in range(len(shape))])
    return level


def routed_block(key, own, number, rows, amount, top, bound, skew):
    order = jax.random.permutation(key, amount)
    packed, ordinary = load_shares(amount, rows * top, bound, skew, True), load_shares(amount, rows * top, bound, skew, False)
    places = jnp.arange(amount)

    def named(sizes, offset_by):
        used = int((sizes > 0).sum())
        fixed = max(1, used // 4)
        moved = fixed + (places - fixed + offset_by * (used - fixed)) % max(1, amount - fixed)
        return jnp.zeros((amount,), jnp.int32).at[order[jnp.where(places < fixed, places, moved)]].set(jnp.asarray(sizes, jnp.int32))

    sizes = jnp.where(number % 4 == 0, named(packed, number // 4), named(ordinary, number - number // 4 - 1))
    mixed = jax.random.permutation(jax.random.fold_in(own, 3), amount)
    donor, receiver = mixed[0:amount // 2 * 2:2], mixed[1:amount // 2 * 2:2]
    room = jnp.minimum(sizes[donor] - 1, bound - sizes[receiver]) // 2
    room = jnp.where((donor == order[0]) | (receiver == order[0]) | (sizes[receiver] == 0), 0, jnp.maximum(room, 0))
    moved = jax.random.randint(jax.random.fold_in(own, 4), (amount // 2,), 0, 1 << 20) % (room + 1)
    sizes = sizes.at[donor].add(-moved).at[receiver].add(moved)
    labels = jnp.searchsorted(jnp.cumsum(sizes), jnp.arange(rows * top), side="right").astype(jnp.int32)
    table = labels.reshape(top, rows).T
    table = table[jax.random.permutation(jax.random.fold_in(own, 1), rows)]
    offset_by = jax.random.randint(jax.random.fold_in(own, 2), (rows, 1), 0, top)
    return jnp.take_along_axis(table, (jnp.arange(top)[None, :] + offset_by) % top, axis=1)


def load_shares(number_of, total, reach, slope, full):
    weights = [(1 << 20) // math.isqrt(grade ** slope) + 1 for grade in range(1, number_of + 1)]
    largest = reach if full else min(reach, max(-(-total // number_of), total * weights[0] // sum(weights)))
    least = 1 if total - largest >= number_of - 1 else 0
    given, surplus = [largest] + [least] * (number_of - 1), total - largest - least * (number_of - 1)
    while surplus > 0:
        candidates = [i for i in range(1, number_of) if given[i] < largest] or [i for i in range(1, number_of) if given[i] < reach]
        pool, left = sum([weights[i] for i in candidates]), surplus
        for i in candidates:
            extra = min(reach - given[i], max(1, left * weights[i] // pool), surplus)
            given[i] = given[i] + extra
            surplus = surplus - extra
    return np.array(given)


def centred(key, extent, deviation, limit, shards=(), dtype=jnp.bfloat16):
    values = deviation * jax.random.normal(key, extent, jnp.float32)
    if shards:
        values = values * shard_levels(key, extent, shards, -0.22, 0.18)
    return jnp.clip(values, -limit, limit).astype(dtype)


def setup_inputs(seed: int = 0) -> dict:
    arg_keys = jax.random.split(jax.random.key(seed), 12)
    temp = centred(arg_keys[0], (K, NLAT, NLON), 1.0, 6.0, ((1, 8), (2, 16)), jnp.float32)
    salt = centred(arg_keys[1], (K, NLAT, NLON), 1.0, 6.0, ((1, 8), (2, 16)), jnp.float32)
    east_face_velocity = jnp.clip(jax.random.uniform(arg_keys[2], (K, NLAT, NLON), jnp.float32, -0.1, 0.1) * shard_levels(arg_keys[2], (K, NLAT, NLON), ((1, 8), (2, 16)), -0.4, 0.0), -0.1, 0.1)
    v_face = jnp.clip(jax.random.uniform(arg_keys[3], (K, NLAT, NLON), jnp.float32, -0.1, 0.1) * shard_levels(arg_keys[3], (K, NLAT, NLON), ((1, 8), (2, 16)), -0.4, 0.0), -0.1, 0.1)
    kappa = jnp.clip(jnp.exp(math.log(0.1) - 2.3025851 * jax.random.uniform(arg_keys[4], (K, NLAT, NLON), jnp.float32) ** shard_levels(arg_keys[4], (K, NLAT, NLON), ((1, 8), (2, 16)), -0.2, 0.2)), 0.01, 0.1)
    land_mask = with_ends((jax.random.randint(arg_keys[5], (NLAT, NLON), 0, 5) < 4).astype(jnp.int32), jax.random.fold_in(arg_keys[5], 1), 0, 1)
    margin_owner_device_keys = jax.random.split(jax.random.fold_in(arg_keys[6], 1), N_LAT * N_LON * NBLK // NBLK)
    margin_owner_device_turns = jax.random.permutation(jax.random.fold_in(arg_keys[6], 3), N_LAT * N_LON * NBLK // NBLK)
    margin_owner_device = jax.vmap(lambda own, number: routed_block(jax.random.fold_in(arg_keys[6], 2), own, number, NBLK, DEVICES, OV, CAP, 2))(margin_owner_device_keys, margin_owner_device_turns).reshape((N_LAT, N_LON, NBLK, OV))
    margin_cell = with_ends(jax.random.randint(arg_keys[7], (N_LAT, N_LON, NBLK, OV), 0, ACELL), jax.random.fold_in(arg_keys[7], 1), 0, ACELL - 1).astype(jnp.int32)
    margin_weight = jnp.clip(0.2 + 0.8 * jax.random.uniform(arg_keys[8], (N_LAT, N_LON, NBLK, OV), jnp.float32) ** shard_levels(arg_keys[8], (N_LAT, N_LON, NBLK, OV), ((0, 8), (1, 16)), -0.2, 0.2), 0.2, 1.0)
    air_temp = centred(arg_keys[9], (N_LON, N_LAT, ACELL, BW), 1.0, 6.0, ((0, 16), (1, 8)), jnp.float32)
    wind_speed = jnp.clip(jnp.exp(math.log(3.0) - 2.3025851 * jax.random.uniform(arg_keys[10], (N_LON, N_LAT, ACELL, BW), jnp.float32) ** shard_levels(arg_keys[10], (N_LON, N_LAT, ACELL, BW), ((0, 16), (1, 8)), -0.2, 0.2)), 0.3, 3.0)
    return {"temp": temp, "salt": salt, "east_face_velocity": east_face_velocity, "v_face": v_face, "kappa": kappa, "land_mask": land_mask, "margin_owner_device": margin_owner_device, "margin_cell": margin_cell, "margin_weight": margin_weight, "air_temp": air_temp, "wind_speed": wind_speed}


bulk_coef = 0.1


def seawater_mass_per_volume(thermal_reading, dissolved_saltiness):
    return -0.25 * thermal_reading - 0.04 * thermal_reading * thermal_reading + 0.8 * dissolved_saltiness + 0.03 * thermal_reading * dissolved_saltiness


def face_flux(speed, diffuse, here, there):
    return 0.5 * (speed + jnp.abs(speed)) * here + 0.5 * (speed - jnp.abs(speed)) * there - diffuse * (there - here)


def horizontal(padded, coefs):
    east_v = coefs[0]
    north_v = coefs[1]
    diffuse = coefs[2]
    centre = padded[..., 1:-1, 1:-1]
    east = face_flux(east_v[..., 1:-1, 1:-1], diffuse[..., 1:-1, 1:-1], centre, padded[..., 1:-1, 2:])
    west = face_flux(east_v[..., 1:-1, :-2], diffuse[..., 1:-1, :-2], padded[..., 1:-1, :-2], centre)
    north = face_flux(north_v[..., 1:-1, 1:-1], diffuse[..., 1:-1, 1:-1], centre, padded[..., 2:, 1:-1])
    south = face_flux(north_v[..., :-2, 1:-1], diffuse[..., :-2, 1:-1], padded[..., :-2, 1:-1], centre)
    return (west - east) + (south - north)


def vertical(passive_scalars, rho):
    mixing = 0.01 + 0.1 * jax.nn.sigmoid(4.0 * (rho[:-1] - rho[1:]))
    fluxes = mixing * (passive_scalars[:, 1:] - passive_scalars[:, :-1])
    zeros = jnp.zeros_like(fluxes[:, :1])
    upper = jnp.concatenate([fluxes, zeros], axis=1)
    lower = jnp.concatenate([zeros, fluxes], axis=1)
    return upper - lower


def advance(passive_scalars, flat_tend, mask, heat):
    rho = seawater_mass_per_volume(passive_scalars[0], passive_scalars[1])
    tend = flat_tend + vertical(passive_scalars, rho)
    tend = tend.at[0, 0].add(heat)
    return passive_scalars + mask * tend


def coupling(surface, margin_owner_device, margin_cell, margin_weight, air_temp, wind_speed):
    nlat, nlon = surface.shape
    blocks = surface.reshape(N_LAT, CLAT, N_LON, CLON // BW, BW).transpose(0, 2, 1, 3, 4).reshape(N_LAT, N_LON, NBLK, BW)
    overlying_gas_lines = air_temp.reshape(-1, BW)
    wind_rows = wind_speed.reshape(-1, BW)
    index = margin_owner_device.astype(jnp.int32) * ACELL + margin_cell.astype(jnp.int32)
    flux = bulk_coef * wind_rows[index] * (overlying_gas_lines[index] - blocks[:, :, :, None, :])
    weights = margin_weight / jnp.sum(margin_weight, axis=-1, keepdims=True)
    heat = jnp.sum(weights[..., None] * flux, axis=3)
    return heat.reshape(N_LAT, N_LON, CLAT, CLON // BW, BW).transpose(0, 2, 1, 3, 4).reshape(nlat, nlon)


def reference(temp, salt, east_face_velocity, v_face, kappa, land_mask, margin_owner_device, margin_cell, margin_weight, air_temp, wind_speed):
    mask = land_mask.astype(jnp.float32)
    heat = coupling(temp[0], margin_owner_device, margin_cell, margin_weight, air_temp, wind_speed)
    coefs = jnp.stack([east_face_velocity, v_face, kappa])
    zero_row = jnp.zeros_like(coefs[:, :, :1])
    coefs = jnp.concatenate([zero_row, coefs, zero_row], axis=2)
    coefs = jnp.concatenate([coefs[..., -1:], coefs, coefs[..., :1]], axis=3)
    mixing_factor_layers = jnp.moveaxis(coefs, 1, 0)
    passive_scalars = jnp.stack([temp, salt])
    for step in range(NSTEP):
        fold = passive_scalars[:, :, -1:, ::-1]
        rows = jnp.concatenate([jnp.zeros_like(fold), passive_scalars, fold], axis=2)
        padded = jnp.concatenate([rows[..., -1:], rows, rows[..., :1]], axis=3)
        flat = lax.map(lambda pair: horizontal(pair[0], pair[1]), (jnp.moveaxis(padded, 1, 0), mixing_factor_layers))
        passive_scalars = advance(passive_scalars, jnp.moveaxis(flat, 0, 1), mask, heat)
    return passive_scalars[0], passive_scalars[1], seawater_mass_per_volume(passive_scalars[0], passive_scalars[1])
```

```python
import jax
import jax.numpy as jnp
from jax import lax
from jax.experimental import pallas as pl
from jax.experimental.pallas import tpu as pltpu
from jax.sharding import PartitionSpec as P

F32 = jnp.float32
BF16 = jnp.bfloat16
AXES = ("lon", "lat")
BULK = 0.1
SLOTS = 8
GROUP = SLOTS + 1
LEVELS = 16
ROWS = 128
LANES = 128
LIMIT = 20 * 1024 * 1024

VM = pl.BlockSpec(memory_space=pltpu.VMEM)
ANY = pl.BlockSpec(memory_space=pl.ANY)


def in_vmem(x):
    return pltpu.with_memory_space_constraint(x, pltpu.VMEM)


def dot(a, b):
    return jnp.dot(a, b, preferred_element_type=F32)


def dot_nt(a, b):
    return lax.dot_general(a, b, (((1,), (1,)), ((), ())), preferred_element_type=F32)


def pieces(x):
    high = x.astype(BF16)
    rest = x - high.astype(F32)
    middle = rest.astype(BF16)
    low = (rest - middle.astype(F32)).astype(BF16)
    return high, middle, low


def pick(onehot, x):
    high, middle, low = pieces(x)
    return dot(onehot, high) + (dot(onehot, middle) + dot(onehot, low))


def iota(shape, dim):
    return lax.broadcasted_iota(jnp.int32, shape, dim)


def roll(x, steps, axis):
    steps = steps % x.shape[axis]
    return x if steps == 0 else pltpu.roll(x, steps, axis)


def as_bf16(flag):
    return flag.astype(F32).astype(BF16)


def request_kernel(owner_ref, cell_ref, weight_ref, surface_ref, out_ref, codes_ref):
    w = weight_ref[...]
    share = w / (w[0:1] + w[1:2])
    before = iota((256, 256), 0)
    after = iota((256, 256), 1)
    perm = as_bf16(before == (after % ROWS) * 2 + after // ROWS)
    lists = jnp.concatenate([owner_ref[...].astype(F32), cell_ref[...].astype(F32)], axis=0)
    lists = dot(lists.astype(BF16), perm)
    share = pick_left(share, perm)
    owner = [lists[m : m + 1].astype(jnp.int32) for m in range(2)]
    cell = [lists[2 + m : 3 + m] for m in range(2)]
    device = iota((128, 256), 0)
    named = [as_bf16(device == owner[m]) for m in range(2)]
    earlier = as_bf16(before < after)
    ones = jnp.ones((256, 256), BF16)
    ahead = [dot(named[0], earlier), dot(named[1], earlier) + dot(named[0], ones)]
    rank = [
        jnp.sum(named[m].astype(F32) * ahead[m], axis=0, keepdims=True).astype(jnp.int32)
        for m in range(2)
    ]
    slot = iota((128, 256), 0)
    ids = sum(
        dot_nt(named[m], jnp.where(slot == rank[m], cell[m], 0.0).astype(BF16)) for m in range(2)
    )
    total = 128 * GROUP
    line = iota((total, 256), 0)
    place = as_bf16(
        (line == owner[0] * GROUP + rank[0]) | (line == owner[1] * GROUP + rank[1])
    )
    id_place = as_bf16(iota((total, 128), 0) == iota((total, 128), 1) * GROUP + SLOTS)
    surface = surface_ref[...]
    blocks = jnp.concatenate([surface[:, :LANES], surface[:, LANES:]], axis=0)
    out_ref[...] = pick(place, blocks) + dot(id_place, ids.astype(BF16))
    table = jnp.concatenate(
        [(owner[m] * SLOTS + rank[m]).astype(F32) for m in range(2)]
        + [share, jnp.zeros((124, 256), F32)],
        axis=0,
    )
    codes_ref[...] = jnp.transpose(table)


def pick_left(x, onehot):
    high, middle, low = pieces(x)
    return dot(high, onehot) + (dot(middle, onehot) + dot(low, onehot))


def make_request(owner, cell, weight, surface):
    return pl.pallas_call(
        request_kernel,
        out_shape=(
            pltpu.VMEM((128 * GROUP, LANES), F32),
            pltpu.VMEM((256, LANES), F32),
        ),
        grid=(1,),
        in_specs=[pl.BlockSpec((2, 256), lambda i: (0, 0))] * 3
        + [pl.BlockSpec((None, ROWS, 2 * LANES), lambda i: (0, 0, 0))],
        out_specs=(VM, VM),
        compiler_params=pltpu.CompilerParams(vmem_limit_bytes=LIMIT),
        cost_estimate=pl.CostEstimate(flops=2 * 10**9, bytes_accessed=2**20, transcendentals=0),
        name="request",
    )(*[pltpu.with_memory_space_constraint(x, pltpu.HBM) for x in (owner, cell, weight, surface)])


def answer_kernel(got_ref, air_ref, wind_ref, out_ref):
    ids = got_ref[pl.ds(SLOTS, 128, stride=GROUP), :].astype(BF16)
    patches = jnp.concatenate([air_ref[...], wind_ref[...]], axis=1)
    high, middle, low = pieces(patches)
    spread = jnp.ones((128, 256), BF16)
    chunk = 128
    for part in range(8):
        line = iota((chunk, 128), 0) + part * chunk
        lane = iota((chunk, 128), 1)
        rows = dot(as_bf16(line // SLOTS == lane), ids)
        rows = jnp.where(lane == line % SLOTS, rows, 0.0)
        wanted = dot(rows.astype(BF16), spread).astype(jnp.int32)
        onehot = as_bf16(wanted == iota((chunk, 256), 1))
        found = dot(onehot, high) + (dot(onehot, middle) + dot(onehot, low))
        for s in range(chunk // SLOTS):
            source = part * (chunk // SLOTS) + s
            cells = got_ref[source * GROUP : source * GROUP + SLOTS, :]
            here = found[s * SLOTS : (s + 1) * SLOTS]
            out_ref[source * SLOTS : (source + 1) * SLOTS, :] = (
                BULK * here[:, LANES:] * (here[:, :LANES] - cells)
            )


def make_answer(got, air, wind):
    return pl.pallas_call(
        answer_kernel,
        out_shape=pltpu.VMEM((128 * SLOTS, LANES), F32),
        in_specs=[VM] * 3,
        out_specs=VM,
        compiler_params=pltpu.CompilerParams(vmem_limit_bytes=LIMIT),
        cost_estimate=pl.CostEstimate(flops=2 * 10**9, bytes_accessed=2**20, transcendentals=0),
        name="answer",
    )(in_vmem(got), air, wind)


def is_odd(axis):
    return lax.rem(lax.axis_index(axis), 2) == 1


def flipped(x):
    back = as_bf16(iota((256, 256), 0) + iota((256, 256), 1) == 255)
    return pick_left(x, back)


def column_edges(load_t, load_s, extra, strip):
    lane = iota((8, LANES), 1)
    west = jnp.zeros((8, LANES), F32)
    east = jnp.zeros((8, LANES), F32)
    other = jnp.zeros((8, LANES), F32)
    for k in range(LEVELS):
        for t, load in enumerate((load_t, load_s)):
            x0, x1 = load(k, strip)
            at = LEVELS * t + k
            west = jnp.where(lane == at, roll(x0, at, 1), west)
            east = jnp.where(lane == at, roll(x1, at - 127, 1), east)
        if extra is not None:
            for f, ref in enumerate(extra):
                at = 32 + 32 * f + k
                x1 = ref[k, pl.ds(strip, 8), LANES:]
                other = jnp.where(lane == at, roll(x1, at - 127, 1), other)
    if extra is not None:
        east = east + (other + roll(other, 16, 1))
    return west, east


def send_columns(west, east, odd, strip, lon_a_ref, lon_b_ref):
    rows = pl.ds(strip, 8)
    lon_a_ref[rows, :] = jnp.where(odd, west, east)
    lon_b_ref[rows, :] = jnp.where(odd, east, west)


def edges_kernel(t_ref, s_ref, u_ref, v_ref, k_ref, lon_a_ref, lon_b_ref, lat_a_ref, lat_b_ref, west_ref):
    odd = is_odd("lon")

    def strip_step(i, carry):
        strip = pl.multiple_of(i * 8, 8)

        def loader(ref):
            return lambda k, r: (ref[k, pl.ds(r, 8), :LANES], ref[k, pl.ds(r, 8), LANES:])

        west, east = column_edges(loader(t_ref), loader(s_ref), (u_ref, k_ref), strip)
        west_ref[pl.ds(strip, 8), :] = west
        send_columns(west, east, odd, strip, lon_a_ref, lon_b_ref)
        return carry

    lax.fori_loop(0, ROWS // 8, strip_step, 0)
    odd_lat = is_odd("lat")
    top = lax.axis_index("lat") == lax.axis_size("lat") - 1
    south = jnp.concatenate(
        [ref[k, 0:1, :] for ref in (t_ref, s_ref) for k in range(LEVELS)], axis=0
    )
    north = jnp.concatenate(
        [ref[k, ROWS - 1 : ROWS, :] for ref in (t_ref, s_ref) for k in range(LEVELS)], axis=0
    )
    faces = jnp.concatenate(
        [ref[k, ROWS - 1 : ROWS, :] for ref in (v_ref, k_ref) for k in range(LEVELS)], axis=0
    )
    fold = flipped(north)
    lat_a_ref[0:32, :] = jnp.where(odd_lat, south, north)
    lat_a_ref[32:64, :] = faces
    lat_b_ref[0:32, :] = jnp.where(odd_lat, jnp.where(top, fold, north), south)
    lat_b_ref[32:64, :] = faces


def make_edges(t, s, u, v, k):
    return pl.pallas_call(
        edges_kernel,
        out_shape=(
            pltpu.VMEM((ROWS, LANES), F32),
            pltpu.VMEM((ROWS, LANES), F32),
            pltpu.VMEM((64, 256), F32),
            pltpu.VMEM((64, 256), F32),
            pltpu.VMEM((ROWS, LANES), F32),
        ),
        in_specs=[VM] * 5,
        out_specs=(VM,) * 5,
        compiler_params=pltpu.CompilerParams(vmem_limit_bytes=LIMIT),
        cost_estimate=pl.CostEstimate(flops=10**7, bytes_accessed=4 * 2**20, transcendentals=0),
        name="edges",
    )(t, s, u, v, k)


def swap_pairs(first, count):
    route = []
    for low in range(first, count - 1, 2):
        route += [(low, low + 1), (low + 1, low)]
    return route


def exchange(lon_a, lon_b, lat_a, lat_b):
    n_lon, n_lat = lax.axis_size("lon"), lax.axis_size("lat")
    ring = swap_pairs(1, n_lon) + [(n_lon - 1, 0), (0, n_lon - 1)]
    got_lon_a = lax.ppermute(lon_a, "lon", swap_pairs(0, n_lon))
    got_lon_b = lax.ppermute(lon_b, "lon", ring)
    got_lat_a = lax.ppermute(lat_a, "lat", swap_pairs(0, n_lat))
    route = [
        (i * n_lat + low, i * n_lat + high) for i in range(n_lon) for low, high in swap_pairs(1, n_lat)
    ]
    route += [(i * n_lat + n_lat - 1, (n_lon - 1 - i) * n_lat + n_lat - 1) for i in range(n_lon)]
    got_lat_b = lax.ppermute(lat_b, AXES, route)
    return got_lon_a, got_lon_b, got_lat_a, got_lat_b


def density_of(t, s):
    return t * (-0.25 - 0.04 * t + 0.03 * s) + 0.8 * s


def twice_density(t, s):
    return t * (-0.5 - 0.08 * t + 0.06 * s) + 1.6 * s


def step_strip(strip, last, load, u_ref, v_ref, k_ref, mask_ref, west_flux_ref, east_ref, north_ref, carry_ref, emit, heat_ref=None):
    rows = pl.ds(strip, 8)
    lane = iota((8, LANES), 1)
    sub = iota((8, LANES), 0)
    first_lane, last_lane = lane == 0, lane == LANES - 1
    row0, row7 = sub == 0, sub == 7
    halves = (slice(0, LANES), slice(LANES, 2 * LANES))
    mask = [mask_ref[rows, h].astype(F32) for h in halves]
    west_flux = west_flux_ref[rows, :]
    east_halo = east_ref[rows, :]
    x = [load(t, 0, strip) for t in range(2)]
    rho = [twice_density(x[0][h], x[1][h]) for h in range(2)]
    below = None
    for k in range(LEVELS):
        if k < LEVELS - 1:
            x_next = [load(t, k + 1, strip) for t in range(2)]
            rho_next = [twice_density(x_next[0][h], x_next[1][h]) for h in range(2)]
            mixing = [0.06 + 0.05 * jnp.tanh(rho[h] - rho_next[h]) for h in range(2)]
        u = [u_ref[k, rows, h] for h in halves]
        v = [v_ref[k, rows, h] for h in halves]
        d = [k_ref[k, rows, h] for h in halves]
        pe = [jnp.maximum(u[h], 0.0) + d[h] for h in range(2)]
        ne = [jnp.minimum(u[h], 0.0) - d[h] for h in range(2)]
        pn = [jnp.maximum(v[h], 0.0) + d[h] for h in range(2)]
        nn = [jnp.minimum(v[h], 0.0) - d[h] for h in range(2)]
        above = [None, None]
        new = [None, None]
        for t in range(2):
            at = LEVELS * t + k
            xt = x[t]
            y = [roll(xt[h], -1, 1) for h in range(2)]
            xe = [
                jnp.where(last_lane, y[1], y[0]),
                jnp.where(last_lane, roll(east_halo, 127 - at, 1), y[1]),
            ]
            east = [pe[h] * xt[h] + ne[h] * xe[h] for h in range(2)]
            z = [roll(east[h], 1, 1) for h in range(2)]
            west = [
                jnp.where(first_lane, roll(west_flux, -at, 1), z[0]),
                jnp.where(first_lane, z[0], z[1]),
            ]
            if last:
                ahead = [jnp.broadcast_to(north_ref[at : at + 1, h], (8, LANES)) for h in halves]
            else:
                ahead = load(t, k, strip + 8)
            xn = [roll(jnp.where(row0, ahead[h], xt[h]), -1, 0) for h in range(2)]
            north = [pn[h] * xt[h] + nn[h] * xn[h] for h in range(2)]
            south = [
                roll(jnp.where(row7, carry_ref[at, :, halves[h]], north[h]), 1, 0) for h in range(2)
            ]
            if not last:
                for h in range(2):
                    carry_ref[at, :, halves[h]] = north[h]
            tend = [(west[h] - east[h]) + (south[h] - north[h]) for h in range(2)]
            if k < LEVELS - 1:
                above[t] = [mixing[h] * (x_next[t][h] - xt[h]) for h in range(2)]
                tend = [tend[h] + above[t][h] for h in range(2)]
            if k > 0:
                tend = [tend[h] - below[t][h] for h in range(2)]
            if heat_ref is not None and t == 0 and k == 0:
                tend = [tend[h] + heat_ref[rows, halves[h]] for h in range(2)]
            new[t] = [xt[h] + mask[h] * tend[h] for h in range(2)]
        emit(k, strip, new)
        below = above
        if k < LEVELS - 1:
            x, rho = x_next, rho_next


def west_fluxes(west, coef, own):
    u = roll(coef, -32, 1)
    d = roll(coef, -64, 1)
    return (jnp.maximum(u, 0.0) + d) * west + (jnp.minimum(u, 0.0) - d) * own


def first_carry(south, faces, load_row, carry_ref):
    for k in range(LEVELS):
        v, d = faces(k), faces(LEVELS + k)
        pn = jnp.maximum(v, 0.0) + d
        nn = jnp.minimum(v, 0.0) - d
        for t in range(2):
            at = LEVELS * t + k
            flux = pn * south(at) + nn * load_row(t, k)
            carry_ref[at] = jnp.broadcast_to(flux, (8, 2 * LANES))


def halo_setup(odd_lon, odd_lat, got, coefs, own_ref, load_row, carry_ref, west_flux_ref, east_ref, north_ref):
    lon_a, lon_b, lat_a, lat_b = got
    c_lon_a, c_lon_b, c_lat_a, c_lat_b = coefs
    west = jnp.where(odd_lon, lon_a[...], lon_b[...])
    coef = jnp.where(odd_lon, c_lon_a[...], c_lon_b[...])
    west_flux_ref[...] = west_fluxes(west, coef, own_ref[...])
    east_ref[...] = jnp.where(odd_lon, lon_b[...], lon_a[...])
    north_ref[...] = jnp.where(odd_lat, lat_b[0:32, :], lat_a[0:32, :])

    def south(at):
        return jnp.where(odd_lat, lat_a[at : at + 1, :], lat_b[at : at + 1, :])

    def faces(at):
        return jnp.where(odd_lat, c_lat_a[32 + at : 33 + at, :], c_lat_b[32 + at : 33 + at, :])

    first_carry(south, faces, load_row, carry_ref)


def pair_loader(refs, top_ref=None):
    def load(t, k, strip):
        rows = pl.ds(strip, 8)
        if t == 0 and k == 0 and top_ref is not None:
            return [top_ref[rows, :LANES], top_ref[rows, LANES:]]
        return [refs[t][k, rows, :LANES], refs[t][k, rows, LANES:]]

    def load_row(t, k):
        if t == 0 and k == 0 and top_ref is not None:
            return top_ref[0:1, :]
        return refs[t][k, 0:1, :]

    return load, load_row


def strips(body):
    def one(i, carry):
        body(pl.multiple_of(i * 8, 8), False)
        return carry

    lax.fori_loop(0, ROWS // 8 - 1, one, 0)
    body(ROWS - 8, True)


def first_kernel(t_ref, s_ref, u_ref, v_ref, k_ref, mask_ref, own_ref, lon_a, lon_b, lat_a, lat_b,
                 t_out, s_out, carry_ref, west_flux_ref, east_ref, north_ref):
    load, load_row = pair_loader((t_ref, s_ref))
    got = (lon_a, lon_b, lat_a, lat_b)
    halo_setup(is_odd("lon"), is_odd("lat"), got, got, own_ref, load_row, carry_ref, west_flux_ref, east_ref, north_ref)
    outs = (t_out, s_out)

    def emit(k, strip, new):
        for t in range(2):
            for h in range(2):
                outs[t][k, pl.ds(strip, 8), h * LANES : (h + 1) * LANES] = new[t][h]

    def body(strip, last):
        step_strip(strip, last, load, u_ref, v_ref, k_ref, mask_ref, west_flux_ref, east_ref, north_ref, carry_ref, emit)

    strips(body)


STEP_SCRATCH = [
    pltpu.VMEM((2 * LEVELS, 8, 2 * LANES), F32),
    pltpu.VMEM((ROWS, LANES), F32),
    pltpu.VMEM((ROWS, LANES), F32),
    pltpu.VMEM((2 * LEVELS, 2 * LANES), F32),
]
STEP_COST = pl.CostEstimate(flops=7 * 10**7, bytes_accessed=25 * 2**20, transcendentals=10**6)


def first_step(t, s, u, v, k, mask, own, got):
    shape = pltpu.VMEM((LEVELS, ROWS, 2 * LANES), F32)
    return pl.pallas_call(
        first_kernel,
        out_shape=(shape, shape),
        in_specs=[VM] * 11,
        out_specs=(VM, VM),
        scratch_shapes=STEP_SCRATCH,
        compiler_params=pltpu.CompilerParams(vmem_limit_bytes=LIMIT),
        cost_estimate=STEP_COST,
        name="first_step",
    )(t, s, u, v, k, mask, own, *got)


def heat_kernel(t_ref, s_ref, mask_ref, back_ref, codes_ref, heat_out, top_out, lon_a_ref, lon_b_ref, lat_a_ref, lat_b_ref, west_ref):
    high, middle, low = pieces(back_ref[...])
    codes = codes_ref[...]
    lane = iota((256, 1024), 1)
    heat = None
    for m in range(2):
        onehot = as_bf16(codes[:, m : m + 1].astype(jnp.int32) == lane)
        flux = dot(onehot, high) + (dot(onehot, middle) + dot(onehot, low))
        part = codes[:, 2 + m : 3 + m] * flux
        heat = part if heat is None else heat + part
    mask = mask_ref[...].astype(F32)
    for h in range(2):
        cols = slice(h * LANES, (h + 1) * LANES)
        heat_out[:, cols] = heat[h * ROWS : (h + 1) * ROWS]
        top_out[:, cols] = t_ref[0, :, cols] + mask[:, cols] * heat[h * ROWS : (h + 1) * ROWS]
    odd = is_odd("lon")
    load, load_row = pair_loader((t_ref, s_ref), top_out)

    def strip_step(i, carry):
        strip = pl.multiple_of(i * 8, 8)
        west, east = column_edges(
            lambda k, r: load(0, k, r), lambda k, r: load(1, k, r), None, strip
        )
        west_ref[pl.ds(strip, 8), :] = west
        send_columns(west, east, odd, strip, lon_a_ref, lon_b_ref)
        return carry

    lax.fori_loop(0, ROWS // 8, strip_step, 0)
    odd_lat = is_odd("lat")
    top = lax.axis_index("lat") == lax.axis_size("lat") - 1
    last_rows = slice(ROWS - 1, ROWS)
    south = jnp.concatenate([load_row(t, k) for t in range(2) for k in range(LEVELS)], axis=0)
    north = jnp.concatenate(
        [top_out[last_rows, :]]
        + [t_ref[k, last_rows, :] for k in range(1, LEVELS)]
        + [s_ref[k, last_rows, :] for k in range(LEVELS)],
        axis=0,
    )
    fold = flipped(north)
    lat_a_ref[...] = jnp.where(odd_lat, south, north)
    lat_b_ref[...] = jnp.where(odd_lat, jnp.where(top, fold, north), south)


def add_heat(t, s, mask, back, codes):
    return pl.pallas_call(
        heat_kernel,
        out_shape=(
            pltpu.VMEM((ROWS, 2 * LANES), F32),
            pltpu.VMEM((ROWS, 2 * LANES), F32),
            pltpu.VMEM((ROWS, LANES), F32),
            pltpu.VMEM((ROWS, LANES), F32),
            pltpu.VMEM((32, 2 * LANES), F32),
            pltpu.VMEM((32, 2 * LANES), F32),
            pltpu.VMEM((ROWS, LANES), F32),
        ),
        in_specs=[VM] * 5,
        out_specs=(VM,) * 7,
        compiler_params=pltpu.CompilerParams(vmem_limit_bytes=LIMIT),
        cost_estimate=pl.CostEstimate(flops=10**9, bytes_accessed=4 * 2**20, transcendentals=0),
        name="heat",
    )(t, s, mask, in_vmem(back), in_vmem(codes))


def second_kernel(t_ref, s_ref, top_ref, heat_ref, u_ref, v_ref, k_ref, mask_ref, own_ref,
                  lon_a, lon_b, lat_a, lat_b, c_lon_a, c_lon_b, c_lat_a, c_lat_b,
                  t_out, s_out, rho_out,
                  carry_ref, west_flux_ref, east_ref, north_ref, t_buf, s_buf, rho_buf, sems):
    load, load_row = pair_loader((t_ref, s_ref), top_ref)
    halo_setup(is_odd("lon"), is_odd("lat"), (lon_a, lon_b, lat_a, lat_b), (c_lon_a, c_lon_b, c_lat_a, c_lat_b),
               own_ref, load_row, carry_ref, west_flux_ref, east_ref, north_ref)
    bufs = (t_buf, s_buf, rho_buf)
    outs = (t_out, s_out, rho_out)

    def emit(k, strip, new):
        for h in range(2):
            at = (k, pl.ds(strip, 8), slice(h * LANES, (h + 1) * LANES))
            for t in range(2):
                bufs[t][at] = new[t][h]
            rho_buf[at] = density_of(new[0][h], new[1][h])

    def copies(strip, index):
        rows = pl.ds(strip, 8)
        return [
            pltpu.make_async_copy(bufs[n].at[:, rows, :], outs[n].at[:, rows, :], sems.at[n, index])
            for n in range(3)
        ]

    def body(strip, last):
        step_strip(strip, last, load, u_ref, v_ref, k_ref, mask_ref, west_flux_ref, east_ref, north_ref, carry_ref, emit, heat_ref)
        index = ROWS // 8 - 1 if last else strip // 8
        for copy in copies(strip, index):
            copy.start()

    strips(body)
    for index in range(ROWS // 8):
        for copy in copies(index * 8, index):
            copy.wait()


def second_step(t, s, top, heat, u, v, k, mask, own, got, coefs):
    shape = jax.ShapeDtypeStruct((LEVELS, ROWS, 2 * LANES), F32)
    buf = pltpu.VMEM((LEVELS, ROWS, 2 * LANES), F32)
    return pl.pallas_call(
        second_kernel,
        out_shape=(shape, shape, shape),
        in_specs=[VM] * 17,
        out_specs=(ANY, ANY, ANY),
        scratch_shapes=STEP_SCRATCH + [buf, buf, buf, pltpu.SemaphoreType.DMA((3, ROWS // 8))],
        compiler_params=pltpu.CompilerParams(vmem_limit_bytes=LIMIT),
        cost_estimate=STEP_COST,
        name="second_step",
    )(t, s, in_vmem(top), in_vmem(heat), u, v, k, mask, in_vmem(own), *[in_vmem(g) for g in got], *coefs)


def body(
    temp,
    salt,
    east_face_velocity,
    v_face,
    kappa,
    land_mask,
    margin_owner_device,
    margin_cell,
    margin_weight,
    air_temp,
    wind_speed,
):
    def lists(x):
        return jnp.transpose(x.reshape(256, 2))

    request, codes = make_request(
        lists(margin_owner_device), lists(margin_cell), lists(margin_weight), temp
    )
    request = request.reshape(128, 1, GROUP * LANES)
    got = lax.all_to_all(request, AXES, split_axis=0, concat_axis=0, tiled=True)
    got = got.reshape(128 * GROUP, LANES)
    t, s, u, v, k = [in_vmem(x) for x in (temp, salt, east_face_velocity, v_face, kappa)]
    mask = in_vmem(land_mask)
    *sent, own = make_edges(t, s, u, v, k)
    halos = exchange(*sent)
    answer = make_answer(got, air_temp.reshape(256, LANES), wind_speed.reshape(256, LANES))
    back = lax.all_to_all(answer, AXES, split_axis=0, concat_axis=0, tiled=True)
    halos = [in_vmem(g) for g in halos]
    t1, s1 = [in_vmem(x) for x in first_step(t, s, u, v, k, mask, in_vmem(own), halos)]
    heat, top, *sent, own = add_heat(t1, s1, mask, back, codes)
    later = exchange(*sent)
    return second_step(t1, s1, top, heat, u, v, k, mask, own, later, halos)


def solution(mesh):
    grid = P(None, "lat", "lon")
    lists = P("lat", "lon", None, None)
    owned = P("lon", "lat", None, None)
    in_specs = (grid,) * 5 + (P("lat", "lon"),) + (lists,) * 3 + (owned,) * 2
    return jax.shard_map(body, mesh=mesh, in_specs=in_specs, out_specs=(grid,) * 3, check_vma=False)
```

```python
import jax
import jax.numpy as jnp
from jax import lax
from jax.experimental import pallas as pl
from jax.experimental.pallas import tpu as pltpu
from jax.sharding import PartitionSpec as P

F32 = jnp.float32
BF16 = jnp.bfloat16
AXES = ("lon", "lat")
BULK = 0.1
SLOTS = 8
GROUP = SLOTS + 1
LEVELS = 16
ROWS = 128
LANES = 128
STRIPS = ROWS // 8
LIMIT = 24 * 1024 * 1024

VM = pl.BlockSpec(memory_space=pltpu.VMEM)
ANY = pl.BlockSpec(memory_space=pl.ANY)


def in_vmem(x):
    return pltpu.with_memory_space_constraint(x, pltpu.VMEM)


def dot(a, b):
    return jnp.dot(a, b, preferred_element_type=F32)


def dot_nt(a, b):
    return lax.dot_general(a, b, (((1,), (1,)), ((), ())), preferred_element_type=F32)


def pieces(x):
    high = x.astype(BF16)
    rest = x - high.astype(F32)
    middle = rest.astype(BF16)
    low = (rest - middle.astype(F32)).astype(BF16)
    return high, middle, low


def pick(onehot, x):
    high, middle, low = pieces(x)
    return dot(onehot, high) + (dot(onehot, middle) + dot(onehot, low))


def iota(shape, dim):
    return lax.broadcasted_iota(jnp.int32, shape, dim)


def roll(x, steps, axis):
    steps = steps % x.shape[axis]
    return x if steps == 0 else pltpu.roll(x, steps, axis)


def as_bf16(flag):
    return flag.astype(F32).astype(BF16)


def make_lists(owner_ref, cell_ref, weight_ref):
    w = weight_ref[...]
    share = w / (w[0:1] + w[1:2])
    before = iota((256, 256), 0)
    after = iota((256, 256), 1)
    perm = as_bf16(before == (after % ROWS) * 2 + after // ROWS)
    lists = jnp.concatenate([owner_ref[...].astype(F32), cell_ref[...].astype(F32)], axis=0)
    lists = dot(lists.astype(BF16), perm)
    share = pick_left(share, perm)
    owner = [lists[m : m + 1].astype(jnp.int32) for m in range(2)]
    cell = [lists[2 + m : 3 + m] for m in range(2)]
    return owner, cell, share


def write_request(owner, cell, share, surface, out_ref, codes_ref):
    device = iota((128, 256), 0)
    named = [as_bf16(device == owner[m]) for m in range(2)]
    earlier = as_bf16(iota((256, 256), 0) < iota((256, 256), 1))
    ones = jnp.ones((256, 256), BF16)
    ahead = [dot(named[0], earlier), dot(named[1], earlier) + dot(named[0], ones)]
    rank = [
        jnp.sum(named[m].astype(F32) * ahead[m], axis=0, keepdims=True).astype(jnp.int32)
        for m in range(2)
    ]
    slot = iota((128, 256), 0)
    ids = sum(
        dot_nt(named[m], jnp.where(slot == rank[m], cell[m], 0.0).astype(BF16)) for m in range(2)
    )
    total = 128 * GROUP
    line = iota((total, 256), 0)
    place = as_bf16(
        (line == owner[0] * GROUP + rank[0]) | (line == owner[1] * GROUP + rank[1])
    )
    id_place = as_bf16(iota((total, 128), 0) == iota((total, 128), 1) * GROUP + SLOTS)
    blocks = jnp.concatenate([surface[:, :LANES], surface[:, LANES:]], axis=0)
    out_ref[...] = pick(place, blocks) + dot(id_place, ids.astype(BF16))
    table = jnp.concatenate(
        [(owner[m] * SLOTS + rank[m]).astype(F32) for m in range(2)]
        + [share, jnp.zeros((124, 256), F32)],
        axis=0,
    )
    codes_ref[...] = jnp.transpose(table)


def pick_left(x, onehot):
    high, middle, low = pieces(x)
    return dot(high, onehot) + (dot(middle, onehot) + dot(low, onehot))


CHUNKS = 4
CHUNK = ROWS // CHUNKS


def request_kernel(owner_ref, cell_ref, weight_ref, t_ref, s_ref, u_ref, v_ref, k_ref,
                   out_ref, codes_ref, lon_a_ref, lon_b_ref, lat_a_ref, lat_b_ref, west_ref,
                   surface_buf, t_buf, s_buf, u_buf, k_buf, v_row, k_row, sems, more_sems):
    last = pl.ds(ROWS - 8, 8)
    first = pltpu.make_async_copy(t_ref.at[0], surface_buf, more_sems.at[0])
    rows = [
        pltpu.make_async_copy(v_ref.at[:, last, :], v_row, more_sems.at[1]),
        pltpu.make_async_copy(k_ref.at[:, last, :], k_row, more_sems.at[2]),
    ]
    eastern = pl.ds(LANES, LANES)

    def chunk_copies(c):
        part = pl.ds(c * CHUNK, CHUNK)
        return [
            pltpu.make_async_copy(t_ref.at[:, part, :], t_buf.at[:, part, :], sems.at[0, c]),
            pltpu.make_async_copy(s_ref.at[:, part, :], s_buf.at[:, part, :], sems.at[1, c]),
            pltpu.make_async_copy(u_ref.at[:, part, eastern], u_buf.at[:, part, :], sems.at[2, c]),
            pltpu.make_async_copy(k_ref.at[:, part, eastern], k_buf.at[:, part, :], sems.at[3, c]),
        ]

    first.start()
    for c in range(CHUNKS):
        for copy in chunk_copies(c):
            copy.start()
    for copy in rows:
        copy.start()
    owner, cell, share = make_lists(owner_ref, cell_ref, weight_ref)
    first.wait()
    write_request(owner, cell, share, surface_buf[...], out_ref, codes_ref)
    odd = is_odd("lon")

    for c in range(CHUNKS):
        for copy in chunk_copies(c):
            copy.wait()

        part = slice(c * CHUNK, (c + 1) * CHUNK)
        west, east = column_edges((t_buf, s_buf), (u_buf, k_buf), part, CHUNK)
        west_ref[part, :] = west
        lon_a_ref[part, :] = jnp.where(odd, west, east)
        lon_b_ref[part, :] = jnp.where(odd, east, west)
    for copy in rows:
        copy.wait()
    south = jnp.concatenate(
        [ref[k, 0:1, :] for ref in (t_buf, s_buf) for k in range(LEVELS)], axis=0
    )
    north = jnp.concatenate(
        [ref[k, ROWS - 1 : ROWS, :] for ref in (t_buf, s_buf) for k in range(LEVELS)], axis=0
    )
    faces = jnp.concatenate(
        [ref[k, 7:8, :] for ref in (v_row, k_row) for k in range(LEVELS)], axis=0
    )
    send_rows(south, north, lat_a_ref, lat_b_ref)
    lat_a_ref[32:64, :] = faces
    lat_b_ref[32:64, :] = faces


def send_rows(south, north, lat_a_ref, lat_b_ref):
    odd = is_odd("lat")
    top = lax.axis_index("lat") == lax.axis_size("lat") - 1
    lat_a_ref[0:32, :] = jnp.where(odd, south, north)
    lat_b_ref[0:32, :] = jnp.where(odd, jnp.where(top, flipped(north), north), south)


def in_hbm(x):
    return pltpu.with_memory_space_constraint(x, pltpu.HBM)


def make_request(owner, cell, weight, fields):
    field = pltpu.VMEM((LEVELS, ROWS, 2 * LANES), F32)
    half = pltpu.VMEM((LEVELS, ROWS, LANES), F32)
    row = pltpu.VMEM((LEVELS, 8, 2 * LANES), F32)
    return pl.pallas_call(
        request_kernel,
        out_shape=(
            pltpu.VMEM((128 * GROUP, LANES), F32),
            pltpu.VMEM((256, LANES), F32),
            pltpu.VMEM((ROWS, LANES), F32),
            pltpu.VMEM((ROWS, LANES), F32),
            pltpu.VMEM((64, 2 * LANES), F32),
            pltpu.VMEM((64, 2 * LANES), F32),
            pltpu.VMEM((ROWS, LANES), F32),
        ),
        grid=(1,),
        in_specs=[pl.BlockSpec((2, 256), lambda i: (0, 0))] * 3 + [ANY] * 5,
        out_specs=(VM,) * 7,
        scratch_shapes=[
            pltpu.VMEM((ROWS, 2 * LANES), F32), field, field, half, half, row, row,
            pltpu.SemaphoreType.DMA((4, CHUNKS)),
            pltpu.SemaphoreType.DMA((3,)),
        ],
        compiler_params=pltpu.CompilerParams(vmem_limit_bytes=LIMIT),
        cost_estimate=pl.CostEstimate(flops=2 * 10**9, bytes_accessed=8 * 2**20, transcendentals=0),
        name="request",
    )(*[in_hbm(x) for x in (owner, cell, weight, *fields)])


def answer_kernel(got_ref, air_ref, wind_ref, *rest):
    out_ref = rest[-1]
    ids = got_ref[pl.ds(SLOTS, 128, stride=GROUP), :].astype(BF16)
    patches = jnp.concatenate([air_ref[...], wind_ref[...]], axis=1)
    high, middle, low = pieces(patches)
    spread = jnp.ones((128, 256), BF16)
    chunk = 128
    for part in range(8):
        line = iota((chunk, 128), 0) + part * chunk
        lane = iota((chunk, 128), 1)
        rows = dot(as_bf16(line // SLOTS == lane), ids)
        rows = jnp.where(lane == line % SLOTS, rows, 0.0)
        wanted = dot(rows.astype(BF16), spread).astype(jnp.int32)
        onehot = as_bf16(wanted == iota((chunk, 256), 1))
        found = dot(onehot, high) + (dot(onehot, middle) + dot(onehot, low))
        for s in range(chunk // SLOTS):
            source = part * (chunk // SLOTS) + s
            cells = got_ref[source * GROUP : source * GROUP + SLOTS, :]
            here = found[s * SLOTS : (s + 1) * SLOTS]
            out_ref[source * SLOTS : (source + 1) * SLOTS, :] = (
                BULK * here[:, LANES:] * (here[:, :LANES] - cells)
            )


def make_answer(got, air, wind, after):
    return pl.pallas_call(
        answer_kernel,
        out_shape=pltpu.VMEM((128 * SLOTS, LANES), F32),
        in_specs=[VM] * 3 + [ANY] * len(after),
        out_specs=VM,
        compiler_params=pltpu.CompilerParams(vmem_limit_bytes=LIMIT),
        cost_estimate=pl.CostEstimate(flops=2 * 10**9, bytes_accessed=2**20, transcendentals=0),
        name="answer",
    )(in_vmem(got), air, wind, *after)


def is_odd(axis):
    return lax.rem(lax.axis_index(axis), 2) == 1


def flipped(x):
    back = as_bf16(iota((256, 256), 0) + iota((256, 256), 1) == 255)
    return pick_left(x, back)


class Columns:
    def __init__(self, rows):
        self.lane = iota((rows, LANES), 1)
        self.west = jnp.zeros((rows, LANES), F32)
        self.east = jnp.zeros((rows, LANES), F32)

    def add_west(self, at, x):
        self.west = jnp.where(self.lane == at, roll(x, at, 1), self.west)

    def add_east(self, at, x):
        self.east = jnp.where(self.lane == at, roll(x, at - 127, 1), self.east)


def column_edges(tracers, extra, rows, count):
    columns = Columns(count)
    for t, ref in enumerate(tracers):
        for k in range(LEVELS):
            columns.add_west(LEVELS * t + k, ref[k, rows, :LANES])
    for t, ref in enumerate(tracers):
        for k in range(LEVELS):
            columns.add_east(LEVELS * t + k, ref[k, rows, LANES:])
    for f, ref in enumerate(extra):
        for k in range(LEVELS):
            columns.add_east(64 + LEVELS * f + k, ref[k, rows, :])
    faces = jnp.where(columns.lane >= 64, columns.east, 0.0)
    tracers_east = jnp.where(columns.lane < 64, columns.east, 0.0)
    u = jnp.where(columns.lane < 80, faces, 0.0)
    d = faces - u
    u = roll(u, -32, 1)
    d = roll(d, -16, 1)
    east = tracers_east + (u + roll(u, 16, 1)) + (d + roll(d, 16, 1))
    return columns.west, east


def swap_pairs(first, count):
    route = []
    for low in range(first, count - 1, 2):
        route += [(low, low + 1), (low + 1, low)]
    return route


def exchange(lon_a, lon_b, lat_a, lat_b):
    n_lon, n_lat = lax.axis_size("lon"), lax.axis_size("lat")
    ring = swap_pairs(1, n_lon) + [(n_lon - 1, 0), (0, n_lon - 1)]
    got_lon_a = lax.ppermute(lon_a, "lon", swap_pairs(0, n_lon))
    got_lon_b = lax.ppermute(lon_b, "lon", ring)
    got_lat_a = lax.ppermute(lat_a, "lat", swap_pairs(0, n_lat))
    route = [
        (i * n_lat + low, i * n_lat + high) for i in range(n_lon) for low, high in swap_pairs(1, n_lat)
    ]
    route += [(i * n_lat + n_lat - 1, (n_lon - 1 - i) * n_lat + n_lat - 1) for i in range(n_lon)]
    got_lat_b = lax.ppermute(lat_b, AXES, route)
    return got_lon_a, got_lon_b, got_lat_a, got_lat_b


def density_of(t, s):
    return t * (-0.25 - 0.04 * t + 0.03 * s) + 0.8 * s


def twice_density(t, s):
    return t * (-0.5 - 0.08 * t + 0.06 * s) + 1.6 * s


def step_strip(strip, last, load, u_ref, v_ref, k_ref, mask_ref, side_ref, north_ref, carry_ref, emit, heat_ref=None):
    rows = pl.ds(strip, 8)
    lane = iota((8, LANES), 1)
    sub = iota((8, LANES), 0)
    first_lane, last_lane = lane == 0, lane == LANES - 1
    row0, row7 = sub == 0, sub == 7
    halves = (slice(0, LANES), slice(LANES, 2 * LANES))
    mask = [mask_ref[rows, h].astype(F32) for h in halves]
    x = [load(t, 0, strip) for t in range(2)]
    rho = [twice_density(x[0][h], x[1][h]) for h in range(2)]
    below = None
    for k in range(LEVELS):
        if k < LEVELS - 1:
            x_next = [load(t, k + 1, strip) for t in range(2)]
            rho_next = [twice_density(x_next[0][h], x_next[1][h]) for h in range(2)]
            mixing = [0.06 + 0.05 * jnp.tanh(rho[h] - rho_next[h]) for h in range(2)]
        u = [u_ref[k, rows, h] for h in halves]
        v = [v_ref[k, rows, h] for h in halves]
        d = [k_ref[k, rows, h] for h in halves]
        pe = [jnp.maximum(u[h], 0.0) + d[h] for h in range(2)]
        ne = [jnp.minimum(u[h], 0.0) - d[h] for h in range(2)]
        pn = [jnp.maximum(v[h], 0.0) + d[h] for h in range(2)]
        nn = [jnp.minimum(v[h], 0.0) - d[h] for h in range(2)]
        above = [None, None]
        new = [None, None]
        for t in range(2):
            at = LEVELS * t + k
            xt = x[t]
            side = side_ref[at, rows, :]
            y = [roll(xt[h], -1, 1) for h in range(2)]
            xe = [
                jnp.where(last_lane, y[1], y[0]),
                jnp.where(last_lane, side, y[1]),
            ]
            east = [pe[h] * xt[h] + ne[h] * xe[h] for h in range(2)]
            z = [roll(east[h], 1, 1) for h in range(2)]
            west = [
                jnp.where(first_lane, side, z[0]),
                jnp.where(first_lane, z[0], z[1]),
            ]
            if last:
                ahead = [jnp.broadcast_to(north_ref[at : at + 1, h], (8, LANES)) for h in halves]
            else:
                ahead = load(t, k, strip + 8)
            xn = [roll(jnp.where(row0, ahead[h], xt[h]), -1, 0) for h in range(2)]
            north = [pn[h] * xt[h] + nn[h] * xn[h] for h in range(2)]
            south = [
                roll(jnp.where(row7, carry_ref[at, :, halves[h]], north[h]), 1, 0) for h in range(2)
            ]
            if not last:
                for h in range(2):
                    carry_ref[at, :, halves[h]] = north[h]
            tend = [(west[h] - east[h]) + (south[h] - north[h]) for h in range(2)]
            if k < LEVELS - 1:
                above[t] = [mixing[h] * (x_next[t][h] - xt[h]) for h in range(2)]
                tend = [tend[h] + above[t][h] for h in range(2)]
            if k > 0:
                tend = [tend[h] - below[t][h] for h in range(2)]
            if heat_ref is not None and t == 0 and k == 0:
                tend = [tend[h] + heat_ref[rows, halves[h]] for h in range(2)]
            new[t] = [xt[h] + mask[h] * tend[h] for h in range(2)]
        emit(k, strip, new)
        below = above
        if k < LEVELS - 1:
            x, rho = x_next, rho_next


def west_fluxes(west, coef, own):
    u = roll(coef, -32, 1)
    d = roll(coef, -64, 1)
    return (jnp.maximum(u, 0.0) + d) * west + (jnp.minimum(u, 0.0) - d) * own


def first_carry(south, faces, load_row, carry_ref):
    for k in range(LEVELS):
        v, d = faces(k), faces(LEVELS + k)
        pn = jnp.maximum(v, 0.0) + d
        nn = jnp.minimum(v, 0.0) - d
        for t in range(2):
            at = LEVELS * t + k
            flux = pn * south(at) + nn * load_row(t, k)
            carry_ref[at] = jnp.broadcast_to(flux, (8, 2 * LANES))


def halo_setup(odd_lon, odd_lat, got, coefs, own_ref, load_row, carry_ref, side_ref, north_ref):
    lon_a, lon_b, lat_a, lat_b = got
    c_lon_a, c_lon_b, c_lat_a, c_lat_b = coefs
    west = jnp.where(odd_lon, lon_a[...], lon_b[...])
    coef = jnp.where(odd_lon, c_lon_a[...], c_lon_b[...])
    flux = west_fluxes(west, coef, own_ref[...])
    east = jnp.where(odd_lon, lon_b[...], lon_a[...])
    last_lane = iota((ROWS, LANES), 1) == LANES - 1
    for at in range(2 * LEVELS):
        side_ref[at] = jnp.where(last_lane, roll(east, 127 - at, 1), roll(flux, -at, 1))
    north_ref[...] = jnp.where(odd_lat, lat_b[0:32, :], lat_a[0:32, :])

    def south(at):
        return jnp.where(odd_lat, lat_a[at : at + 1, :], lat_b[at : at + 1, :])

    def faces(at):
        return jnp.where(odd_lat, c_lat_a[32 + at : 33 + at, :], c_lat_b[32 + at : 33 + at, :])

    first_carry(south, faces, load_row, carry_ref)


def pair_loader(refs, top_ref=None):
    def load(t, k, strip):
        rows = pl.ds(strip, 8)
        if t == 0 and k == 0 and top_ref is not None:
            return [top_ref[rows, :LANES], top_ref[rows, LANES:]]
        return [refs[t][k, rows, :LANES], refs[t][k, rows, LANES:]]

    def load_row(t, k):
        if t == 0 and k == 0 and top_ref is not None:
            return top_ref[0:1, :]
        return refs[t][k, 0:1, :]

    return load, load_row


def strips(body):
    def one(i, carry):
        body(pl.multiple_of(i * 8, 8), False)
        return carry

    lax.fori_loop(0, ROWS // 8 - 1, one, 0)
    body(ROWS - 8, True)


def first_kernel(t_hbm, s_hbm, u_hbm, v_hbm, k_hbm, mask_hbm, own_ref, lon_a, lon_b, lat_a, lat_b,
                 t_out, s_out, top_out, west_out, east_out, south_out, north_out,
                 carry_ref, side_ref, north_ref,
                 t_ref, s_ref, u_ref, v_ref, k_ref, t_new, s_new, mask_ref, sems, out_sems):
    sources = (t_hbm, s_hbm, u_hbm, v_hbm, k_hbm)
    bufs = (t_ref, s_ref, u_ref, v_ref, k_ref)
    new_bufs = (t_new, s_new)
    outs = (t_out, s_out)

    def copy_in(f, index):
        rows = pl.ds(pl.multiple_of(index * 8, 8), 8)
        return pltpu.make_async_copy(sources[f].at[:, rows, :], bufs[f].at[:, rows, :], sems.at[f, index])

    def copy_out(t, index):
        rows = pl.ds(pl.multiple_of(index * 8, 8), 8)
        return pltpu.make_async_copy(new_bufs[t].at[:, rows, :], outs[t].at[:, rows, :], out_sems.at[t, index])

    def start(index, carry):
        for f in range(5):
            copy_in(f, index).start()
        return carry

    mask_copy = pltpu.make_async_copy(mask_hbm, mask_ref, sems.at[5, 0])
    start(0, 0)
    mask_copy.start()
    lax.fori_loop(1, STRIPS, start, 0)
    copy_in(0, 0).wait()
    copy_in(1, 0).wait()
    load, load_row = pair_loader((t_ref, s_ref))
    got = (lon_a, lon_b, lat_a, lat_b)
    halo_setup(is_odd("lon"), is_odd("lat"), got, got, own_ref, load_row, carry_ref, side_ref, north_ref)
    mask_copy.wait()

    def body(strip, last):
        index = STRIPS - 1 if last else strip // 8
        for f in range(2, 5):
            copy_in(f, index).wait()
        if not last:
            for f in range(2):
                copy_in(f, index + 1).wait()
        columns = Columns(8)

        def emit(k, strip, new):
            rows = pl.ds(strip, 8)
            for t in range(2):
                for h in range(2):
                    new_bufs[t][k, rows, h * LANES : (h + 1) * LANES] = new[t][h]
                    if t == 0 and k == 0:
                        top_out[rows, h * LANES : (h + 1) * LANES] = new[t][h]
                columns.add_west(LEVELS * t + k, new[t][0])
                columns.add_east(LEVELS * t + k, new[t][1])

        step_strip(strip, last, load, u_ref, v_ref, k_ref, mask_ref, side_ref, north_ref, carry_ref, emit)
        west_out[pl.ds(strip, 8), :] = columns.west
        east_out[pl.ds(strip, 8), :] = columns.east
        for t in range(2):
            copy_out(t, index).start()

    strips(body)
    south_out[...] = jnp.concatenate([ref[k, 0:1, :] for ref in new_bufs for k in range(LEVELS)], axis=0)
    north_out[...] = jnp.concatenate(
        [ref[k, ROWS - 1 : ROWS, :] for ref in new_bufs for k in range(LEVELS)], axis=0
    )

    def finish(index, carry):
        for t in range(2):
            copy_out(t, index).wait()
        return carry

    lax.fori_loop(0, STRIPS, finish, 0)


STEP_SCRATCH = [
    pltpu.VMEM((2 * LEVELS, 8, 2 * LANES), F32),
    pltpu.VMEM((2 * LEVELS, ROWS, LANES), F32),
    pltpu.VMEM((2 * LEVELS, 2 * LANES), F32),
]
STEP_COST = pl.CostEstimate(flops=7 * 10**7, bytes_accessed=25 * 2**20, transcendentals=10**6)


def first_step(fields, mask, own, got):
    shape = pltpu.HBM((LEVELS, ROWS, 2 * LANES), F32)
    buf = pltpu.VMEM((LEVELS, ROWS, 2 * LANES), F32)
    return pl.pallas_call(
        first_kernel,
        out_shape=(
            shape,
            shape,
            pltpu.VMEM((ROWS, 2 * LANES), F32),
            pltpu.VMEM((ROWS, LANES), F32),
            pltpu.VMEM((ROWS, LANES), F32),
            pltpu.VMEM((2 * LEVELS, 2 * LANES), F32),
            pltpu.VMEM((2 * LEVELS, 2 * LANES), F32),
        ),
        in_specs=[ANY] * 6 + [VM] * 5,
        out_specs=(ANY, ANY) + (VM,) * 5,
        scratch_shapes=STEP_SCRATCH
        + [buf] * 7
        + [pltpu.VMEM((ROWS, 2 * LANES), jnp.int32), pltpu.SemaphoreType.DMA((6, STRIPS)), pltpu.SemaphoreType.DMA((2, STRIPS))],
        compiler_params=pltpu.CompilerParams(vmem_limit_bytes=LIMIT),
        cost_estimate=STEP_COST,
        name="first_step",
    )(*[in_hbm(x) for x in fields], in_hbm(mask), own, *got)


def heat_kernel(top_ref, west_ref, east_ref, south_ref, north_ref, mask_hbm, back_ref, codes_ref,
                heat_out, top_out, lon_a_ref, lon_b_ref, lat_a_ref, lat_b_ref, own_out, mask_ref, sem):
    mask_copy = pltpu.make_async_copy(mask_hbm, mask_ref, sem)
    mask_copy.start()
    high, middle, low = pieces(back_ref[...])
    codes = codes_ref[...]
    lane = iota((256, 1024), 1)
    heat = None
    for m in range(2):
        onehot = as_bf16(codes[:, m : m + 1].astype(jnp.int32) == lane)
        flux = dot(onehot, high) + (dot(onehot, middle) + dot(onehot, low))
        part = codes[:, 2 + m : 3 + m] * flux
        heat = part if heat is None else heat + part
    mask_copy.wait()
    mask = mask_ref[...].astype(F32)
    added = []
    for h in range(2):
        cols = slice(h * LANES, (h + 1) * LANES)
        here = heat[h * ROWS : (h + 1) * ROWS]
        heat_out[:, cols] = here
        added.append(mask[:, cols] * here)
        top_out[:, cols] = top_ref[:, cols] + added[h]
    first = iota((ROWS, LANES), 1) == 0
    west = west_ref[...] + jnp.where(first, added[0], 0.0)
    east = east_ref[...] + jnp.where(first, roll(added[1], 1, 1), 0.0)
    own_out[...] = west
    odd = is_odd("lon")
    lon_a_ref[...] = jnp.where(odd, west, east)
    lon_b_ref[...] = jnp.where(odd, east, west)
    south = jnp.concatenate([top_out[0:1, :], south_ref[1:, :]], axis=0)
    north = jnp.concatenate([top_out[ROWS - 1 : ROWS, :], north_ref[1:, :]], axis=0)
    send_rows(south, north, lat_a_ref, lat_b_ref)


def add_heat(top, west, east, south, north, mask, back, codes):
    return pl.pallas_call(
        heat_kernel,
        out_shape=(
            pltpu.VMEM((ROWS, 2 * LANES), F32),
            pltpu.VMEM((ROWS, 2 * LANES), F32),
            pltpu.VMEM((ROWS, LANES), F32),
            pltpu.VMEM((ROWS, LANES), F32),
            pltpu.VMEM((32, 2 * LANES), F32),
            pltpu.VMEM((32, 2 * LANES), F32),
            pltpu.VMEM((ROWS, LANES), F32),
        ),
        in_specs=[VM] * 5 + [ANY] + [VM] * 2,
        out_specs=(VM,) * 7,
        scratch_shapes=[pltpu.VMEM((ROWS, 2 * LANES), jnp.int32), pltpu.SemaphoreType.DMA],
        compiler_params=pltpu.CompilerParams(vmem_limit_bytes=LIMIT),
        cost_estimate=pl.CostEstimate(flops=10**9, bytes_accessed=2**20, transcendentals=0),
        name="heat",
    )(*[in_vmem(x) for x in (top, west, east, south, north)], in_hbm(mask), in_vmem(back), in_vmem(codes))


def second_kernel(t_hbm, s_hbm, u_hbm, v_hbm, k_hbm, mask_hbm, top_ref, heat_ref, own_ref,
                  lon_a, lon_b, lat_a, lat_b, c_lon_a, c_lon_b, c_lat_a, c_lat_b,
                  t_out, s_out, rho_out,
                  carry_ref, side_ref, north_ref,
                  t_ref, s_ref, u_ref, v_ref, k_ref, t_buf, s_buf, rho_buf, mask_ref, in_sems, sems):
    sources = (t_hbm, s_hbm, u_hbm, v_hbm, k_hbm)
    held = (t_ref, s_ref, u_ref, v_ref, k_ref)

    def copy_in(t, index):
        rows = pl.ds(pl.multiple_of(index * 8, 8), 8)
        return pltpu.make_async_copy(sources[t].at[:, rows, :], held[t].at[:, rows, :], in_sems.at[t, index])

    def start(index, carry):
        for f in range(5):
            copy_in(f, index).start()
        return carry

    mask_copy = pltpu.make_async_copy(mask_hbm, mask_ref, in_sems.at[5, 0])
    start(0, 0)
    mask_copy.start()
    lax.fori_loop(1, STRIPS, start, 0)
    copy_in(0, 0).wait()
    copy_in(1, 0).wait()
    load, load_row = pair_loader((t_ref, s_ref), top_ref)
    halo_setup(is_odd("lon"), is_odd("lat"), (lon_a, lon_b, lat_a, lat_b), (c_lon_a, c_lon_b, c_lat_a, c_lat_b),
               own_ref, load_row, carry_ref, side_ref, north_ref)
    mask_copy.wait()
    bufs = (t_buf, s_buf, rho_buf)
    outs = (t_out, s_out, rho_out)

    def emit(k, strip, new):
        for h in range(2):
            at = (k, pl.ds(strip, 8), slice(h * LANES, (h + 1) * LANES))
            for t in range(2):
                bufs[t][at] = new[t][h]
            rho_buf[at] = density_of(new[0][h], new[1][h])

    def copies(index):
        rows = pl.ds(pl.multiple_of(index * 8, 8), 8)
        return [
            pltpu.make_async_copy(bufs[n].at[:, rows, :], outs[n].at[:, rows, :], sems.at[n, index])
            for n in range(3)
        ]

    def body(strip, last):
        index = STRIPS - 1 if last else strip // 8
        for f in range(2, 5):
            copy_in(f, index).wait()
        if not last:
            for t in range(2):
                copy_in(t, index + 1).wait()
        step_strip(strip, last, load, u_ref, v_ref, k_ref, mask_ref, side_ref, north_ref, carry_ref, emit, heat_ref)
        for copy in copies(index):
            copy.start()

    strips(body)

    def finish(index, carry):
        for copy in copies(index):
            copy.wait()
        return carry

    lax.fori_loop(0, STRIPS, finish, 0)


def second_step(t, s, fields, mask, top, heat, own, got, coefs):
    shape = jax.ShapeDtypeStruct((LEVELS, ROWS, 2 * LANES), F32)
    buf = pltpu.VMEM((LEVELS, ROWS, 2 * LANES), F32)
    return pl.pallas_call(
        second_kernel,
        out_shape=(shape, shape, shape),
        in_specs=[ANY] * 6 + [VM] * 11,
        out_specs=(ANY, ANY, ANY),
        scratch_shapes=STEP_SCRATCH
        + [buf] * 8
        + [pltpu.VMEM((ROWS, 2 * LANES), jnp.int32), pltpu.SemaphoreType.DMA((6, STRIPS)), pltpu.SemaphoreType.DMA((3, STRIPS))],
        compiler_params=pltpu.CompilerParams(vmem_limit_bytes=LIMIT),
        cost_estimate=STEP_COST,
        name="second_step",
    )(in_hbm(t), in_hbm(s), *[in_hbm(x) for x in fields], in_hbm(mask), in_vmem(top), in_vmem(heat), in_vmem(own), *[in_vmem(g) for g in got], *coefs)


def body(
    temp,
    salt,
    east_face_velocity,
    v_face,
    kappa,
    land_mask,
    margin_owner_device,
    margin_cell,
    margin_weight,
    air_temp,
    wind_speed,
):
    def lists(x):
        return jnp.transpose(x.reshape(256, 2))

    fields = (temp, salt, east_face_velocity, v_face, kappa)
    request, codes, *sent, own = make_request(
        lists(margin_owner_device), lists(margin_cell), lists(margin_weight), fields
    )
    request = request.reshape(128, 1, GROUP * LANES)
    got = lax.all_to_all(request, AXES, split_axis=0, concat_axis=0, tiled=True)
    got = got.reshape(128 * GROUP, LANES)
    halos = [in_vmem(g) for g in exchange(*sent)]
    answer = make_answer(got, air_temp.reshape(256, LANES), wind_speed.reshape(256, LANES), halos)
    back = lax.all_to_all(answer, AXES, split_axis=0, concat_axis=0, tiled=True)
    t1, s1, *edges = first_step(fields, land_mask, in_vmem(own), halos)
    heat, top, *sent, own = add_heat(*edges, land_mask, back, codes)
    later = exchange(*sent)
    return second_step(t1, s1, fields[2:], land_mask, top, heat, own, later, halos)


def solution(mesh):
    grid = P(None, "lat", "lon")
    lists = P("lat", "lon", None, None)
    owned = P("lon", "lat", None, None)
    in_specs = (grid,) * 5 + (P("lat", "lon"),) + (lists,) * 3 + (owned,) * 2
    return jax.shard_map(body, mesh=mesh, in_specs=in_specs, out_specs=(grid,) * 3, check_vma=False)
```

```python
import jax
import jax.numpy as jnp
from jax import lax
from jax.experimental import pallas as pl
from jax.experimental.pallas import tpu as pltpu
from jax.sharding import PartitionSpec as P

F32 = jnp.float32
BF16 = jnp.bfloat16
AXES = ("lon", "lat")
BULK = 0.1
SLOTS = 8
LEVELS = 16
ROWS = 128
LANES = 128
STRIPS = ROWS // 8
LIMIT = 24 * 1024 * 1024

VM = pl.BlockSpec(memory_space=pltpu.VMEM)
ANY = pl.BlockSpec(memory_space=pl.ANY)


def in_vmem(x):
    return pltpu.with_memory_space_constraint(x, pltpu.VMEM)


def dot(a, b):
    return jnp.dot(a, b, preferred_element_type=F32)


def dot_nt(a, b):
    return lax.dot_general(a, b, (((1,), (1,)), ((), ())), preferred_element_type=F32)


def pieces(x):
    high = x.astype(BF16)
    rest = x - high.astype(F32)
    middle = rest.astype(BF16)
    low = (rest - middle.astype(F32)).astype(BF16)
    return high, middle, low


def pick(onehot, x):
    high, middle, low = pieces(x)
    return dot(onehot, high) + (dot(onehot, middle) + dot(onehot, low))


def iota(shape, dim):
    return lax.broadcasted_iota(jnp.int32, shape, dim)


def roll(x, steps, axis):
    steps = steps % x.shape[axis]
    return x if steps == 0 else pltpu.roll(x, steps, axis)


def as_bf16(flag):
    return flag.astype(F32).astype(BF16)


def make_lists(owner_ref, cell_ref, weight_ref):
    w = weight_ref[...]
    share = w / (w[0:1] + w[1:2])
    before = iota((256, 256), 0)
    after = iota((256, 256), 1)
    perm = as_bf16(before == (after % ROWS) * 2 + after // ROWS)
    lists = jnp.concatenate([owner_ref[...].astype(F32), cell_ref[...].astype(F32)], axis=0)
    lists = dot(lists.astype(BF16), perm)
    share = pick_left(share, perm)
    owner = [lists[m : m + 1].astype(jnp.int32) for m in range(2)]
    cell = [lists[2 + m : 3 + m] for m in range(2)]
    return owner, cell, share


def request_kernel(owner_ref, cell_ref, weight_ref, ids_ref, codes_ref):
    owner, cell, share = make_lists(owner_ref, cell_ref, weight_ref)
    device = iota((128, 256), 0)
    named = [as_bf16(device == owner[m]) for m in range(2)]
    earlier = as_bf16(iota((256, 256), 0) < iota((256, 256), 1))
    ones = jnp.ones((256, 256), BF16)
    ahead = [dot(named[0], earlier), dot(named[1], earlier) + dot(named[0], ones)]
    rank = [
        jnp.sum(named[m].astype(F32) * ahead[m], axis=0, keepdims=True).astype(jnp.int32)
        for m in range(2)
    ]
    slot = iota((128, 256), 0)
    ids = sum(
        dot_nt(named[m], jnp.where(slot == rank[m], cell[m], 0.0).astype(BF16)) for m in range(2)
    )
    ids_ref[...] = ids[:, :SLOTS]
    table = jnp.concatenate(
        [(owner[m] * SLOTS + rank[m]).astype(F32) for m in range(2)]
        + [share, jnp.zeros((124, 256), F32)],
        axis=0,
    )
    codes_ref[...] = jnp.transpose(table)


def in_hbm(x):
    return pltpu.with_memory_space_constraint(x, pltpu.HBM)


def make_request(owner, cell, weight):
    return pl.pallas_call(
        request_kernel,
        out_shape=(pltpu.VMEM((128, SLOTS), F32), pltpu.VMEM((256, LANES), F32)),
        grid=(1,),
        in_specs=[pl.BlockSpec((2, 256), lambda i: (0, 0))] * 3,
        out_specs=(VM,) * 2,
        compiler_params=pltpu.CompilerParams(vmem_limit_bytes=LIMIT),
        cost_estimate=pl.CostEstimate(flops=5 * 10**8, bytes_accessed=2**18, transcendentals=0),
        name="request",
    )(*[in_hbm(x) for x in (owner, cell, weight)])


def pick_left(x, onehot):
    high, middle, low = pieces(x)
    return dot(high, onehot) + (dot(middle, onehot) + dot(low, onehot))


CHUNKS = 4
CHUNK = ROWS // CHUNKS


def edges_kernel(t_ref, s_ref, u_ref, v_ref, k_ref,
                 lon_a_ref, lon_b_ref, lat_a_ref, lat_b_ref, west_ref,
                 t_buf, s_buf, u_buf, k_buf, v_row, k_row, sems, more_sems):
    last = pl.ds(ROWS - 8, 8)
    rows = [
        pltpu.make_async_copy(v_ref.at[:, last, :], v_row, more_sems.at[0]),
        pltpu.make_async_copy(k_ref.at[:, last, :], k_row, more_sems.at[1]),
    ]
    eastern = pl.ds(LANES, LANES)

    def chunk_copies(c):
        part = pl.ds(c * CHUNK, CHUNK)
        return [
            pltpu.make_async_copy(t_ref.at[:, part, :], t_buf.at[:, part, :], sems.at[0, c]),
            pltpu.make_async_copy(s_ref.at[:, part, :], s_buf.at[:, part, :], sems.at[1, c]),
            pltpu.make_async_copy(u_ref.at[:, part, eastern], u_buf.at[:, part, :], sems.at[2, c]),
            pltpu.make_async_copy(k_ref.at[:, part, eastern], k_buf.at[:, part, :], sems.at[3, c]),
        ]

    for c in range(CHUNKS):
        for copy in chunk_copies(c):
            copy.start()
    for copy in rows:
        copy.start()
    odd = is_odd("lon")

    for c in range(CHUNKS):
        for copy in chunk_copies(c):
            copy.wait()

        part = slice(c * CHUNK, (c + 1) * CHUNK)
        west, east = column_edges((t_buf, s_buf), (u_buf, k_buf), part, CHUNK)
        west_ref[part, :] = west
        lon_a_ref[part, :] = jnp.where(odd, west, east)
        lon_b_ref[part, :] = jnp.where(odd, east, west)
    for copy in rows:
        copy.wait()
    south = jnp.concatenate(
        [ref[k, 0:1, :] for ref in (t_buf, s_buf) for k in range(LEVELS)], axis=0
    )
    north = jnp.concatenate(
        [ref[k, ROWS - 1 : ROWS, :] for ref in (t_buf, s_buf) for k in range(LEVELS)], axis=0
    )
    faces = jnp.concatenate(
        [ref[k, 7:8, :] for ref in (v_row, k_row) for k in range(LEVELS)], axis=0
    )
    send_rows(south, north, lat_a_ref, lat_b_ref)
    lat_a_ref[32:64, :] = faces
    lat_b_ref[32:64, :] = faces


def send_rows(south, north, lat_a_ref, lat_b_ref):
    odd = is_odd("lat")
    top = lax.axis_index("lat") == lax.axis_size("lat") - 1
    lat_a_ref[0:32, :] = jnp.where(odd, south, north)
    lat_b_ref[0:32, :] = jnp.where(odd, jnp.where(top, flipped(north), north), south)


def make_edges(fields):
    field = pltpu.VMEM((LEVELS, ROWS, 2 * LANES), F32)
    half = pltpu.VMEM((LEVELS, ROWS, LANES), F32)
    row = pltpu.VMEM((LEVELS, 8, 2 * LANES), F32)
    return pl.pallas_call(
        edges_kernel,
        out_shape=(
            pltpu.VMEM((ROWS, LANES), F32),
            pltpu.VMEM((ROWS, LANES), F32),
            pltpu.VMEM((64, 2 * LANES), F32),
            pltpu.VMEM((64, 2 * LANES), F32),
            pltpu.VMEM((ROWS, LANES), F32),
        ),
        in_specs=[ANY] * 5,
        out_specs=(VM,) * 5,
        scratch_shapes=[
            field, field, half, half, row, row,
            pltpu.SemaphoreType.DMA((4, CHUNKS)),
            pltpu.SemaphoreType.DMA((2,)),
        ],
        compiler_params=pltpu.CompilerParams(vmem_limit_bytes=LIMIT),
        cost_estimate=pl.CostEstimate(flops=10**8, bytes_accessed=8 * 2**20, transcendentals=0),
        name="edges",
    )(*[in_hbm(x) for x in fields])


def answer_kernel(ids_ref, air_ref, wind_ref, *rest):
    out_ref = rest[4]
    ids = ids_ref[...].astype(BF16)
    patches = jnp.concatenate([air_ref[...], wind_ref[...]], axis=1)
    high, middle, low = pieces(patches)
    spread = jnp.ones((SLOTS, 256), BF16)
    chunk = 128
    for part in range(8):
        line = iota((chunk, 128), 0) + part * chunk
        lane = iota((chunk, 128), 1)
        rows = dot(as_bf16(line // SLOTS == lane), ids)
        rows = jnp.where(lane[:, :SLOTS] == line[:, :SLOTS] % SLOTS, rows, 0.0)
        wanted = dot(rows.astype(BF16), spread).astype(jnp.int32)
        onehot = as_bf16(wanted == iota((chunk, 256), 1))
        found = dot(onehot, high) + (dot(onehot, middle) + dot(onehot, low))
        sources = slice(part * 16, part * 16 + 16)
        out_ref[sources, :SLOTS, :] = found[:, :LANES].reshape(16, SLOTS, LANES)
        out_ref[sources, SLOTS:, :] = found[:, LANES:].reshape(16, SLOTS, LANES)


def make_answer(ids, air, wind, through):
    out = pl.pallas_call(
        answer_kernel,
        out_shape=(pltpu.VMEM((128, 2 * SLOTS, LANES), F32),)
        + tuple(pltpu.VMEM(x.shape, F32) for x in through),
        in_specs=[VM] * 3 + [ANY] * 4,
        out_specs=(VM,) + (ANY,) * 4,
        input_output_aliases={3: 1, 4: 2, 5: 3, 6: 4},
        compiler_params=pltpu.CompilerParams(vmem_limit_bytes=LIMIT),
        cost_estimate=pl.CostEstimate(flops=10**9, bytes_accessed=2**21, transcendentals=0),
        name="answer",
    )(in_vmem(ids), air, wind, *[in_vmem(x) for x in through])
    return out[0], out[1:]


def is_odd(axis):
    return lax.rem(lax.axis_index(axis), 2) == 1


def flipped(x):
    back = as_bf16(iota((256, 256), 0) + iota((256, 256), 1) == 255)
    return pick_left(x, back)


class Columns:
    def __init__(self, rows):
        self.lane = iota((rows, LANES), 1)
        self.west = jnp.zeros((rows, LANES), F32)
        self.east = jnp.zeros((rows, LANES), F32)

    def add_west(self, at, x):
        self.west = jnp.where(self.lane == at, roll(x, at, 1), self.west)

    def add_east(self, at, x):
        self.east = jnp.where(self.lane == at, roll(x, at - 127, 1), self.east)


def column_edges(tracers, extra, rows, count):
    columns = Columns(count)
    for t, ref in enumerate(tracers):
        for k in range(LEVELS):
            columns.add_west(LEVELS * t + k, ref[k, rows, :LANES])
    for t, ref in enumerate(tracers):
        for k in range(LEVELS):
            columns.add_east(LEVELS * t + k, ref[k, rows, LANES:])
    for f, ref in enumerate(extra):
        for k in range(LEVELS):
            columns.add_east(64 + LEVELS * f + k, ref[k, rows, :])
    faces = jnp.where(columns.lane >= 64, columns.east, 0.0)
    tracers_east = jnp.where(columns.lane < 64, columns.east, 0.0)
    u = jnp.where(columns.lane < 80, faces, 0.0)
    d = faces - u
    u = roll(u, -32, 1)
    d = roll(d, -16, 1)
    east = tracers_east + (u + roll(u, 16, 1)) + (d + roll(d, 16, 1))
    return columns.west, east


def swap_pairs(first, count):
    route = []
    for low in range(first, count - 1, 2):
        route += [(low, low + 1), (low + 1, low)]
    return route


def exchange(lon_a, lon_b, lat_a, lat_b):
    n_lon, n_lat = lax.axis_size("lon"), lax.axis_size("lat")
    ring = swap_pairs(1, n_lon) + [(n_lon - 1, 0), (0, n_lon - 1)]
    got_lon_a = lax.ppermute(lon_a, "lon", swap_pairs(0, n_lon))
    got_lon_b = lax.ppermute(lon_b, "lon", ring)
    got_lat_a = lax.ppermute(lat_a, "lat", swap_pairs(0, n_lat))
    route = [
        (i * n_lat + low, i * n_lat + high) for i in range(n_lon) for low, high in swap_pairs(1, n_lat)
    ]
    route += [(i * n_lat + n_lat - 1, (n_lon - 1 - i) * n_lat + n_lat - 1) for i in range(n_lon)]
    got_lat_b = lax.ppermute(lat_b, AXES, route)
    return got_lon_a, got_lon_b, got_lat_a, got_lat_b


def density_of(t, s):
    return t * (-0.25 - 0.04 * t + 0.03 * s) + 0.8 * s


def twice_density(t, s):
    return t * (-0.5 - 0.08 * t + 0.06 * s) + 1.6 * s


def step_strip(strip, last, load, u_ref, v_ref, k_ref, mask_ref, side_ref, north_ref, carry_ref, emit, heat_ref=None):
    rows = pl.ds(strip, 8)
    lane = iota((8, LANES), 1)
    sub = iota((8, LANES), 0)
    first_lane, last_lane = lane == 0, lane == LANES - 1
    row0, row7 = sub == 0, sub == 7
    halves = (slice(0, LANES), slice(LANES, 2 * LANES))
    mask = [mask_ref[rows, h].astype(F32) for h in halves]
    x = [load(t, 0, strip) for t in range(2)]
    rho = [twice_density(x[0][h], x[1][h]) for h in range(2)]
    below = None
    for k in range(LEVELS):
        if k < LEVELS - 1:
            x_next = [load(t, k + 1, strip) for t in range(2)]
            rho_next = [twice_density(x_next[0][h], x_next[1][h]) for h in range(2)]
            mixing = [0.06 + 0.05 * jnp.tanh(rho[h] - rho_next[h]) for h in range(2)]
        u = [u_ref[k, rows, h] for h in halves]
        v = [v_ref[k, rows, h] for h in halves]
        d = [k_ref[k, rows, h] for h in halves]
        pe = [jnp.maximum(u[h], 0.0) + d[h] for h in range(2)]
        ne = [jnp.minimum(u[h], 0.0) - d[h] for h in range(2)]
        pn = [jnp.maximum(v[h], 0.0) + d[h] for h in range(2)]
        nn = [jnp.minimum(v[h], 0.0) - d[h] for h in range(2)]
        above = [None, None]
        new = [None, None]
        for t in range(2):
            at = LEVELS * t + k
            xt = x[t]
            side = side_ref[at, rows, :]
            y = [roll(xt[h], -1, 1) for h in range(2)]
            xe = [
                jnp.where(last_lane, y[1], y[0]),
                jnp.where(last_lane, side, y[1]),
            ]
            east = [pe[h] * xt[h] + ne[h] * xe[h] for h in range(2)]
            z = [roll(east[h], 1, 1) for h in range(2)]
            west = [
                jnp.where(first_lane, side, z[0]),
                jnp.where(first_lane, z[0], z[1]),
            ]
            if last:
                ahead = [jnp.broadcast_to(north_ref[at : at + 1, h], (8, LANES)) for h in halves]
            else:
                ahead = load(t, k, strip + 8)
            xn = [roll(jnp.where(row0, ahead[h], xt[h]), -1, 0) for h in range(2)]
            north = [pn[h] * xt[h] + nn[h] * xn[h] for h in range(2)]
            south = [
                roll(jnp.where(row7, carry_ref[at, :, halves[h]], north[h]), 1, 0) for h in range(2)
            ]
            if not last:
                for h in range(2):
                    carry_ref[at, :, halves[h]] = north[h]
            tend = [(west[h] - east[h]) + (south[h] - north[h]) for h in range(2)]
            if k < LEVELS - 1:
                above[t] = [mixing[h] * (x_next[t][h] - xt[h]) for h in range(2)]
                tend = [tend[h] + above[t][h] for h in range(2)]
            if k > 0:
                tend = [tend[h] - below[t][h] for h in range(2)]
            if heat_ref is not None and t == 0 and k == 0:
                tend = [tend[h] + heat_ref[rows, halves[h]] for h in range(2)]
            new[t] = [xt[h] + mask[h] * tend[h] for h in range(2)]
        emit(k, strip, new)
        below = above
        if k < LEVELS - 1:
            x, rho = x_next, rho_next


def west_fluxes(west, coef, own):
    u = roll(coef, -32, 1)
    d = roll(coef, -64, 1)
    return (jnp.maximum(u, 0.0) + d) * west + (jnp.minimum(u, 0.0) - d) * own


def first_carry(south, faces, load_row, carry_ref):
    for k in range(LEVELS):
        v, d = faces(k), faces(LEVELS + k)
        pn = jnp.maximum(v, 0.0) + d
        nn = jnp.minimum(v, 0.0) - d
        for t in range(2):
            at = LEVELS * t + k
            flux = pn * south(at) + nn * load_row(t, k)
            carry_ref[at] = jnp.broadcast_to(flux, (8, 2 * LANES))


def halo_setup(odd_lon, odd_lat, got, coefs, own_ref, load_row, carry_ref, side_ref, north_ref):
    lon_a, lon_b, lat_a, lat_b = got
    c_lon_a, c_lon_b, c_lat_a, c_lat_b = coefs
    west = jnp.where(odd_lon, lon_a[...], lon_b[...])
    coef = jnp.where(odd_lon, c_lon_a[...], c_lon_b[...])
    flux = west_fluxes(west, coef, own_ref[...])
    east = jnp.where(odd_lon, lon_b[...], lon_a[...])
    last_lane = iota((ROWS, LANES), 1) == LANES - 1
    for at in range(2 * LEVELS):
        side_ref[at] = jnp.where(last_lane, roll(east, 127 - at, 1), roll(flux, -at, 1))
    north_ref[...] = jnp.where(odd_lat, lat_b[0:32, :], lat_a[0:32, :])

    def south(at):
        return jnp.where(odd_lat, lat_a[at : at + 1, :], lat_b[at : at + 1, :])

    def faces(at):
        return jnp.where(odd_lat, c_lat_a[32 + at : 33 + at, :], c_lat_b[32 + at : 33 + at, :])

    first_carry(south, faces, load_row, carry_ref)


def pair_loader(refs, top_ref=None):
    def load(t, k, strip):
        rows = pl.ds(strip, 8)
        if t == 0 and k == 0 and top_ref is not None:
            return [top_ref[rows, :LANES], top_ref[rows, LANES:]]
        return [refs[t][k, rows, :LANES], refs[t][k, rows, LANES:]]

    def load_row(t, k):
        if t == 0 and k == 0 and top_ref is not None:
            return top_ref[0:1, :]
        return refs[t][k, 0:1, :]

    return load, load_row


def strips(body):
    def one(i, carry):
        body(pl.multiple_of(i * 8, 8), False)
        return carry

    lax.fori_loop(0, ROWS // 8 - 1, one, 0)
    body(ROWS - 8, True)


def first_kernel(t_hbm, s_hbm, u_hbm, v_hbm, k_hbm, mask_hbm, own_ref, lon_a, lon_b, lat_a, lat_b,
                 t_out, s_out, top_out, west_out, east_out, south_out, north_out,
                 carry_ref, side_ref, north_ref,
                 t_ref, s_ref, u_ref, v_ref, k_ref, t_new, s_new, mask_ref, sems, out_sems):
    sources = (t_hbm, s_hbm, u_hbm, v_hbm, k_hbm)
    bufs = (t_ref, s_ref, u_ref, v_ref, k_ref)
    new_bufs = (t_new, s_new)
    outs = (t_out, s_out)

    def copy_in(f, index):
        rows = pl.ds(pl.multiple_of(index * 8, 8), 8)
        return pltpu.make_async_copy(sources[f].at[:, rows, :], bufs[f].at[:, rows, :], sems.at[f, index])

    def copy_out(t, index):
        rows = pl.ds(pl.multiple_of(index * 8, 8), 8)
        return pltpu.make_async_copy(new_bufs[t].at[:, rows, :], outs[t].at[:, rows, :], out_sems.at[t, index])

    def start(index, carry):
        for f in range(5):
            copy_in(f, index).start()
        return carry

    mask_copy = pltpu.make_async_copy(mask_hbm, mask_ref, sems.at[5, 0])
    start(0, 0)
    mask_copy.start()
    lax.fori_loop(1, STRIPS, start, 0)
    copy_in(0, 0).wait()
    copy_in(1, 0).wait()
    load, load_row = pair_loader((t_ref, s_ref))
    got = (lon_a, lon_b, lat_a, lat_b)
    halo_setup(is_odd("lon"), is_odd("lat"), got, got, own_ref, load_row, carry_ref, side_ref, north_ref)
    mask_copy.wait()

    def body(strip, last):
        index = STRIPS - 1 if last else strip // 8
        for f in range(2, 5):
            copy_in(f, index).wait()
        if not last:
            for f in range(2):
                copy_in(f, index + 1).wait()
        columns = Columns(8)

        def emit(k, strip, new):
            rows = pl.ds(strip, 8)
            for t in range(2):
                for h in range(2):
                    new_bufs[t][k, rows, h * LANES : (h + 1) * LANES] = new[t][h]
                    if t == 0 and k == 0:
                        top_out[rows, h * LANES : (h + 1) * LANES] = new[t][h]
                columns.add_west(LEVELS * t + k, new[t][0])
                columns.add_east(LEVELS * t + k, new[t][1])

        step_strip(strip, last, load, u_ref, v_ref, k_ref, mask_ref, side_ref, north_ref, carry_ref, emit)
        west_out[pl.ds(strip, 8), :] = columns.west
        east_out[pl.ds(strip, 8), :] = columns.east
        for t in range(2):
            copy_out(t, index).start()

    strips(body)
    south_out[...] = jnp.concatenate([ref[k, 0:1, :] for ref in new_bufs for k in range(LEVELS)], axis=0)
    north_out[...] = jnp.concatenate(
        [ref[k, ROWS - 1 : ROWS, :] for ref in new_bufs for k in range(LEVELS)], axis=0
    )

    def finish(index, carry):
        for t in range(2):
            copy_out(t, index).wait()
        return carry

    lax.fori_loop(0, STRIPS, finish, 0)


STEP_SCRATCH = [
    pltpu.VMEM((2 * LEVELS, 8, 2 * LANES), F32),
    pltpu.VMEM((2 * LEVELS, ROWS, LANES), F32),
    pltpu.VMEM((2 * LEVELS, 2 * LANES), F32),
]
STEP_COST = pl.CostEstimate(flops=7 * 10**7, bytes_accessed=25 * 2**20, transcendentals=10**6)


def first_step(fields, mask, own, got):
    shape = pltpu.HBM((LEVELS, ROWS, 2 * LANES), F32)
    buf = pltpu.VMEM((LEVELS, ROWS, 2 * LANES), F32)
    return pl.pallas_call(
        first_kernel,
        out_shape=(
            shape,
            shape,
            pltpu.VMEM((ROWS, 2 * LANES), F32),
            pltpu.VMEM((ROWS, LANES), F32),
            pltpu.VMEM((ROWS, LANES), F32),
            pltpu.VMEM((2 * LEVELS, 2 * LANES), F32),
            pltpu.VMEM((2 * LEVELS, 2 * LANES), F32),
        ),
        in_specs=[ANY] * 6 + [VM] * 5,
        out_specs=(ANY, ANY) + (VM,) * 5,
        scratch_shapes=STEP_SCRATCH
        + [buf] * 7
        + [pltpu.VMEM((ROWS, 2 * LANES), jnp.int32), pltpu.SemaphoreType.DMA((6, STRIPS)), pltpu.SemaphoreType.DMA((2, STRIPS))],
        compiler_params=pltpu.CompilerParams(vmem_limit_bytes=LIMIT),
        cost_estimate=STEP_COST,
        name="first_step",
    )(*[in_hbm(x) for x in fields], in_hbm(mask), own, *got)


def heat_kernel(top_ref, west_ref, east_ref, south_ref, north_ref, mask_hbm, t_hbm, back_ref, codes_ref,
                heat_out, top_out, lon_a_ref, lon_b_ref, lat_a_ref, lat_b_ref, own_out, mask_ref, t_ref, sems):
    mask_copy = pltpu.make_async_copy(mask_hbm, mask_ref, sems.at[0])
    mask_copy.start()
    t_copy = pltpu.make_async_copy(t_hbm.at[0], t_ref, sems.at[1])
    t_copy.start()
    air = back_ref[:, :SLOTS, :].reshape(128 * SLOTS, LANES)
    wind = back_ref[:, SLOTS:, :].reshape(128 * SLOTS, LANES)
    high, middle, low = pieces(jnp.concatenate([air, wind], axis=1))
    codes = codes_ref[...]
    lane = iota((256, 1024), 1)
    t_copy.wait()
    surface = jnp.concatenate([t_ref[:, :LANES], t_ref[:, LANES:]], axis=0)
    heat = None
    for m in range(2):
        onehot = as_bf16(codes[:, m : m + 1].astype(jnp.int32) == lane)
        found = dot(onehot, high) + (dot(onehot, middle) + dot(onehot, low))
        flux = BULK * found[:, LANES:] * (found[:, :LANES] - surface)
        part = codes[:, 2 + m : 3 + m] * flux
        heat = part if heat is None else heat + part
    mask_copy.wait()
    mask = mask_ref[...].astype(F32)
    added = []
    for h in range(2):
        cols = slice(h * LANES, (h + 1) * LANES)
        here = heat[h * ROWS : (h + 1) * ROWS]
        heat_out[:, cols] = here
        added.append(mask[:, cols] * here)
        top_out[:, cols] = top_ref[:, cols] + added[h]
    first = iota((ROWS, LANES), 1) == 0
    west = west_ref[...] + jnp.where(first, added[0], 0.0)
    east = east_ref[...] + jnp.where(first, roll(added[1], 1, 1), 0.0)
    own_out[...] = west
    odd = is_odd("lon")
    lon_a_ref[...] = jnp.where(odd, west, east)
    lon_b_ref[...] = jnp.where(odd, east, west)
    south = jnp.concatenate([top_out[0:1, :], south_ref[1:, :]], axis=0)
    north = jnp.concatenate([top_out[ROWS - 1 : ROWS, :], north_ref[1:, :]], axis=0)
    send_rows(south, north, lat_a_ref, lat_b_ref)


def add_heat(top, west, east, south, north, mask, temp, back, codes):
    return pl.pallas_call(
        heat_kernel,
        out_shape=(
            pltpu.VMEM((ROWS, 2 * LANES), F32),
            pltpu.VMEM((ROWS, 2 * LANES), F32),
            pltpu.VMEM((ROWS, LANES), F32),
            pltpu.VMEM((ROWS, LANES), F32),
            pltpu.VMEM((32, 2 * LANES), F32),
            pltpu.VMEM((32, 2 * LANES), F32),
            pltpu.VMEM((ROWS, LANES), F32),
        ),
        in_specs=[VM] * 5 + [ANY] * 2 + [VM] * 2,
        out_specs=(VM,) * 7,
        scratch_shapes=[
            pltpu.VMEM((ROWS, 2 * LANES), jnp.int32),
            pltpu.VMEM((ROWS, 2 * LANES), F32),
            pltpu.SemaphoreType.DMA((2,)),
        ],
        compiler_params=pltpu.CompilerParams(vmem_limit_bytes=LIMIT),
        cost_estimate=pl.CostEstimate(flops=10**9, bytes_accessed=2**20, transcendentals=0),
        name="heat",
    )(*[in_vmem(x) for x in (top, west, east, south, north)], in_hbm(mask), in_hbm(temp), in_vmem(back), in_vmem(codes))


def second_kernel(t_hbm, s_hbm, u_hbm, v_hbm, k_hbm, mask_hbm, top_ref, heat_ref, own_ref,
                  lon_a, lon_b, lat_a, lat_b, c_lon_a, c_lon_b, c_lat_a, c_lat_b,
                  t_out, s_out, rho_out,
                  carry_ref, side_ref, north_ref,
                  t_ref, s_ref, u_ref, v_ref, k_ref, t_buf, s_buf, rho_buf, mask_ref, in_sems, sems):
    sources = (t_hbm, s_hbm, u_hbm, v_hbm, k_hbm)
    held = (t_ref, s_ref, u_ref, v_ref, k_ref)

    def copy_in(t, index):
        rows = pl.ds(pl.multiple_of(index * 8, 8), 8)
        return pltpu.make_async_copy(sources[t].at[:, rows, :], held[t].at[:, rows, :], in_sems.at[t, index])

    def start(index, carry):
        for f in range(5):
            copy_in(f, index).start()
        return carry

    mask_copy = pltpu.make_async_copy(mask_hbm, mask_ref, in_sems.at[5, 0])
    start(0, 0)
    mask_copy.start()
    lax.fori_loop(1, STRIPS, start, 0)
    copy_in(0, 0).wait()
    copy_in(1, 0).wait()
    load, load_row = pair_loader((t_ref, s_ref), top_ref)
    halo_setup(is_odd("lon"), is_odd("lat"), (lon_a, lon_b, lat_a, lat_b), (c_lon_a, c_lon_b, c_lat_a, c_lat_b),
               own_ref, load_row, carry_ref, side_ref, north_ref)
    mask_copy.wait()
    bufs = (t_buf, s_buf, rho_buf)
    outs = (t_out, s_out, rho_out)

    def emit(k, strip, new):
        for h in range(2):
            at = (k, pl.ds(strip, 8), slice(h * LANES, (h + 1) * LANES))
            for t in range(2):
                bufs[t][at] = new[t][h]
            rho_buf[at] = density_of(new[0][h], new[1][h])

    def copies(index):
        rows = pl.ds(pl.multiple_of(index * 8, 8), 8)
        return [
            pltpu.make_async_copy(bufs[n].at[:, rows, :], outs[n].at[:, rows, :], sems.at[n, index])
            for n in range(3)
        ]

    def body(strip, last):
        index = STRIPS - 1 if last else strip // 8
        for f in range(2, 5):
            copy_in(f, index).wait()
        if not last:
            for t in range(2):
                copy_in(t, index + 1).wait()
        step_strip(strip, last, load, u_ref, v_ref, k_ref, mask_ref, side_ref, north_ref, carry_ref, emit, heat_ref)
        for copy in copies(index):
            copy.start()

    strips(body)

    def finish(index, carry):
        for copy in copies(index):
            copy.wait()
        return carry

    lax.fori_loop(0, STRIPS, finish, 0)


def second_step(t, s, fields, mask, top, heat, own, got, coefs):
    shape = jax.ShapeDtypeStruct((LEVELS, ROWS, 2 * LANES), F32)
    buf = pltpu.VMEM((LEVELS, ROWS, 2 * LANES), F32)
    return pl.pallas_call(
        second_kernel,
        out_shape=(shape, shape, shape),
        in_specs=[ANY] * 6 + [VM] * 11,
        out_specs=(ANY, ANY, ANY),
        scratch_shapes=STEP_SCRATCH
        + [buf] * 8
        + [pltpu.VMEM((ROWS, 2 * LANES), jnp.int32), pltpu.SemaphoreType.DMA((6, STRIPS)), pltpu.SemaphoreType.DMA((3, STRIPS))],
        compiler_params=pltpu.CompilerParams(vmem_limit_bytes=LIMIT),
        cost_estimate=STEP_COST,
        name="second_step",
    )(in_hbm(t), in_hbm(s), *[in_hbm(x) for x in fields], in_hbm(mask), in_vmem(top), in_vmem(heat), in_vmem(own), *[in_vmem(g) for g in got], *coefs)


def body(
    temp,
    salt,
    east_face_velocity,
    v_face,
    kappa,
    land_mask,
    margin_owner_device,
    margin_cell,
    margin_weight,
    air_temp,
    wind_speed,
):
    def lists(x):
        return jnp.transpose(x.reshape(256, 2))

    fields = (temp, salt, east_face_velocity, v_face, kappa)
    ids, codes = make_request(
        lists(margin_owner_device), lists(margin_cell), lists(margin_weight)
    )
    ids = lax.all_to_all(ids, AXES, split_axis=0, concat_axis=0, tiled=True)
    *sent, own = make_edges(fields)
    answer, sent = make_answer(
        ids, air_temp.reshape(256, LANES), wind_speed.reshape(256, LANES), sent
    )
    back = lax.all_to_all(answer, AXES, split_axis=0, concat_axis=0, tiled=True)
    halos = [in_vmem(g) for g in exchange(*sent)]
    t1, s1, *edges = first_step(fields, land_mask, in_vmem(own), halos)
    heat, top, *sent, own = add_heat(*edges, land_mask, temp, back, codes)
    later = exchange(*sent)
    return second_step(t1, s1, fields[2:], land_mask, top, heat, own, later, halos)


def solution(mesh):
    grid = P(None, "lat", "lon")
    lists = P("lat", "lon", None, None)
    owned = P("lon", "lat", None, None)
    in_specs = (grid,) * 5 + (P("lat", "lon"),) + (lists,) * 3 + (owned,) * 2
    return jax.shard_map(body, mesh=mesh, in_specs=in_specs, out_specs=(grid,) * 3, check_vma=False)
```

```python
import jax
import jax.numpy as jnp
from jax import lax
from jax.experimental import pallas as pl
from jax.experimental.pallas import tpu as pltpu
from jax.sharding import PartitionSpec as P

F32 = jnp.float32
BF16 = jnp.bfloat16
AXES = ("lon", "lat")
BULK = 0.1
SLOTS = 8
LEVELS = 16
ROWS = 128
LANES = 128
STRIPS = ROWS // 8
LIMIT = 24 * 1024 * 1024

VM = pl.BlockSpec(memory_space=pltpu.VMEM)
ANY = pl.BlockSpec(memory_space=pl.ANY)


def in_vmem(x):
    return pltpu.with_memory_space_constraint(x, pltpu.VMEM)


def dot(a, b):
    return jnp.dot(a, b, preferred_element_type=F32)


def dot_nt(a, b):
    return lax.dot_general(a, b, (((1,), (1,)), ((), ())), preferred_element_type=F32)


def pieces(x):
    high = x.astype(BF16)
    rest = x - high.astype(F32)
    middle = rest.astype(BF16)
    low = (rest - middle.astype(F32)).astype(BF16)
    return high, middle, low


def pick(onehot, x):
    high, middle, low = pieces(x)
    return dot(onehot, high) + (dot(onehot, middle) + dot(onehot, low))


def iota(shape, dim):
    return lax.broadcasted_iota(jnp.int32, shape, dim)


def roll(x, steps, axis):
    steps = steps % x.shape[axis]
    return x if steps == 0 else pltpu.roll(x, steps, axis)


def as_bf16(flag):
    return flag.astype(F32).astype(BF16)


def make_lists(owner_ref, cell_ref, weight_ref):
    w = weight_ref[...]
    share = w / (w[0:1] + w[1:2])
    before = iota((256, 256), 0)
    after = iota((256, 256), 1)
    perm = as_bf16(before == (after % ROWS) * 2 + after // ROWS)
    lists = jnp.concatenate([owner_ref[...].astype(F32), cell_ref[...].astype(F32)], axis=0)
    lists = dot(lists.astype(BF16), perm)
    share = pick_left(share, perm)
    owner = [lists[m : m + 1].astype(jnp.int32) for m in range(2)]
    cell = [lists[2 + m : 3 + m] for m in range(2)]
    return owner, cell, share


def request_kernel(owner_ref, cell_ref, weight_ref, ids_ref, codes_ref):
    owner, cell, share = make_lists(owner_ref, cell_ref, weight_ref)
    device = iota((128, 256), 0)
    named = [as_bf16(device == owner[m]) for m in range(2)]
    earlier = as_bf16(iota((256, 256), 0) < iota((256, 256), 1))
    ones = jnp.ones((256, 256), BF16)
    ahead = [dot(named[0], earlier), dot(named[1], earlier) + dot(named[0], ones)]
    rank = [
        jnp.sum(named[m].astype(F32) * ahead[m], axis=0, keepdims=True).astype(jnp.int32)
        for m in range(2)
    ]
    slot = iota((128, 256), 0)
    ids = sum(
        dot_nt(named[m], jnp.where(slot == rank[m], cell[m], 0.0).astype(BF16)) for m in range(2)
    )
    ids_ref[...] = ids[:, :SLOTS]
    table = jnp.concatenate(
        [(owner[m] * SLOTS + rank[m]).astype(F32) for m in range(2)]
        + [share, jnp.zeros((124, 256), F32)],
        axis=0,
    )
    codes_ref[...] = jnp.transpose(table)


def in_hbm(x):
    return pltpu.with_memory_space_constraint(x, pltpu.HBM)


def make_request(owner, cell, weight):
    return pl.pallas_call(
        request_kernel,
        out_shape=(pltpu.VMEM((128, SLOTS), F32), pltpu.VMEM((256, LANES), F32)),
        grid=(1,),
        in_specs=[pl.BlockSpec((2, 256), lambda i: (0, 0))] * 3,
        out_specs=(VM,) * 2,
        compiler_params=pltpu.CompilerParams(vmem_limit_bytes=LIMIT),
        cost_estimate=pl.CostEstimate(flops=5 * 10**8, bytes_accessed=2**18, transcendentals=0),
        name="request",
    )(*[in_hbm(x) for x in (owner, cell, weight)])


def pick_left(x, onehot):
    high, middle, low = pieces(x)
    return dot(high, onehot) + (dot(middle, onehot) + dot(low, onehot))


CHUNKS = 4
CHUNK = ROWS // CHUNKS


def edges_kernel(t_ref, s_ref, u_ref, v_ref, k_ref,
                 lon_a_ref, lon_b_ref, lat_a_ref, lat_b_ref, west_ref,
                 t_buf, s_buf, u_buf, k_buf, v_row, k_row, sems, more_sems):
    last = pl.ds(ROWS - 8, 8)
    rows = [
        pltpu.make_async_copy(v_ref.at[:, last, :], v_row, more_sems.at[0]),
        pltpu.make_async_copy(k_ref.at[:, last, :], k_row, more_sems.at[1]),
    ]
    eastern = pl.ds(LANES, LANES)

    def chunk_copies(c):
        part = pl.ds(c * CHUNK, CHUNK)
        return [
            pltpu.make_async_copy(t_ref.at[:, part, :], t_buf.at[:, part, :], sems.at[0, c]),
            pltpu.make_async_copy(s_ref.at[:, part, :], s_buf.at[:, part, :], sems.at[1, c]),
            pltpu.make_async_copy(u_ref.at[:, part, eastern], u_buf.at[:, part, :], sems.at[2, c]),
            pltpu.make_async_copy(k_ref.at[:, part, eastern], k_buf.at[:, part, :], sems.at[3, c]),
        ]

    for c in range(CHUNKS):
        for copy in chunk_copies(c):
            copy.start()
    for copy in rows:
        copy.start()
    odd = is_odd("lon")

    for c in range(CHUNKS):
        for copy in chunk_copies(c):
            copy.wait()

        part = slice(c * CHUNK, (c + 1) * CHUNK)
        west, east = column_edges((t_buf, s_buf), (u_buf, k_buf), part, CHUNK)
        west_ref[part, :] = west
        lon_a_ref[part, :] = jnp.where(odd, west, east)
        lon_b_ref[part, :] = jnp.where(odd, east, west)
    for copy in rows:
        copy.wait()
    south = jnp.concatenate(
        [ref[k, 0:1, :] for ref in (t_buf, s_buf) for k in range(LEVELS)], axis=0
    )
    north = jnp.concatenate(
        [ref[k, ROWS - 1 : ROWS, :] for ref in (t_buf, s_buf) for k in range(LEVELS)], axis=0
    )
    faces = jnp.concatenate(
        [ref[k, 7:8, :] for ref in (v_row, k_row) for k in range(LEVELS)], axis=0
    )
    send_rows(south, north, lat_a_ref, lat_b_ref)
    lat_a_ref[32:64, :] = faces
    lat_b_ref[32:64, :] = faces


def send_rows(south, north, lat_a_ref, lat_b_ref):
    odd = is_odd("lat")
    top = lax.axis_index("lat") == lax.axis_size("lat") - 1
    lat_a_ref[0:32, :] = jnp.where(odd, south, north)
    lat_b_ref[0:32, :] = jnp.where(odd, jnp.where(top, flipped(north), north), south)


def make_edges(fields):
    field = pltpu.VMEM((LEVELS, ROWS, 2 * LANES), F32)
    half = pltpu.VMEM((LEVELS, ROWS, LANES), F32)
    row = pltpu.VMEM((LEVELS, 8, 2 * LANES), F32)
    return pl.pallas_call(
        edges_kernel,
        out_shape=(
            pltpu.VMEM((ROWS, LANES), F32),
            pltpu.VMEM((ROWS, LANES), F32),
            pltpu.VMEM((64, 2 * LANES), F32),
            pltpu.VMEM((64, 2 * LANES), F32),
            pltpu.VMEM((ROWS, LANES), F32),
        ),
        in_specs=[ANY] * 5,
        out_specs=(VM,) * 5,
        scratch_shapes=[
            field, field, half, half, row, row,
            pltpu.SemaphoreType.DMA((4, CHUNKS)),
            pltpu.SemaphoreType.DMA((2,)),
        ],
        compiler_params=pltpu.CompilerParams(vmem_limit_bytes=LIMIT),
        cost_estimate=pl.CostEstimate(flops=10**8, bytes_accessed=8 * 2**20, transcendentals=0),
        name="edges",
    )(*[in_hbm(x) for x in fields])


def answer_kernel(ids_ref, air_ref, wind_ref, *rest):
    out_ref = rest[-1]
    ids = ids_ref[...].astype(BF16)
    patches = jnp.concatenate([air_ref[...], wind_ref[...]], axis=1)
    high, middle, low = pieces(patches)
    spread = jnp.ones((SLOTS, 256), BF16)
    chunk = 128
    for part in range(8):
        line = iota((chunk, 128), 0) + part * chunk
        lane = iota((chunk, 128), 1)
        rows = dot(as_bf16(line // SLOTS == lane), ids)
        rows = jnp.where(lane[:, :SLOTS] == line[:, :SLOTS] % SLOTS, rows, 0.0)
        wanted = dot(rows.astype(BF16), spread).astype(jnp.int32)
        onehot = as_bf16(wanted == iota((chunk, 256), 1))
        found = dot(onehot, high) + (dot(onehot, middle) + dot(onehot, low))
        sources = slice(part * 16, part * 16 + 16)
        out_ref[sources, :SLOTS, :] = found[:, :LANES].reshape(16, SLOTS, LANES)
        out_ref[sources, SLOTS:, :] = found[:, LANES:].reshape(16, SLOTS, LANES)


def make_answer(ids, air, wind, after):
    return pl.pallas_call(
        answer_kernel,
        out_shape=pltpu.VMEM((128, 2 * SLOTS, LANES), F32),
        in_specs=[VM] * 3 + [ANY] * len(after),
        out_specs=VM,
        compiler_params=pltpu.CompilerParams(vmem_limit_bytes=LIMIT),
        cost_estimate=pl.CostEstimate(flops=10**9, bytes_accessed=2**21, transcendentals=0),
        name="answer",
    )(in_vmem(ids), air, wind, *after)


def is_odd(axis):
    return lax.rem(lax.axis_index(axis), 2) == 1


def flipped(x):
    back = as_bf16(iota((256, 256), 0) + iota((256, 256), 1) == 255)
    return pick_left(x, back)


class Columns:
    def __init__(self, rows):
        self.lane = iota((rows, LANES), 1)
        self.west = jnp.zeros((rows, LANES), F32)
        self.east = jnp.zeros((rows, LANES), F32)

    def add_west(self, at, x):
        self.west = jnp.where(self.lane == at, roll(x, at, 1), self.west)

    def add_east(self, at, x):
        self.east = jnp.where(self.lane == at, roll(x, at - 127, 1), self.east)


def column_edges(tracers, extra, rows, count):
    columns = Columns(count)
    for t, ref in enumerate(tracers):
        for k in range(LEVELS):
            columns.add_west(LEVELS * t + k, ref[k, rows, :LANES])
    for t, ref in enumerate(tracers):
        for k in range(LEVELS):
            columns.add_east(LEVELS * t + k, ref[k, rows, LANES:])
    for f, ref in enumerate(extra):
        for k in range(LEVELS):
            columns.add_east(64 + LEVELS * f + k, ref[k, rows, :])
    faces = jnp.where(columns.lane >= 64, columns.east, 0.0)
    tracers_east = jnp.where(columns.lane < 64, columns.east, 0.0)
    u = jnp.where(columns.lane < 80, faces, 0.0)
    d = faces - u
    u = roll(u, -32, 1)
    d = roll(d, -16, 1)
    east = tracers_east + (u + roll(u, 16, 1)) + (d + roll(d, 16, 1))
    return columns.west, east


def swap_pairs(first, count):
    route = []
    for low in range(first, count - 1, 2):
        route += [(low, low + 1), (low + 1, low)]
    return route


def exchange(lon_a, lon_b, lat_a, lat_b):
    n_lon, n_lat = lax.axis_size("lon"), lax.axis_size("lat")
    ring = swap_pairs(1, n_lon) + [(n_lon - 1, 0), (0, n_lon - 1)]
    got_lon_a = lax.ppermute(lon_a, "lon", swap_pairs(0, n_lon))
    got_lon_b = lax.ppermute(lon_b, "lon", ring)
    got_lat_a = lax.ppermute(lat_a, "lat", swap_pairs(0, n_lat))
    route = [
        (i * n_lat + low, i * n_lat + high) for i in range(n_lon) for low, high in swap_pairs(1, n_lat)
    ]
    route += [(i * n_lat + n_lat - 1, (n_lon - 1 - i) * n_lat + n_lat - 1) for i in range(n_lon)]
    got_lat_b = lax.ppermute(lat_b, AXES, route)
    return got_lon_a, got_lon_b, got_lat_a, got_lat_b


def density_of(t, s):
    return t * (-0.25 - 0.04 * t + 0.03 * s) + 0.8 * s


def twice_density(t, s):
    return t * (-0.5 - 0.08 * t + 0.06 * s) + 1.6 * s


def step_strip(strip, last, load, u_ref, v_ref, k_ref, mask_ref, side_ref, north_ref, carry_ref, emit, heat_ref=None):
    rows = pl.ds(strip, 8)
    lane = iota((8, LANES), 1)
    sub = iota((8, LANES), 0)
    first_lane, last_lane = lane == 0, lane == LANES - 1
    row0, row7 = sub == 0, sub == 7
    halves = (slice(0, LANES), slice(LANES, 2 * LANES))
    mask = [mask_ref[rows, h].astype(F32) for h in halves]
    x = [load(t, 0, strip) for t in range(2)]
    rho = [twice_density(x[0][h], x[1][h]) for h in range(2)]
    below = None
    for k in range(LEVELS):
        if k < LEVELS - 1:
            x_next = [load(t, k + 1, strip) for t in range(2)]
            rho_next = [twice_density(x_next[0][h], x_next[1][h]) for h in range(2)]
            mixing = [0.06 + 0.05 * jnp.tanh(rho[h] - rho_next[h]) for h in range(2)]
        u = [u_ref[k, rows, h] for h in halves]
        v = [v_ref[k, rows, h] for h in halves]
        d = [k_ref[k, rows, h] for h in halves]
        pe = [jnp.maximum(u[h], 0.0) + d[h] for h in range(2)]
        ne = [jnp.minimum(u[h], 0.0) - d[h] for h in range(2)]
        pn = [jnp.maximum(v[h], 0.0) + d[h] for h in range(2)]
        nn = [jnp.minimum(v[h], 0.0) - d[h] for h in range(2)]
        above = [None, None]
        new = [None, None]
        for t in range(2):
            at = LEVELS * t + k
            xt = x[t]
            side = side_ref[at, rows, :]
            y = [roll(xt[h], -1, 1) for h in range(2)]
            xe = [
                jnp.where(last_lane, y[1], y[0]),
                jnp.where(last_lane, side, y[1]),
            ]
            east = [pe[h] * xt[h] + ne[h] * xe[h] for h in range(2)]
            z = [roll(east[h], 1, 1) for h in range(2)]
            west = [
                jnp.where(first_lane, side, z[0]),
                jnp.where(first_lane, z[0], z[1]),
            ]
            if last:
                ahead = [jnp.broadcast_to(north_ref[at : at + 1, h], (8, LANES)) for h in halves]
            else:
                ahead = load(t, k, strip + 8)
            xn = [roll(jnp.where(row0, ahead[h], xt[h]), -1, 0) for h in range(2)]
            north = [pn[h] * xt[h] + nn[h] * xn[h] for h in range(2)]
            south = [
                roll(jnp.where(row7, carry_ref[at, :, halves[h]], north[h]), 1, 0) for h in range(2)
            ]
            if not last:
                for h in range(2):
                    carry_ref[at, :, halves[h]] = north[h]
            tend = [(west[h] - east[h]) + (south[h] - north[h]) for h in range(2)]
            if k < LEVELS - 1:
                above[t] = [mixing[h] * (x_next[t][h] - xt[h]) for h in range(2)]
                tend = [tend[h] + above[t][h] for h in range(2)]
            if k > 0:
                tend = [tend[h] - below[t][h] for h in range(2)]
            if heat_ref is not None and t == 0 and k == 0:
                tend = [tend[h] + heat_ref[rows, halves[h]] for h in range(2)]
            new[t] = [xt[h] + mask[h] * tend[h] for h in range(2)]
        emit(k, strip, new)
        below = above
        if k < LEVELS - 1:
            x, rho = x_next, rho_next


def west_fluxes(west, coef, own):
    u = roll(coef, -32, 1)
    d = roll(coef, -64, 1)
    return (jnp.maximum(u, 0.0) + d) * west + (jnp.minimum(u, 0.0) - d) * own


def first_carry(south, faces, load_row, carry_ref):
    for k in range(LEVELS):
        v, d = faces(k), faces(LEVELS + k)
        pn = jnp.maximum(v, 0.0) + d
        nn = jnp.minimum(v, 0.0) - d
        for t in range(2):
            at = LEVELS * t + k
            flux = pn * south(at) + nn * load_row(t, k)
            carry_ref[at] = jnp.broadcast_to(flux, (8, 2 * LANES))


def halo_setup(odd_lon, odd_lat, got, coefs, own_ref, load_row, carry_ref, side_ref, north_ref):
    lon_a, lon_b, lat_a, lat_b = got
    c_lon_a, c_lon_b, c_lat_a, c_lat_b = coefs
    west = jnp.where(odd_lon, lon_a[...], lon_b[...])
    coef = jnp.where(odd_lon, c_lon_a[...], c_lon_b[...])
    flux = west_fluxes(west, coef, own_ref[...])
    east = jnp.where(odd_lon, lon_b[...], lon_a[...])
    last_lane = iota((ROWS, LANES), 1) == LANES - 1
    for at in range(2 * LEVELS):
        side_ref[at] = jnp.where(last_lane, roll(east, 127 - at, 1), roll(flux, -at, 1))
    north_ref[...] = jnp.where(odd_lat, lat_b[0:32, :], lat_a[0:32, :])

    def south(at):
        return jnp.where(odd_lat, lat_a[at : at + 1, :], lat_b[at : at + 1, :])

    def faces(at):
        return jnp.where(odd_lat, c_lat_a[32 + at : 33 + at, :], c_lat_b[32 + at : 33 + at, :])

    first_carry(south, faces, load_row, carry_ref)


def pair_loader(refs, top_ref=None):
    def load(t, k, strip):
        rows = pl.ds(strip, 8)
        if t == 0 and k == 0 and top_ref is not None:
            return [top_ref[rows, :LANES], top_ref[rows, LANES:]]
        return [refs[t][k, rows, :LANES], refs[t][k, rows, LANES:]]

    def load_row(t, k):
        if t == 0 and k == 0 and top_ref is not None:
            return top_ref[0:1, :]
        return refs[t][k, 0:1, :]

    return load, load_row


def strips(body):
    def one(i, carry):
        body(pl.multiple_of(i * 8, 8), False)
        return carry

    lax.fori_loop(0, ROWS // 8 - 1, one, 0)
    body(ROWS - 8, True)


def first_kernel(t_hbm, s_hbm, u_hbm, v_hbm, k_hbm, mask_hbm, own_ref, lon_a, lon_b, lat_a, lat_b,
                 t_out, s_out, top_out, west_out, east_out, south_out, north_out,
                 carry_ref, side_ref, north_ref,
                 t_ref, s_ref, u_ref, v_ref, k_ref, t_new, s_new, mask_ref, sems, out_sems):
    sources = (t_hbm, s_hbm, u_hbm, v_hbm, k_hbm)
    bufs = (t_ref, s_ref, u_ref, v_ref, k_ref)
    new_bufs = (t_new, s_new)
    outs = (t_out, s_out)

    def copy_in(f, index):
        rows = pl.ds(pl.multiple_of(index * 8, 8), 8)
        return pltpu.make_async_copy(sources[f].at[:, rows, :], bufs[f].at[:, rows, :], sems.at[f, index])

    def copy_out(t, index):
        rows = pl.ds(pl.multiple_of(index * 8, 8), 8)
        return pltpu.make_async_copy(new_bufs[t].at[:, rows, :], outs[t].at[:, rows, :], out_sems.at[t, index])

    def start(index, carry):
        for f in range(5):
            copy_in(f, index).start()
        return carry

    mask_copy = pltpu.make_async_copy(mask_hbm, mask_ref, sems.at[5, 0])
    start(0, 0)
    mask_copy.start()
    lax.fori_loop(1, STRIPS, start, 0)
    copy_in(0, 0).wait()
    copy_in(1, 0).wait()
    load, load_row = pair_loader((t_ref, s_ref))
    got = (lon_a, lon_b, lat_a, lat_b)
    halo_setup(is_odd("lon"), is_odd("lat"), got, got, own_ref, load_row, carry_ref, side_ref, north_ref)
    mask_copy.wait()

    def body(strip, last):
        index = STRIPS - 1 if last else strip // 8
        for f in range(2, 5):
            copy_in(f, index).wait()
        if not last:
            for f in range(2):
                copy_in(f, index + 1).wait()
        columns = Columns(8)

        def emit(k, strip, new):
            rows = pl.ds(strip, 8)
            for t in range(2):
                for h in range(2):
                    new_bufs[t][k, rows, h * LANES : (h + 1) * LANES] = new[t][h]
                    if t == 0 and k == 0:
                        top_out[rows, h * LANES : (h + 1) * LANES] = new[t][h]
                columns.add_west(LEVELS * t + k, new[t][0])
                columns.add_east(LEVELS * t + k, new[t][1])

        step_strip(strip, last, load, u_ref, v_ref, k_ref, mask_ref, side_ref, north_ref, carry_ref, emit)
        west_out[pl.ds(strip, 8), :] = columns.west
        east_out[pl.ds(strip, 8), :] = columns.east
        for t in range(2):
            copy_out(t, index).start()

    strips(body)
    south_out[...] = jnp.concatenate([ref[k, 0:1, :] for ref in new_bufs for k in range(LEVELS)], axis=0)
    north_out[...] = jnp.concatenate(
        [ref[k, ROWS - 1 : ROWS, :] for ref in new_bufs for k in range(LEVELS)], axis=0
    )

    def finish(index, carry):
        for t in range(2):
            copy_out(t, index).wait()
        return carry

    lax.fori_loop(0, STRIPS, finish, 0)


STEP_SCRATCH = [
    pltpu.VMEM((2 * LEVELS, 8, 2 * LANES), F32),
    pltpu.VMEM((2 * LEVELS, ROWS, LANES), F32),
    pltpu.VMEM((2 * LEVELS, 2 * LANES), F32),
]
STEP_COST = pl.CostEstimate(flops=7 * 10**7, bytes_accessed=25 * 2**20, transcendentals=10**6)


def first_step(fields, mask, own, got):
    shape = pltpu.HBM((LEVELS, ROWS, 2 * LANES), F32)
    buf = pltpu.VMEM((LEVELS, ROWS, 2 * LANES), F32)
    return pl.pallas_call(
        first_kernel,
        out_shape=(
            shape,
            shape,
            pltpu.VMEM((ROWS, 2 * LANES), F32),
            pltpu.VMEM((ROWS, LANES), F32),
            pltpu.VMEM((ROWS, LANES), F32),
            pltpu.VMEM((2 * LEVELS, 2 * LANES), F32),
            pltpu.VMEM((2 * LEVELS, 2 * LANES), F32),
        ),
        in_specs=[ANY] * 6 + [VM] * 5,
        out_specs=(ANY, ANY) + (VM,) * 5,
        scratch_shapes=STEP_SCRATCH
        + [buf] * 7
        + [pltpu.VMEM((ROWS, 2 * LANES), jnp.int32), pltpu.SemaphoreType.DMA((6, STRIPS)), pltpu.SemaphoreType.DMA((2, STRIPS))],
        compiler_params=pltpu.CompilerParams(vmem_limit_bytes=LIMIT),
        cost_estimate=STEP_COST,
        name="first_step",
    )(*[in_hbm(x) for x in fields], in_hbm(mask), own, *got)


def heat_kernel(top_ref, west_ref, east_ref, south_ref, north_ref, mask_hbm, t_hbm, t1_hbm, s1_hbm, back_ref, codes_ref,
                t1_out, s1_out, heat_out, top_out, lon_a_ref, lon_b_ref, lat_a_ref, lat_b_ref, own_out, mask_ref, t_ref, sems):
    mask_copy = pltpu.make_async_copy(mask_hbm, mask_ref, sems.at[0])
    mask_copy.start()
    t_copy = pltpu.make_async_copy(t_hbm.at[0], t_ref, sems.at[1])
    t_copy.start()
    moves = [
        pltpu.make_async_copy(t1_hbm, t1_out, sems.at[2]),
        pltpu.make_async_copy(s1_hbm, s1_out, sems.at[3]),
    ]
    for move in moves:
        move.start()
    air = back_ref[:, :SLOTS, :].reshape(128 * SLOTS, LANES)
    wind = back_ref[:, SLOTS:, :].reshape(128 * SLOTS, LANES)
    high, middle, low = pieces(jnp.concatenate([air, wind], axis=1))
    codes = codes_ref[...]
    lane = iota((256, 1024), 1)
    t_copy.wait()
    surface = jnp.concatenate([t_ref[:, :LANES], t_ref[:, LANES:]], axis=0)
    heat = None
    for m in range(2):
        onehot = as_bf16(codes[:, m : m + 1].astype(jnp.int32) == lane)
        found = dot(onehot, high) + (dot(onehot, middle) + dot(onehot, low))
        flux = BULK * found[:, LANES:] * (found[:, :LANES] - surface)
        part = codes[:, 2 + m : 3 + m] * flux
        heat = part if heat is None else heat + part
    mask_copy.wait()
    mask = mask_ref[...].astype(F32)
    added = []
    for h in range(2):
        cols = slice(h * LANES, (h + 1) * LANES)
        here = heat[h * ROWS : (h + 1) * ROWS]
        heat_out[:, cols] = here
        added.append(mask[:, cols] * here)
        top_out[:, cols] = top_ref[:, cols] + added[h]
    first = iota((ROWS, LANES), 1) == 0
    west = west_ref[...] + jnp.where(first, added[0], 0.0)
    east = east_ref[...] + jnp.where(first, roll(added[1], 1, 1), 0.0)
    own_out[...] = west
    odd = is_odd("lon")
    lon_a_ref[...] = jnp.where(odd, west, east)
    lon_b_ref[...] = jnp.where(odd, east, west)
    south = jnp.concatenate([top_out[0:1, :], south_ref[1:, :]], axis=0)
    north = jnp.concatenate([top_out[ROWS - 1 : ROWS, :], north_ref[1:, :]], axis=0)
    send_rows(south, north, lat_a_ref, lat_b_ref)
    for move in moves:
        move.wait()


def add_heat(t1, s1, top, west, east, south, north, mask, temp, back, codes):
    field = pltpu.VMEM((LEVELS, ROWS, 2 * LANES), F32)
    return pl.pallas_call(
        heat_kernel,
        out_shape=(
            field,
            field,
            pltpu.VMEM((ROWS, 2 * LANES), F32),
            pltpu.VMEM((ROWS, 2 * LANES), F32),
            pltpu.VMEM((ROWS, LANES), F32),
            pltpu.VMEM((ROWS, LANES), F32),
            pltpu.VMEM((32, 2 * LANES), F32),
            pltpu.VMEM((32, 2 * LANES), F32),
            pltpu.VMEM((ROWS, LANES), F32),
        ),
        in_specs=[VM] * 5 + [ANY] * 4 + [VM] * 2,
        out_specs=(VM,) * 9,
        scratch_shapes=[
            pltpu.VMEM((ROWS, 2 * LANES), jnp.int32),
            pltpu.VMEM((ROWS, 2 * LANES), F32),
            pltpu.SemaphoreType.DMA((4,)),
        ],
        compiler_params=pltpu.CompilerParams(vmem_limit_bytes=LIMIT),
        cost_estimate=pl.CostEstimate(flops=10**9, bytes_accessed=2**20, transcendentals=0),
        name="heat",
    )(*[in_vmem(x) for x in (top, west, east, south, north)], in_hbm(mask), in_hbm(temp), in_hbm(t1), in_hbm(s1), in_vmem(back), in_vmem(codes))


def second_kernel(t_ref, s_ref, u_hbm, v_hbm, k_hbm, mask_hbm, top_ref, heat_ref, own_ref,
                  lon_a, lon_b, lat_a, lat_b, c_lon_a, c_lon_b, c_lat_a, c_lat_b,
                  t_out, s_out, rho_out,
                  carry_ref, side_ref, north_ref,
                  u_ref, v_ref, k_ref, t_buf, s_buf, rho_buf, mask_ref, in_sems, sems):
    sources = (u_hbm, v_hbm, k_hbm)
    held = (u_ref, v_ref, k_ref)

    def copy_in(t, index):
        rows = pl.ds(pl.multiple_of(index * 8, 8), 8)
        return pltpu.make_async_copy(sources[t].at[:, rows, :], held[t].at[:, rows, :], in_sems.at[t, index])

    def start(index, carry):
        for f in range(3):
            copy_in(f, index).start()
        return carry

    mask_copy = pltpu.make_async_copy(mask_hbm, mask_ref, in_sems.at[3, 0])
    start(0, 0)
    mask_copy.start()
    lax.fori_loop(1, STRIPS, start, 0)
    load, load_row = pair_loader((t_ref, s_ref), top_ref)
    halo_setup(is_odd("lon"), is_odd("lat"), (lon_a, lon_b, lat_a, lat_b), (c_lon_a, c_lon_b, c_lat_a, c_lat_b),
               own_ref, load_row, carry_ref, side_ref, north_ref)
    mask_copy.wait()
    bufs = (t_buf, s_buf, rho_buf)
    outs = (t_out, s_out, rho_out)

    def emit(k, strip, new):
        for h in range(2):
            at = (k, pl.ds(strip, 8), slice(h * LANES, (h + 1) * LANES))
            for t in range(2):
                bufs[t][at] = new[t][h]
            rho_buf[at] = density_of(new[0][h], new[1][h])

    def copies(index):
        rows = pl.ds(pl.multiple_of(index * 8, 8), 8)
        return [
            pltpu.make_async_copy(bufs[n].at[:, rows, :], outs[n].at[:, rows, :], sems.at[n, index])
            for n in range(3)
        ]

    def body(strip, last):
        index = STRIPS - 1 if last else strip // 8
        for f in range(3):
            copy_in(f, index).wait()
        step_strip(strip, last, load, u_ref, v_ref, k_ref, mask_ref, side_ref, north_ref, carry_ref, emit, heat_ref)
        for copy in copies(index):
            copy.start()

    strips(body)

    def finish(index, carry):
        for copy in copies(index):
            copy.wait()
        return carry

    lax.fori_loop(0, STRIPS, finish, 0)


def second_step(t, s, fields, mask, top, heat, own, got, coefs):
    shape = jax.ShapeDtypeStruct((LEVELS, ROWS, 2 * LANES), F32)
    buf = pltpu.VMEM((LEVELS, ROWS, 2 * LANES), F32)
    return pl.pallas_call(
        second_kernel,
        out_shape=(shape, shape, shape),
        in_specs=[VM] * 2 + [ANY] * 4 + [VM] * 11,
        out_specs=(ANY, ANY, ANY),
        scratch_shapes=STEP_SCRATCH
        + [buf] * 6
        + [pltpu.VMEM((ROWS, 2 * LANES), jnp.int32), pltpu.SemaphoreType.DMA((4, STRIPS)), pltpu.SemaphoreType.DMA((3, STRIPS))],
        compiler_params=pltpu.CompilerParams(vmem_limit_bytes=LIMIT),
        cost_estimate=STEP_COST,
        name="second_step",
    )(in_vmem(t), in_vmem(s), *[in_hbm(x) for x in fields], in_hbm(mask), in_vmem(top), in_vmem(heat), in_vmem(own), *[in_vmem(g) for g in got], *coefs)


def body(
    temp,
    salt,
    east_face_velocity,
    v_face,
    kappa,
    land_mask,
    margin_owner_device,
    margin_cell,
    margin_weight,
    air_temp,
    wind_speed,
):
    def lists(x):
        return jnp.transpose(x.reshape(256, 2))

    fields = (temp, salt, east_face_velocity, v_face, kappa)
    ids, codes = make_request(
        lists(margin_owner_device), lists(margin_cell), lists(margin_weight)
    )
    ids = lax.all_to_all(ids, AXES, split_axis=0, concat_axis=0, tiled=True)
    *sent, own = make_edges(fields)
    halos = [in_vmem(g) for g in exchange(*sent)]
    answer = make_answer(
        ids, air_temp.reshape(256, LANES), wind_speed.reshape(256, LANES), halos
    )
    back = lax.all_to_all(answer, AXES, split_axis=0, concat_axis=0, tiled=True)
    t1, s1, *edges = first_step(fields, land_mask, in_vmem(own), halos)
    t1, s1, heat, top, *sent, own = add_heat(t1, s1, *edges, land_mask, temp, back, codes)
    later = exchange(*sent)
    return second_step(t1, s1, fields[2:], land_mask, top, heat, own, later, halos)


def solution(mesh):
    grid = P(None, "lat", "lon")
    lists = P("lat", "lon", None, None)
    owned = P("lon", "lat", None, None)
    in_specs = (grid,) * 5 + (P("lat", "lon"),) + (lists,) * 3 + (owned,) * 2
    return jax.shard_map(body, mesh=mesh, in_specs=in_specs, out_specs=(grid,) * 3, check_vma=False)
```

```python
import jax
import jax.numpy as jnp
from jax import lax
from jax.experimental import pallas as pl
from jax.experimental.pallas import tpu as pltpu
from jax.sharding import PartitionSpec as P

F32 = jnp.float32
BF16 = jnp.bfloat16
AXES = ("lon", "lat")
BULK = 0.1
SLOTS = 8
GROUP = SLOTS + 1
LEVELS = 16
ROWS = 128
LANES = 128
STRIPS = ROWS // 8
LIMIT = 24 * 1024 * 1024

VM = pl.BlockSpec(memory_space=pltpu.VMEM)
ANY = pl.BlockSpec(memory_space=pl.ANY)


def in_vmem(x):
    return pltpu.with_memory_space_constraint(x, pltpu.VMEM)


def dot(a, b):
    return jnp.dot(a, b, preferred_element_type=F32)


def dot_nt(a, b):
    return lax.dot_general(a, b, (((1,), (1,)), ((), ())), preferred_element_type=F32)


def pieces(x):
    high = x.astype(BF16)
    rest = x - high.astype(F32)
    middle = rest.astype(BF16)
    low = (rest - middle.astype(F32)).astype(BF16)
    return high, middle, low


def pick(onehot, x):
    high, middle, low = pieces(x)
    return dot(onehot, high) + (dot(onehot, middle) + dot(onehot, low))


def iota(shape, dim):
    return lax.broadcasted_iota(jnp.int32, shape, dim)


def roll(x, steps, axis):
    steps = steps % x.shape[axis]
    return x if steps == 0 else pltpu.roll(x, steps, axis)


def as_bf16(flag):
    return flag.astype(F32).astype(BF16)


def make_lists(owner_ref, cell_ref, weight_ref):
    w = weight_ref[...]
    share = w / (w[0:1] + w[1:2])
    before = iota((256, 256), 0)
    after = iota((256, 256), 1)
    perm = as_bf16(before == (after % ROWS) * 2 + after // ROWS)
    lists = jnp.concatenate([owner_ref[...].astype(F32), cell_ref[...].astype(F32)], axis=0)
    lists = dot(lists.astype(BF16), perm)
    share = pick_left(share, perm)
    owner = [lists[m : m + 1].astype(jnp.int32) for m in range(2)]
    cell = [lists[2 + m : 3 + m] for m in range(2)]
    return owner, cell, share


def write_request(owner, cell, share, surface, out_ref, codes_ref):
    device = iota((128, 256), 0)
    named = [as_bf16(device == owner[m]) for m in range(2)]
    earlier = as_bf16(iota((256, 256), 0) < iota((256, 256), 1))
    ones = jnp.ones((256, 256), BF16)
    ahead = [dot(named[0], earlier), dot(named[1], earlier) + dot(named[0], ones)]
    rank = [
        jnp.sum(named[m].astype(F32) * ahead[m], axis=0, keepdims=True).astype(jnp.int32)
        for m in range(2)
    ]
    slot = iota((128, 256), 0)
    ids = sum(
        dot_nt(named[m], jnp.where(slot == rank[m], cell[m], 0.0).astype(BF16)) for m in range(2)
    )
    total = 128 * GROUP
    line = iota((total, 256), 0)
    place = as_bf16(
        (line == owner[0] * GROUP + rank[0]) | (line == owner[1] * GROUP + rank[1])
    )
    id_place = as_bf16(iota((total, 128), 0) == iota((total, 128), 1) * GROUP + SLOTS)
    blocks = jnp.concatenate([surface[:, :LANES], surface[:, LANES:]], axis=0)
    out_ref[...] = pick(place, blocks) + dot(id_place, ids.astype(BF16))
    table = jnp.concatenate(
        [(owner[m] * SLOTS + rank[m]).astype(F32) for m in range(2)]
        + [share, jnp.zeros((124, 256), F32)],
        axis=0,
    )
    codes_ref[...] = jnp.transpose(table)


def request_kernel(owner_ref, cell_ref, weight_ref, surface_ref, out_ref, codes_ref):
    owner, cell, share = make_lists(owner_ref, cell_ref, weight_ref)
    write_request(owner, cell, share, surface_ref[...], out_ref, codes_ref)


def in_hbm(x):
    return pltpu.with_memory_space_constraint(x, pltpu.HBM)


def make_request(owner, cell, weight, temp):
    return pl.pallas_call(
        request_kernel,
        out_shape=(pltpu.VMEM((128 * GROUP, LANES), F32), pltpu.VMEM((256, LANES), F32)),
        grid=(1,),
        in_specs=[pl.BlockSpec((2, 256), lambda i: (0, 0))] * 3
        + [pl.BlockSpec((None, ROWS, 2 * LANES), lambda i: (0, 0, 0))],
        out_specs=(VM,) * 2,
        compiler_params=pltpu.CompilerParams(vmem_limit_bytes=LIMIT),
        cost_estimate=pl.CostEstimate(flops=5 * 10**8, bytes_accessed=2**20, transcendentals=0),
        name="request",
    )(*[in_hbm(x) for x in (owner, cell, weight, temp)])


def pick_left(x, onehot):
    high, middle, low = pieces(x)
    return dot(high, onehot) + (dot(middle, onehot) + dot(low, onehot))


def edges_kernel(t_ref, s_ref, u_ref, v_ref, k_ref, _,
                 lon_a_ref, lon_b_ref, lat_a_ref, lat_b_ref, west_ref,
                 t_buf, s_buf, u_buf, k_buf, v_row, k_row, sems, more_sems):
    last = pl.ds(ROWS - 8, 8)
    rows = [
        pltpu.make_async_copy(v_ref.at[:, last, :], v_row, more_sems.at[0]),
        pltpu.make_async_copy(k_ref.at[:, last, :], k_row, more_sems.at[1]),
    ]
    eastern = pl.ds(LANES, LANES)

    copies = [
        pltpu.make_async_copy(t_ref, t_buf, sems.at[0]),
        pltpu.make_async_copy(s_ref, s_buf, sems.at[1]),
        pltpu.make_async_copy(u_ref.at[:, :, eastern], u_buf, sems.at[2]),
        pltpu.make_async_copy(k_ref.at[:, :, eastern], k_buf, sems.at[3]),
    ]
    for copy in copies + rows:
        copy.start()
    odd = is_odd("lon")
    columns = Columns(ROWS)
    for t, ref in enumerate((t_buf, s_buf)):
        copies[t].wait()
        for k in range(LEVELS):
            columns.add_west(LEVELS * t + k, ref[k, :, :LANES])
        for k in range(LEVELS):
            columns.add_east(LEVELS * t + k, ref[k, :, LANES:])
    for f, ref in enumerate((u_buf, k_buf)):
        copies[2 + f].wait()
        for k in range(LEVELS):
            columns.add_east(64 + LEVELS * f + k, ref[k])
    west, east = columns.west, with_faces(columns)
    west_ref[...] = west
    lon_a_ref[...] = jnp.where(odd, west, east)
    lon_b_ref[...] = jnp.where(odd, east, west)
    for copy in rows:
        copy.wait()
    south = jnp.concatenate(
        [ref[k, 0:1, :] for ref in (t_buf, s_buf) for k in range(LEVELS)], axis=0
    )
    north = jnp.concatenate(
        [ref[k, ROWS - 1 : ROWS, :] for ref in (t_buf, s_buf) for k in range(LEVELS)], axis=0
    )
    faces = jnp.concatenate(
        [ref[k, 7:8, :] for ref in (v_row, k_row) for k in range(LEVELS)], axis=0
    )
    send_rows(south, north, lat_a_ref, lat_b_ref)
    lat_a_ref[32:64, :] = faces
    lat_b_ref[32:64, :] = faces


def send_rows(south, north, lat_a_ref, lat_b_ref):
    odd = is_odd("lat")
    top = lax.axis_index("lat") == lax.axis_size("lat") - 1
    lat_a_ref[0:32, :] = jnp.where(odd, south, north)
    lat_b_ref[0:32, :] = jnp.where(odd, jnp.where(top, flipped(north), north), south)


def make_edges(fields, after):
    field = pltpu.VMEM((LEVELS, ROWS, 2 * LANES), F32)
    half = pltpu.VMEM((LEVELS, ROWS, LANES), F32)
    row = pltpu.VMEM((LEVELS, 8, 2 * LANES), F32)
    return pl.pallas_call(
        edges_kernel,
        out_shape=(
            pltpu.VMEM((ROWS, LANES), F32),
            pltpu.VMEM((ROWS, LANES), F32),
            pltpu.VMEM((64, 2 * LANES), F32),
            pltpu.VMEM((64, 2 * LANES), F32),
            pltpu.VMEM((ROWS, LANES), F32),
        ),
        in_specs=[ANY] * 6,
        out_specs=(VM,) * 5,
        scratch_shapes=[
            field, field, half, half, row, row,
            pltpu.SemaphoreType.DMA((4,)),
            pltpu.SemaphoreType.DMA((2,)),
        ],
        compiler_params=pltpu.CompilerParams(vmem_limit_bytes=LIMIT),
        cost_estimate=pl.CostEstimate(flops=10**8, bytes_accessed=8 * 2**20, transcendentals=0),
        name="edges",
    )(*[in_hbm(x) for x in fields], after)


def answer_kernel(got_ref, air_ref, wind_ref, *rest):
    out_ref = rest[-1]
    ids = got_ref[pl.ds(SLOTS, 128, stride=GROUP), :].astype(BF16)
    patches = jnp.concatenate([air_ref[...], wind_ref[...]], axis=1)
    high, middle, low = pieces(patches)
    spread = jnp.ones((128, 256), BF16)
    chunk = 128
    for part in range(8):
        line = iota((chunk, 128), 0) + part * chunk
        lane = iota((chunk, 128), 1)
        rows = dot(as_bf16(line // SLOTS == lane), ids)
        rows = jnp.where(lane == line % SLOTS, rows, 0.0)
        wanted = dot(rows.astype(BF16), spread).astype(jnp.int32)
        onehot = as_bf16(wanted == iota((chunk, 256), 1))
        found = dot(onehot, high) + (dot(onehot, middle) + dot(onehot, low))
        for s in range(chunk // SLOTS):
            source = part * (chunk // SLOTS) + s
            cells = got_ref[source * GROUP : source * GROUP + SLOTS, :]
            here = found[s * SLOTS : (s + 1) * SLOTS]
            out_ref[source * SLOTS : (source + 1) * SLOTS, :] = (
                BULK * here[:, LANES:] * (here[:, :LANES] - cells)
            )


def make_answer(got, air, wind, after):
    return pl.pallas_call(
        answer_kernel,
        out_shape=pltpu.VMEM((128 * SLOTS, LANES), F32),
        in_specs=[VM] * 3 + [ANY] * len(after),
        out_specs=VM,
        compiler_params=pltpu.CompilerParams(vmem_limit_bytes=LIMIT),
        cost_estimate=pl.CostEstimate(flops=2 * 10**9, bytes_accessed=2**20, transcendentals=0),
        name="answer",
    )(in_vmem(got), air, wind, *after)


def is_odd(axis):
    return lax.rem(lax.axis_index(axis), 2) == 1


def flipped(x):
    back = as_bf16(iota((256, 256), 0) + iota((256, 256), 1) == 255)
    return pick_left(x, back)


class Columns:
    def __init__(self, rows):
        self.lane = iota((rows, LANES), 1)
        self.west = jnp.zeros((rows, LANES), F32)
        self.east = jnp.zeros((rows, LANES), F32)

    def add_west(self, at, x):
        self.west = jnp.where(self.lane == at, roll(x, at, 1), self.west)

    def add_east(self, at, x):
        self.east = jnp.where(self.lane == at, roll(x, at - 127, 1), self.east)


def with_faces(columns):
    faces = jnp.where(columns.lane >= 64, columns.east, 0.0)
    tracers_east = jnp.where(columns.lane < 64, columns.east, 0.0)
    u = jnp.where(columns.lane < 80, faces, 0.0)
    d = faces - u
    u = roll(u, -32, 1)
    d = roll(d, -16, 1)
    east = tracers_east + (u + roll(u, 16, 1)) + (d + roll(d, 16, 1))
    return east


def swap_pairs(first, count):
    route = []
    for low in range(first, count - 1, 2):
        route += [(low, low + 1), (low + 1, low)]
    return route


def exchange(lon_a, lon_b, lat_a, lat_b):
    n_lon, n_lat = lax.axis_size("lon"), lax.axis_size("lat")
    ring = swap_pairs(1, n_lon) + [(n_lon - 1, 0), (0, n_lon - 1)]
    got_lon_a = lax.ppermute(lon_a, "lon", swap_pairs(0, n_lon))
    got_lon_b = lax.ppermute(lon_b, "lon", ring)
    got_lat_a = lax.ppermute(lat_a, "lat", swap_pairs(0, n_lat))
    route = [
        (i * n_lat + low, i * n_lat + high) for i in range(n_lon) for low, high in swap_pairs(1, n_lat)
    ]
    route += [(i * n_lat + n_lat - 1, (n_lon - 1 - i) * n_lat + n_lat - 1) for i in range(n_lon)]
    got_lat_b = lax.ppermute(lat_b, AXES, route)
    return got_lon_a, got_lon_b, got_lat_a, got_lat_b


def density_of(t, s):
    return t * (-0.25 - 0.04 * t + 0.03 * s) + 0.8 * s


def twice_density(t, s):
    return t * (-0.5 - 0.08 * t + 0.06 * s) + 1.6 * s


def step_strip(strip, last, load, u_ref, v_ref, k_ref, mask_ref, side_ref, north_ref, carry_ref, emit, heat_ref=None):
    rows = pl.ds(strip, 8)
    lane = iota((8, LANES), 1)
    sub = iota((8, LANES), 0)
    first_lane, last_lane = lane == 0, lane == LANES - 1
    row0, row7 = sub == 0, sub == 7
    halves = (slice(0, LANES), slice(LANES, 2 * LANES))
    mask = [mask_ref[rows, h].astype(F32) for h in halves]
    x = [load(t, 0, strip) for t in range(2)]
    rho = [twice_density(x[0][h], x[1][h]) for h in range(2)]
    below = None
    for k in range(LEVELS):
        if k < LEVELS - 1:
            x_next = [load(t, k + 1, strip) for t in range(2)]
            rho_next = [twice_density(x_next[0][h], x_next[1][h]) for h in range(2)]
            mixing = [0.06 + 0.05 * jnp.tanh(rho[h] - rho_next[h]) for h in range(2)]
        u = [u_ref[k, rows, h] for h in halves]
        v = [v_ref[k, rows, h] for h in halves]
        d = [k_ref[k, rows, h] for h in halves]
        pe = [jnp.maximum(u[h], 0.0) + d[h] for h in range(2)]
        ne = [jnp.minimum(u[h], 0.0) - d[h] for h in range(2)]
        pn = [jnp.maximum(v[h], 0.0) + d[h] for h in range(2)]
        nn = [jnp.minimum(v[h], 0.0) - d[h] for h in range(2)]
        above = [None, None]
        new = [None, None]
        for t in range(2):
            at = LEVELS * t + k
            xt = x[t]
            side = side_ref[at, rows, :]
            y = [roll(xt[h], -1, 1) for h in range(2)]
            xe = [
                jnp.where(last_lane, y[1], y[0]),
                jnp.where(last_lane, side, y[1]),
            ]
            east = [pe[h] * xt[h] + ne[h] * xe[h] for h in range(2)]
            z = [roll(east[h], 1, 1) for h in range(2)]
            west = [
                jnp.where(first_lane, side, z[0]),
                jnp.where(first_lane, z[0], z[1]),
            ]
            if last:
                ahead = [jnp.broadcast_to(north_ref[at : at + 1, h], (8, LANES)) for h in halves]
            else:
                ahead = load(t, k, strip + 8)
            xn = [roll(jnp.where(row0, ahead[h], xt[h]), -1, 0) for h in range(2)]
            north = [pn[h] * xt[h] + nn[h] * xn[h] for h in range(2)]
            south = [
                roll(jnp.where(row7, carry_ref[at, :, halves[h]], north[h]), 1, 0) for h in range(2)
            ]
            if not last:
                for h in range(2):
                    carry_ref[at, :, halves[h]] = north[h]
            tend = [(west[h] - east[h]) + (south[h] - north[h]) for h in range(2)]
            if k < LEVELS - 1:
                above[t] = [mixing[h] * (x_next[t][h] - xt[h]) for h in range(2)]
                tend = [tend[h] + above[t][h] for h in range(2)]
            if k > 0:
                tend = [tend[h] - below[t][h] for h in range(2)]
            if heat_ref is not None and t == 0 and k == 0:
                tend = [tend[h] + heat_ref[rows, halves[h]] for h in range(2)]
            new[t] = [xt[h] + mask[h] * tend[h] for h in range(2)]
        emit(k, strip, new)
        below = above
        if k < LEVELS - 1:
            x, rho = x_next, rho_next


def west_fluxes(west, coef, own):
    u = roll(coef, -32, 1)
    d = roll(coef, -64, 1)
    return (jnp.maximum(u, 0.0) + d) * west + (jnp.minimum(u, 0.0) - d) * own


def first_carry(south, faces, load_row, carry_ref):
    for k in range(LEVELS):
        v, d = faces(k), faces(LEVELS + k)
        pn = jnp.maximum(v, 0.0) + d
        nn = jnp.minimum(v, 0.0) - d
        for t in range(2):
            at = LEVELS * t + k
            flux = pn * south(at) + nn * load_row(t, k)
            carry_ref[at] = jnp.broadcast_to(flux, (8, 2 * LANES))


def halo_setup(odd_lon, odd_lat, got, coefs, own_ref, load_row, carry_ref, side_ref, north_ref):
    lon_a, lon_b, lat_a, lat_b = got
    c_lon_a, c_lon_b, c_lat_a, c_lat_b = coefs
    west = jnp.where(odd_lon, lon_a[...], lon_b[...])
    coef = jnp.where(odd_lon, c_lon_a[...], c_lon_b[...])
    flux = west_fluxes(west, coef, own_ref[...])
    east = jnp.where(odd_lon, lon_b[...], lon_a[...])
    last_lane = iota((ROWS, LANES), 1) == LANES - 1
    for at in range(2 * LEVELS):
        side_ref[at] = jnp.where(last_lane, roll(east, 127 - at, 1), roll(flux, -at, 1))
    north_ref[...] = jnp.where(odd_lat, lat_b[0:32, :], lat_a[0:32, :])

    def south(at):
        return jnp.where(odd_lat, lat_a[at : at + 1, :], lat_b[at : at + 1, :])

    def faces(at):
        return jnp.where(odd_lat, c_lat_a[32 + at : 33 + at, :], c_lat_b[32 + at : 33 + at, :])

    first_carry(south, faces, load_row, carry_ref)


def pair_loader(refs, top_ref=None):
    def load(t, k, strip):
        rows = pl.ds(strip, 8)
        if t == 0 and k == 0 and top_ref is not None:
            return [top_ref[rows, :LANES], top_ref[rows, LANES:]]
        return [refs[t][k, rows, :LANES], refs[t][k, rows, LANES:]]

    def load_row(t, k):
        if t == 0 and k == 0 and top_ref is not None:
            return top_ref[0:1, :]
        return refs[t][k, 0:1, :]

    return load, load_row


def strips(body):
    def one(i, carry):
        body(pl.multiple_of(i * 8, 8), False)
        return carry

    lax.fori_loop(0, ROWS // 8 - 1, one, 0)
    body(ROWS - 8, True)


def first_kernel(t_hbm, s_hbm, u_hbm, v_hbm, k_hbm, mask_hbm, own_ref, lon_a, lon_b, lat_a, lat_b,
                 t_new, s_out, top_out, west_out, east_out, south_out, north_out,
                 carry_ref, side_ref, north_ref,
                 t_ref, s_ref, u_ref, v_ref, k_ref, s_new, mask_ref, sems, out_sems):
    sources = (t_hbm, s_hbm, u_hbm, v_hbm, k_hbm)
    bufs = (t_ref, s_ref, u_ref, v_ref, k_ref)
    new_bufs = (t_new, s_new)

    def copy_in(f, index):
        rows = pl.ds(pl.multiple_of(index * 8, 8), 8)
        return pltpu.make_async_copy(sources[f].at[:, rows, :], bufs[f].at[:, rows, :], sems.at[f, index])

    def copy_out(index):
        rows = pl.ds(pl.multiple_of(index * 8, 8), 8)
        return pltpu.make_async_copy(s_new.at[:, rows, :], s_out.at[:, rows, :], out_sems.at[index])

    def start(index, carry):
        for f in range(5):
            copy_in(f, index).start()
        return carry

    mask_copy = pltpu.make_async_copy(mask_hbm, mask_ref, sems.at[5, 0])
    start(0, 0)
    mask_copy.start()
    lax.fori_loop(1, STRIPS, start, 0)
    copy_in(0, 0).wait()
    copy_in(1, 0).wait()
    load, load_row = pair_loader((t_ref, s_ref))
    got = (lon_a, lon_b, lat_a, lat_b)
    halo_setup(is_odd("lon"), is_odd("lat"), got, got, own_ref, load_row, carry_ref, side_ref, north_ref)
    mask_copy.wait()

    def body(strip, last):
        index = STRIPS - 1 if last else strip // 8
        for f in range(2, 5):
            copy_in(f, index).wait()
        if not last:
            for f in range(2):
                copy_in(f, index + 1).wait()
        columns = Columns(8)

        def emit(k, strip, new):
            rows = pl.ds(strip, 8)
            for t in range(2):
                for h in range(2):
                    new_bufs[t][k, rows, h * LANES : (h + 1) * LANES] = new[t][h]
                    if t == 0 and k == 0:
                        top_out[rows, h * LANES : (h + 1) * LANES] = new[t][h]
                columns.add_west(LEVELS * t + k, new[t][0])
                columns.add_east(LEVELS * t + k, new[t][1])

        step_strip(strip, last, load, u_ref, v_ref, k_ref, mask_ref, side_ref, north_ref, carry_ref, emit)
        west_out[pl.ds(strip, 8), :] = columns.west
        east_out[pl.ds(strip, 8), :] = columns.east
        copy_out(index).start()

    strips(body)
    south_out[...] = jnp.concatenate([ref[k, 0:1, :] for ref in new_bufs for k in range(LEVELS)], axis=0)
    north_out[...] = jnp.concatenate(
        [ref[k, ROWS - 1 : ROWS, :] for ref in new_bufs for k in range(LEVELS)], axis=0
    )

    def finish(index, carry):
        copy_out(index).wait()
        return carry

    lax.fori_loop(0, STRIPS, finish, 0)


STEP_SCRATCH = [
    pltpu.VMEM((2 * LEVELS, 8, 2 * LANES), F32),
    pltpu.VMEM((2 * LEVELS, ROWS, LANES), F32),
    pltpu.VMEM((2 * LEVELS, 2 * LANES), F32),
]
STEP_COST = pl.CostEstimate(flops=7 * 10**7, bytes_accessed=25 * 2**20, transcendentals=10**6)


def first_step(fields, mask, own, got):
    shape = pltpu.HBM((LEVELS, ROWS, 2 * LANES), F32)
    buf = pltpu.VMEM((LEVELS, ROWS, 2 * LANES), F32)
    return pl.pallas_call(
        first_kernel,
        out_shape=(
            buf,
            shape,
            pltpu.VMEM((ROWS, 2 * LANES), F32),
            pltpu.VMEM((ROWS, LANES), F32),
            pltpu.VMEM((ROWS, LANES), F32),
            pltpu.VMEM((2 * LEVELS, 2 * LANES), F32),
            pltpu.VMEM((2 * LEVELS, 2 * LANES), F32),
        ),
        in_specs=[ANY] * 6 + [VM] * 5,
        out_specs=(VM, ANY) + (VM,) * 5,
        scratch_shapes=STEP_SCRATCH
        + [buf] * 6
        + [pltpu.VMEM((ROWS, 2 * LANES), jnp.int32), pltpu.SemaphoreType.DMA((6, STRIPS)), pltpu.SemaphoreType.DMA((STRIPS,))],
        compiler_params=pltpu.CompilerParams(vmem_limit_bytes=LIMIT),
        cost_estimate=STEP_COST,
        name="first_step",
    )(*[in_hbm(x) for x in fields], in_hbm(mask), own, *got)


def heat_kernel(top_ref, west_ref, east_ref, south_ref, north_ref, mask_hbm, s1_hbm, back_ref, codes_ref,
                s1_out, heat_out, top_out, lon_a_ref, lon_b_ref, lat_a_ref, lat_b_ref, own_out, mask_ref, sems):
    mask_copy = pltpu.make_async_copy(mask_hbm, mask_ref, sems.at[0])
    mask_copy.start()
    move = pltpu.make_async_copy(s1_hbm, s1_out, sems.at[1])
    move.start()
    high, middle, low = pieces(back_ref[...])
    codes = codes_ref[...]
    lane = iota((256, 1024), 1)
    heat = None
    for m in range(2):
        onehot = as_bf16(codes[:, m : m + 1].astype(jnp.int32) == lane)
        flux = dot(onehot, high) + (dot(onehot, middle) + dot(onehot, low))
        part = codes[:, 2 + m : 3 + m] * flux
        heat = part if heat is None else heat + part
    mask_copy.wait()
    mask = mask_ref[...].astype(F32)
    added = []
    for h in range(2):
        cols = slice(h * LANES, (h + 1) * LANES)
        here = heat[h * ROWS : (h + 1) * ROWS]
        heat_out[:, cols] = here
        added.append(mask[:, cols] * here)
        top_out[:, cols] = top_ref[:, cols] + added[h]
    first = iota((ROWS, LANES), 1) == 0
    west = west_ref[...] + jnp.where(first, added[0], 0.0)
    east = east_ref[...] + jnp.where(first, roll(added[1], 1, 1), 0.0)
    own_out[...] = west
    odd = is_odd("lon")
    lon_a_ref[...] = jnp.where(odd, west, east)
    lon_b_ref[...] = jnp.where(odd, east, west)
    south = jnp.concatenate([top_out[0:1, :], south_ref[1:, :]], axis=0)
    north = jnp.concatenate([top_out[ROWS - 1 : ROWS, :], north_ref[1:, :]], axis=0)
    send_rows(south, north, lat_a_ref, lat_b_ref)
    move.wait()


def add_heat(s1, top, west, east, south, north, mask, back, codes):
    field = pltpu.VMEM((LEVELS, ROWS, 2 * LANES), F32)
    return pl.pallas_call(
        heat_kernel,
        out_shape=(
            field,
            pltpu.VMEM((ROWS, 2 * LANES), F32),
            pltpu.VMEM((ROWS, 2 * LANES), F32),
            pltpu.VMEM((ROWS, LANES), F32),
            pltpu.VMEM((ROWS, LANES), F32),
            pltpu.VMEM((32, 2 * LANES), F32),
            pltpu.VMEM((32, 2 * LANES), F32),
            pltpu.VMEM((ROWS, LANES), F32),
        ),
        in_specs=[VM] * 5 + [ANY] * 2 + [VM] * 2,
        out_specs=(VM,) * 8,
        scratch_shapes=[
            pltpu.VMEM((ROWS, 2 * LANES), jnp.int32),
            pltpu.SemaphoreType.DMA((2,)),
        ],
        compiler_params=pltpu.CompilerParams(vmem_limit_bytes=LIMIT),
        cost_estimate=pl.CostEstimate(flops=10**9, bytes_accessed=2**20, transcendentals=0),
        name="heat",
    )(*[in_vmem(x) for x in (top, west, east, south, north)], in_hbm(mask), in_hbm(s1), in_vmem(back), in_vmem(codes))


def second_kernel(t_ref, s_ref, u_hbm, v_hbm, k_hbm, mask_hbm, top_ref, heat_ref, own_ref,
                  lon_a, lon_b, lat_a, lat_b, c_lon_a, c_lon_b, c_lat_a, c_lat_b,
                  t_out, s_out, rho_out,
                  carry_ref, side_ref, north_ref,
                  u_ref, v_ref, k_ref, t_buf, s_buf, rho_buf, mask_ref, in_sems, sems):
    sources = (u_hbm, v_hbm, k_hbm)
    held = (u_ref, v_ref, k_ref)

    def copy_in(t, index):
        rows = pl.ds(pl.multiple_of(index * 8, 8), 8)
        return pltpu.make_async_copy(sources[t].at[:, rows, :], held[t].at[:, rows, :], in_sems.at[t, index])

    def start(index, carry):
        for f in range(3):
            copy_in(f, index).start()
        return carry

    mask_copy = pltpu.make_async_copy(mask_hbm, mask_ref, in_sems.at[3, 0])
    start(0, 0)
    mask_copy.start()
    lax.fori_loop(1, STRIPS, start, 0)
    load, load_row = pair_loader((t_ref, s_ref), top_ref)
    halo_setup(is_odd("lon"), is_odd("lat"), (lon_a, lon_b, lat_a, lat_b), (c_lon_a, c_lon_b, c_lat_a, c_lat_b),
               own_ref, load_row, carry_ref, side_ref, north_ref)
    mask_copy.wait()
    bufs = (t_buf, s_buf, rho_buf)
    outs = (t_out, s_out, rho_out)

    def emit(k, strip, new):
        for h in range(2):
            at = (k, pl.ds(strip, 8), slice(h * LANES, (h + 1) * LANES))
            for t in range(2):
                bufs[t][at] = new[t][h]
            rho_buf[at] = density_of(new[0][h], new[1][h])

    def copies(index):
        rows = pl.ds(pl.multiple_of(index * 16, 16), 16)
        return [
            pltpu.make_async_copy(bufs[n].at[:, rows, :], outs[n].at[:, rows, :], sems.at[n, index])
            for n in range(3)
        ]

    def body(strip, last):
        index = STRIPS - 1 if last else strip // 8
        for f in range(3):
            copy_in(f, index).wait()
        step_strip(strip, last, load, u_ref, v_ref, k_ref, mask_ref, side_ref, north_ref, carry_ref, emit, heat_ref)

        def send():
            for copy in copies(index // 2):
                copy.start()

        if last:
            send()
        else:
            pl.when(lax.rem(index, 2) == 1)(send)

    strips(body)

    def finish(index, carry):
        for copy in copies(index):
            copy.wait()
        return carry

    lax.fori_loop(0, STRIPS // 2, finish, 0)


def second_step(t, s, fields, mask, top, heat, own, got, coefs):
    shape = jax.ShapeDtypeStruct((LEVELS, ROWS, 2 * LANES), F32)
    buf = pltpu.VMEM((LEVELS, ROWS, 2 * LANES), F32)
    return pl.pallas_call(
        second_kernel,
        out_shape=(shape, shape, shape),
        in_specs=[VM] * 2 + [ANY] * 4 + [VM] * 11,
        out_specs=(ANY, ANY, ANY),
        scratch_shapes=STEP_SCRATCH
        + [buf] * 6
        + [pltpu.VMEM((ROWS, 2 * LANES), jnp.int32), pltpu.SemaphoreType.DMA((4, STRIPS)), pltpu.SemaphoreType.DMA((3, STRIPS // 2))],
        compiler_params=pltpu.CompilerParams(vmem_limit_bytes=LIMIT),
        cost_estimate=STEP_COST,
        name="second_step",
    )(in_vmem(t), in_vmem(s), *[in_hbm(x) for x in fields], in_hbm(mask), in_vmem(top), in_vmem(heat), in_vmem(own), *[in_vmem(g) for g in got], *coefs)


def body(
    temp,
    salt,
    east_face_velocity,
    v_face,
    kappa,
    land_mask,
    margin_owner_device,
    margin_cell,
    margin_weight,
    air_temp,
    wind_speed,
):
    def lists(x):
        return jnp.transpose(x.reshape(256, 2))

    fields = (temp, salt, east_face_velocity, v_face, kappa)
    request, codes = make_request(
        lists(margin_owner_device), lists(margin_cell), lists(margin_weight), temp
    )
    request = request.reshape(128, 1, GROUP * LANES)
    got = lax.all_to_all(request, AXES, split_axis=0, concat_axis=0, tiled=True)
    got = got.reshape(128 * GROUP, LANES)
    *sent, own = make_edges(fields, codes)
    halos = [in_vmem(g) for g in exchange(*sent)]
    answer = make_answer(
        got, air_temp.reshape(256, LANES), wind_speed.reshape(256, LANES), halos
    )
    back = lax.all_to_all(answer, AXES, split_axis=0, concat_axis=0, tiled=True)
    t1, s1, *edges = first_step(fields, land_mask, in_vmem(own), halos)
    s1, heat, top, *sent, own = add_heat(s1, *edges, land_mask, back, codes)
    later = exchange(*sent)
    return second_step(t1, s1, fields[2:], land_mask, top, heat, own, later, halos)


def solution(mesh):
    grid = P(None, "lat", "lon")
    lists = P("lat", "lon", None, None)
    owned = P("lon", "lat", None, None)
    in_specs = (grid,) * 5 + (P("lat", "lon"),) + (lists,) * 3 + (owned,) * 2
    return jax.shard_map(body, mesh=mesh, in_specs=in_specs, out_specs=(grid,) * 3, check_vma=False)
```

```python
import jax
import jax.numpy as jnp
from jax import lax
from jax.experimental import pallas as pl
from jax.experimental.pallas import tpu as pltpu
from jax.sharding import PartitionSpec as P

F32 = jnp.float32
BF16 = jnp.bfloat16
AXES = ("lon", "lat")
BULK = 0.1
SLOTS = 8
GROUP = SLOTS + 1
LEVELS = 16
ROWS = 128
LANES = 128
STRIPS = ROWS // 8
LIMIT = 24 * 1024 * 1024

VM = pl.BlockSpec(memory_space=pltpu.VMEM)
ANY = pl.BlockSpec(memory_space=pl.ANY)


def in_vmem(x):
    return pltpu.with_memory_space_constraint(x, pltpu.VMEM)


def dot(a, b):
    return jnp.dot(a, b, preferred_element_type=F32)


def dot_nt(a, b):
    return lax.dot_general(a, b, (((1,), (1,)), ((), ())), preferred_element_type=F32)


def pieces(x):
    high = x.astype(BF16)
    rest = x - high.astype(F32)
    middle = rest.astype(BF16)
    low = (rest - middle.astype(F32)).astype(BF16)
    return high, middle, low


def pick(onehot, x):
    high, middle, low = pieces(x)
    return dot(onehot, high) + (dot(onehot, middle) + dot(onehot, low))


def iota(shape, dim):
    return lax.broadcasted_iota(jnp.int32, shape, dim)


def roll(x, steps, axis):
    steps = steps % x.shape[axis]
    return x if steps == 0 else pltpu.roll(x, steps, axis)


def as_bf16(flag):
    return flag.astype(F32).astype(BF16)


def make_lists(owner_ref, cell_ref, weight_ref):
    w = weight_ref[...]
    share = w / (w[0:1] + w[1:2])
    before = iota((256, 256), 0)
    after = iota((256, 256), 1)
    perm = as_bf16(before == (after % ROWS) * 2 + after // ROWS)
    lists = jnp.concatenate([owner_ref[...].astype(F32), cell_ref[...].astype(F32)], axis=0)
    lists = dot(lists.astype(BF16), perm)
    share = pick_left(share, perm)
    owner = [lists[m : m + 1].astype(jnp.int32) for m in range(2)]
    cell = [lists[2 + m : 3 + m] for m in range(2)]
    return owner, cell, share


def write_request(owner, cell, share, surface, out_ref, codes_ref):
    device = iota((128, 256), 0)
    named = [as_bf16(device == owner[m]) for m in range(2)]
    earlier = as_bf16(iota((256, 256), 0) < iota((256, 256), 1))
    ones = jnp.ones((256, 256), BF16)
    ahead = [dot(named[0], earlier), dot(named[1], earlier) + dot(named[0], ones)]
    rank = [
        jnp.sum(named[m].astype(F32) * ahead[m], axis=0, keepdims=True).astype(jnp.int32)
        for m in range(2)
    ]
    slot = iota((128, 256), 0)
    ids = sum(
        dot_nt(named[m], jnp.where(slot == rank[m], cell[m], 0.0).astype(BF16)) for m in range(2)
    )
    total = 128 * GROUP
    line = iota((total, 256), 0)
    place = as_bf16(
        (line == owner[0] * GROUP + rank[0]) | (line == owner[1] * GROUP + rank[1])
    )
    id_place = as_bf16(iota((total, 128), 0) == iota((total, 128), 1) * GROUP + SLOTS)
    blocks = jnp.concatenate([surface[:, :LANES], surface[:, LANES:]], axis=0)
    out_ref[...] = pick(place, blocks) + dot(id_place, ids.astype(BF16))
    table = jnp.concatenate(
        [(owner[m] * SLOTS + rank[m]).astype(F32) for m in range(2)]
        + [share, jnp.zeros((124, 256), F32)],
        axis=0,
    )
    codes_ref[...] = jnp.transpose(table)


def request_kernel(owner_ref, cell_ref, weight_ref, surface_ref, out_ref, codes_ref):
    owner, cell, share = make_lists(owner_ref, cell_ref, weight_ref)
    write_request(owner, cell, share, surface_ref[...], out_ref, codes_ref)


def in_hbm(x):
    return pltpu.with_memory_space_constraint(x, pltpu.HBM)


def make_request(owner, cell, weight, temp):
    return pl.pallas_call(
        request_kernel,
        out_shape=(pltpu.VMEM((128 * GROUP, LANES), F32), pltpu.VMEM((256, LANES), F32)),
        grid=(1,),
        in_specs=[pl.BlockSpec((2, 256), lambda i: (0, 0))] * 3
        + [pl.BlockSpec((None, ROWS, 2 * LANES), lambda i: (0, 0, 0))],
        out_specs=(VM,) * 2,
        compiler_params=pltpu.CompilerParams(vmem_limit_bytes=LIMIT),
        cost_estimate=pl.CostEstimate(flops=5 * 10**8, bytes_accessed=2**20, transcendentals=0),
        name="request",
    )(*[in_hbm(x) for x in (owner, cell, weight, temp)])


def pick_left(x, onehot):
    high, middle, low = pieces(x)
    return dot(high, onehot) + (dot(middle, onehot) + dot(low, onehot))


def edges_kernel(t_ref, s_ref, u_ref, v_ref, k_ref, _,
                 lon_a_ref, lon_b_ref, lat_a_ref, lat_b_ref, west_ref,
                 t_buf, s_buf, u_buf, k_buf, v_row, k_row, sems, more_sems):
    last = pl.ds(ROWS - 8, 8)
    rows = [
        pltpu.make_async_copy(v_ref.at[:, last, :], v_row, more_sems.at[0]),
        pltpu.make_async_copy(k_ref.at[:, last, :], k_row, more_sems.at[1]),
    ]
    eastern = pl.ds(LANES, LANES)

    copies = [
        pltpu.make_async_copy(t_ref, t_buf, sems.at[0]),
        pltpu.make_async_copy(s_ref, s_buf, sems.at[1]),
        pltpu.make_async_copy(u_ref.at[:, :, eastern], u_buf, sems.at[2]),
        pltpu.make_async_copy(k_ref.at[:, :, eastern], k_buf, sems.at[3]),
    ]
    for copy in copies + rows:
        copy.start()
    odd = is_odd("lon")
    columns = Columns(ROWS)
    for t, ref in enumerate((t_buf, s_buf)):
        copies[t].wait()
        for k in range(LEVELS):
            columns.add_west(LEVELS * t + k, ref[k, :, :LANES])
        for k in range(LEVELS):
            columns.add_east(LEVELS * t + k, ref[k, :, LANES:])
    for f, ref in enumerate((u_buf, k_buf)):
        copies[2 + f].wait()
        for k in range(LEVELS):
            columns.add_east(64 + LEVELS * f + k, ref[k])
    west, east = columns.west, with_faces(columns)
    west_ref[...] = west
    lon_a_ref[...] = jnp.where(odd, west, east)
    lon_b_ref[...] = jnp.where(odd, east, west)
    for copy in rows:
        copy.wait()
    south = jnp.concatenate(
        [ref[k, 0:1, :] for ref in (t_buf, s_buf) for k in range(LEVELS)], axis=0
    )
    north = jnp.concatenate(
        [ref[k, ROWS - 1 : ROWS, :] for ref in (t_buf, s_buf) for k in range(LEVELS)], axis=0
    )
    faces = jnp.concatenate(
        [ref[k, 7:8, :] for ref in (v_row, k_row) for k in range(LEVELS)], axis=0
    )
    send_rows(south, north, lat_a_ref, lat_b_ref)
    lat_a_ref[32:64, :] = faces
    lat_b_ref[32:64, :] = faces


def send_rows(south, north, lat_a_ref, lat_b_ref):
    odd = is_odd("lat")
    top = lax.axis_index("lat") == lax.axis_size("lat") - 1
    lat_a_ref[0:32, :] = jnp.where(odd, south, north)
    lat_b_ref[0:32, :] = jnp.where(odd, jnp.where(top, flipped(north), north), south)


def make_edges(fields, after):
    field = pltpu.VMEM((LEVELS, ROWS, 2 * LANES), F32)
    half = pltpu.VMEM((LEVELS, ROWS, LANES), F32)
    row = pltpu.VMEM((LEVELS, 8, 2 * LANES), F32)
    return pl.pallas_call(
        edges_kernel,
        out_shape=(
            pltpu.VMEM((ROWS, LANES), F32),
            pltpu.VMEM((ROWS, LANES), F32),
            pltpu.VMEM((64, 2 * LANES), F32),
            pltpu.VMEM((64, 2 * LANES), F32),
            pltpu.VMEM((ROWS, LANES), F32),
        ),
        in_specs=[ANY] * 6,
        out_specs=(VM,) * 5,
        scratch_shapes=[
            field, field, half, half, row, row,
            pltpu.SemaphoreType.DMA((4,)),
            pltpu.SemaphoreType.DMA((2,)),
        ],
        compiler_params=pltpu.CompilerParams(vmem_limit_bytes=LIMIT),
        cost_estimate=pl.CostEstimate(flops=10**8, bytes_accessed=8 * 2**20, transcendentals=0),
        name="edges",
    )(*[in_hbm(x) for x in fields], after)


def answer_kernel(got_ref, air_ref, wind_ref, *rest):
    out_ref = rest[-1]
    ids = got_ref[pl.ds(SLOTS, 128, stride=GROUP), :].astype(BF16)
    patches = jnp.concatenate([air_ref[...], wind_ref[...]], axis=1)
    high, middle, low = pieces(patches)
    spread = jnp.ones((128, 256), BF16)
    chunk = 512
    for part in range(2):
        line = iota((chunk, 128), 0) + part * chunk
        lane = iota((chunk, 128), 1)
        rows = dot(as_bf16(line // SLOTS == lane), ids)
        rows = jnp.where(lane == line % SLOTS, rows, 0.0)
        wanted = dot(rows.astype(BF16), spread).astype(jnp.int32)
        onehot = as_bf16(wanted == iota((chunk, 256), 1))
        found = dot(onehot, high) + (dot(onehot, middle) + dot(onehot, low))
        for s in range(chunk // SLOTS):
            source = part * (chunk // SLOTS) + s
            cells = got_ref[source * GROUP : source * GROUP + SLOTS, :]
            here = found[s * SLOTS : (s + 1) * SLOTS]
            out_ref[source * SLOTS : (source + 1) * SLOTS, :] = (
                BULK * here[:, LANES:] * (here[:, :LANES] - cells)
            )


def make_answer(got, air, wind, after):
    return pl.pallas_call(
        answer_kernel,
        out_shape=pltpu.VMEM((128 * SLOTS, LANES), F32),
        in_specs=[VM] * 3 + [ANY] * len(after),
        out_specs=VM,
        compiler_params=pltpu.CompilerParams(vmem_limit_bytes=LIMIT),
        cost_estimate=pl.CostEstimate(flops=2 * 10**9, bytes_accessed=2**20, transcendentals=0),
        name="answer",
    )(in_vmem(got), air, wind, *after)


def is_odd(axis):
    return lax.rem(lax.axis_index(axis), 2) == 1


def flipped(x):
    back = as_bf16(iota((256, 256), 0) + iota((256, 256), 1) == 255)
    return pick_left(x, back)


class Columns:
    def __init__(self, rows):
        self.lane = iota((rows, LANES), 1)
        self.west = jnp.zeros((rows, LANES), F32)
        self.east = jnp.zeros((rows, LANES), F32)

    def add_west(self, at, x):
        self.west = jnp.where(self.lane == at, roll(x, at, 1), self.west)

    def add_east(self, at, x):
        self.east = jnp.where(self.lane == at, roll(x, at - 127, 1), self.east)


def with_faces(columns):
    faces = jnp.where(columns.lane >= 64, columns.east, 0.0)
    tracers_east = jnp.where(columns.lane < 64, columns.east, 0.0)
    u = jnp.where(columns.lane < 80, faces, 0.0)
    d = faces - u
    u = roll(u, -32, 1)
    d = roll(d, -16, 1)
    east = tracers_east + (u + roll(u, 16, 1)) + (d + roll(d, 16, 1))
    return east


def swap_pairs(first, count):
    route = []
    for low in range(first, count - 1, 2):
        route += [(low, low + 1), (low + 1, low)]
    return route


def exchange(lon_a, lon_b, lat_a, lat_b):
    n_lon, n_lat = lax.axis_size("lon"), lax.axis_size("lat")
    ring = swap_pairs(1, n_lon) + [(n_lon - 1, 0), (0, n_lon - 1)]
    got_lon_a = lax.ppermute(lon_a, "lon", swap_pairs(0, n_lon))
    got_lon_b = lax.ppermute(lon_b, "lon", ring)
    got_lat_a = lax.ppermute(lat_a, "lat", swap_pairs(0, n_lat))
    route = [
        (i * n_lat + low, i * n_lat + high) for i in range(n_lon) for low, high in swap_pairs(1, n_lat)
    ]
    route += [(i * n_lat + n_lat - 1, (n_lon - 1 - i) * n_lat + n_lat - 1) for i in range(n_lon)]
    got_lat_b = lax.ppermute(lat_b, AXES, route)
    return got_lon_a, got_lon_b, got_lat_a, got_lat_b


def density_of(t, s):
    return t * (-0.25 - 0.04 * t + 0.03 * s) + 0.8 * s


def twice_density(t, s):
    return t * (-0.5 - 0.08 * t + 0.06 * s) + 1.6 * s


def step_strip(strip, last, load, u_ref, v_ref, k_ref, mask_ref, side_ref, north_ref, carry_ref, emit, heat_ref=None):
    rows = pl.ds(strip, 8)
    lane = iota((8, LANES), 1)
    sub = iota((8, LANES), 0)
    first_lane, last_lane = lane == 0, lane == LANES - 1
    row0, row7 = sub == 0, sub == 7
    halves = (slice(0, LANES), slice(LANES, 2 * LANES))
    mask = [mask_ref[rows, h].astype(F32) for h in halves]
    x = [load(t, 0, strip) for t in range(2)]
    rho = [twice_density(x[0][h], x[1][h]) for h in range(2)]
    below = None
    for k in range(LEVELS):
        if k < LEVELS - 1:
            x_next = [load(t, k + 1, strip) for t in range(2)]
            rho_next = [twice_density(x_next[0][h], x_next[1][h]) for h in range(2)]
            mixing = [0.06 + 0.05 * jnp.tanh(rho[h] - rho_next[h]) for h in range(2)]
        u = [u_ref[k, rows, h] for h in halves]
        v = [v_ref[k, rows, h] for h in halves]
        d = [k_ref[k, rows, h] for h in halves]
        pe = [jnp.maximum(u[h], 0.0) + d[h] for h in range(2)]
        ne = [jnp.minimum(u[h], 0.0) - d[h] for h in range(2)]
        pn = [jnp.maximum(v[h], 0.0) + d[h] for h in range(2)]
        nn = [jnp.minimum(v[h], 0.0) - d[h] for h in range(2)]
        above = [None, None]
        new = [None, None]
        for t in range(2):
            at = LEVELS * t + k
            xt = x[t]
            side = side_ref[at, rows, :]
            y = [roll(xt[h], -1, 1) for h in range(2)]
            xe = [
                jnp.where(last_lane, y[1], y[0]),
                jnp.where(last_lane, side, y[1]),
            ]
            east = [pe[h] * xt[h] + ne[h] * xe[h] for h in range(2)]
            z = [roll(east[h], 1, 1) for h in range(2)]
            west = [
                jnp.where(first_lane, side, z[0]),
                jnp.where(first_lane, z[0], z[1]),
            ]
            if last:
                ahead = [jnp.broadcast_to(north_ref[at : at + 1, h], (8, LANES)) for h in halves]
            else:
                ahead = load(t, k, strip + 8)
            xn = [roll(jnp.where(row0, ahead[h], xt[h]), -1, 0) for h in range(2)]
            north = [pn[h] * xt[h] + nn[h] * xn[h] for h in range(2)]
            south = [
                roll(jnp.where(row7, carry_ref[at, :, halves[h]], north[h]), 1, 0) for h in range(2)
            ]
            if not last:
                for h in range(2):
                    carry_ref[at, :, halves[h]] = north[h]
            tend = [(west[h] - east[h]) + (south[h] - north[h]) for h in range(2)]
            if k < LEVELS - 1:
                above[t] = [mixing[h] * (x_next[t][h] - xt[h]) for h in range(2)]
                tend = [tend[h] + above[t][h] for h in range(2)]
            if k > 0:
                tend = [tend[h] - below[t][h] for h in range(2)]
            if heat_ref is not None and t == 0 and k == 0:
                tend = [tend[h] + heat_ref[rows, halves[h]] for h in range(2)]
            new[t] = [xt[h] + mask[h] * tend[h] for h in range(2)]
        emit(k, strip, new)
        below = above
        if k < LEVELS - 1:
            x, rho = x_next, rho_next


def west_fluxes(west, coef, own):
    u = roll(coef, -32, 1)
    d = roll(coef, -64, 1)
    return (jnp.maximum(u, 0.0) + d) * west + (jnp.minimum(u, 0.0) - d) * own


def first_carry(south, faces, load_row, carry_ref):
    for k in range(LEVELS):
        v, d = faces(k), faces(LEVELS + k)
        pn = jnp.maximum(v, 0.0) + d
        nn = jnp.minimum(v, 0.0) - d
        for t in range(2):
            at = LEVELS * t + k
            flux = pn * south(at) + nn * load_row(t, k)
            carry_ref[at] = jnp.broadcast_to(flux, (8, 2 * LANES))


def halo_setup(odd_lon, odd_lat, got, coefs, own_ref, load_row, carry_ref, side_ref, north_ref):
    lon_a, lon_b, lat_a, lat_b = got
    c_lon_a, c_lon_b, c_lat_a, c_lat_b = coefs
    west = jnp.where(odd_lon, lon_a[...], lon_b[...])
    coef = jnp.where(odd_lon, c_lon_a[...], c_lon_b[...])
    flux = west_fluxes(west, coef, own_ref[...])
    east = jnp.where(odd_lon, lon_b[...], lon_a[...])
    last_lane = iota((ROWS, LANES), 1) == LANES - 1
    for at in range(2 * LEVELS):
        side_ref[at] = jnp.where(last_lane, roll(east, 127 - at, 1), roll(flux, -at, 1))
    north_ref[...] = jnp.where(odd_lat, lat_b[0:32, :], lat_a[0:32, :])

    def south(at):
        return jnp.where(odd_lat, lat_a[at : at + 1, :], lat_b[at : at + 1, :])

    def faces(at):
        return jnp.where(odd_lat, c_lat_a[32 + at : 33 + at, :], c_lat_b[32 + at : 33 + at, :])

    first_carry(south, faces, load_row, carry_ref)


def pair_loader(refs, top_ref=None):
    def load(t, k, strip):
        rows = pl.ds(strip, 8)
        if t == 0 and k == 0 and top_ref is not None:
            return [top_ref[rows, :LANES], top_ref[rows, LANES:]]
        return [refs[t][k, rows, :LANES], refs[t][k, rows, LANES:]]

    def load_row(t, k):
        if t == 0 and k == 0 and top_ref is not None:
            return top_ref[0:1, :]
        return refs[t][k, 0:1, :]

    return load, load_row


def strips(body):
    def one(i, carry):
        body(pl.multiple_of(i * 8, 8), False)
        return carry

    lax.fori_loop(0, ROWS // 8 - 1, one, 0)
    body(ROWS - 8, True)


def first_kernel(t_hbm, s_hbm, u_hbm, v_hbm, k_hbm, mask_hbm, own_ref, lon_a, lon_b, lat_a, lat_b,
                 t_new, s_out, top_out, west_out, east_out, south_out, north_out,
                 carry_ref, side_ref, north_ref,
                 t_ref, s_ref, u_ref, v_ref, k_ref, s_new, mask_ref, sems, out_sems):
    sources = (t_hbm, s_hbm, u_hbm, v_hbm, k_hbm)
    bufs = (t_ref, s_ref, u_ref, v_ref, k_ref)
    new_bufs = (t_new, s_new)

    def copy_in(f, index):
        rows = pl.ds(pl.multiple_of(index * 8, 8), 8)
        return pltpu.make_async_copy(sources[f].at[:, rows, :], bufs[f].at[:, rows, :], sems.at[f, index])

    def copy_out(index):
        rows = pl.ds(pl.multiple_of(index * 8, 8), 8)
        return pltpu.make_async_copy(s_new.at[:, rows, :], s_out.at[:, rows, :], out_sems.at[index])

    def start(index, carry):
        for f in range(5):
            copy_in(f, index).start()
        return carry

    mask_copy = pltpu.make_async_copy(mask_hbm, mask_ref, sems.at[5, 0])
    start(0, 0)
    mask_copy.start()
    lax.fori_loop(1, STRIPS, start, 0)
    copy_in(0, 0).wait()
    copy_in(1, 0).wait()
    load, load_row = pair_loader((t_ref, s_ref))
    got = (lon_a, lon_b, lat_a, lat_b)
    halo_setup(is_odd("lon"), is_odd("lat"), got, got, own_ref, load_row, carry_ref, side_ref, north_ref)
    mask_copy.wait()

    def body(strip, last):
        index = STRIPS - 1 if last else strip // 8
        for f in range(2, 5):
            copy_in(f, index).wait()
        if not last:
            for f in range(2):
                copy_in(f, index + 1).wait()
        columns = Columns(8)

        def emit(k, strip, new):
            rows = pl.ds(strip, 8)
            for t in range(2):
                for h in range(2):
                    new_bufs[t][k, rows, h * LANES : (h + 1) * LANES] = new[t][h]
                    if t == 0 and k == 0:
                        top_out[rows, h * LANES : (h + 1) * LANES] = new[t][h]
                columns.add_west(LEVELS * t + k, new[t][0])
                columns.add_east(LEVELS * t + k, new[t][1])

        step_strip(strip, last, load, u_ref, v_ref, k_ref, mask_ref, side_ref, north_ref, carry_ref, emit)
        west_out[pl.ds(strip, 8), :] = columns.west
        east_out[pl.ds(strip, 8), :] = columns.east
        copy_out(index).start()

    strips(body)
    south_out[...] = jnp.concatenate([ref[k, 0:1, :] for ref in new_bufs for k in range(LEVELS)], axis=0)
    north_out[...] = jnp.concatenate(
        [ref[k, ROWS - 1 : ROWS, :] for ref in new_bufs for k in range(LEVELS)], axis=0
    )

    def finish(index, carry):
        copy_out(index).wait()
        return carry

    lax.fori_loop(0, STRIPS, finish, 0)


STEP_SCRATCH = [
    pltpu.VMEM((2 * LEVELS, 8, 2 * LANES), F32),
    pltpu.VMEM((2 * LEVELS, ROWS, LANES), F32),
    pltpu.VMEM((2 * LEVELS, 2 * LANES), F32),
]
STEP_COST = pl.CostEstimate(flops=7 * 10**7, bytes_accessed=25 * 2**20, transcendentals=10**6)


def first_step(fields, mask, own, got):
    shape = pltpu.HBM((LEVELS, ROWS, 2 * LANES), F32)
    buf = pltpu.VMEM((LEVELS, ROWS, 2 * LANES), F32)
    return pl.pallas_call(
        first_kernel,
        out_shape=(
            buf,
            shape,
            pltpu.VMEM((ROWS, 2 * LANES), F32),
            pltpu.VMEM((ROWS, LANES), F32),
            pltpu.VMEM((ROWS, LANES), F32),
            pltpu.VMEM((2 * LEVELS, 2 * LANES), F32),
            pltpu.VMEM((2 * LEVELS, 2 * LANES), F32),
        ),
        in_specs=[ANY] * 6 + [VM] * 5,
        out_specs=(VM, ANY) + (VM,) * 5,
        scratch_shapes=STEP_SCRATCH
        + [buf] * 6
        + [pltpu.VMEM((ROWS, 2 * LANES), jnp.int32), pltpu.SemaphoreType.DMA((6, STRIPS)), pltpu.SemaphoreType.DMA((STRIPS,))],
        compiler_params=pltpu.CompilerParams(vmem_limit_bytes=LIMIT),
        cost_estimate=STEP_COST,
        name="first_step",
    )(*[in_hbm(x) for x in fields], in_hbm(mask), own, *got)


def heat_kernel(top_ref, west_ref, east_ref, south_ref, north_ref, mask_hbm, s1_hbm, back_ref, codes_ref,
                s1_out, heat_out, top_out, lon_a_ref, lon_b_ref, lat_a_ref, lat_b_ref, own_out, mask_ref, sems):
    mask_copy = pltpu.make_async_copy(mask_hbm, mask_ref, sems.at[0])
    mask_copy.start()
    move = pltpu.make_async_copy(s1_hbm, s1_out, sems.at[1])
    move.start()
    high, middle, low = pieces(back_ref[...])
    codes = codes_ref[...]
    lane = iota((256, 1024), 1)
    onehot = jnp.concatenate(
        [as_bf16(codes[:, m : m + 1].astype(jnp.int32) == lane) for m in range(2)], axis=0
    )
    upper = dot(onehot, jnp.concatenate([high, middle], axis=1))
    flux = upper[:, :LANES] + (upper[:, LANES:] + dot(onehot, low))
    heat = codes[:, 2:3] * flux[:256] + codes[:, 3:4] * flux[256:]
    mask_copy.wait()
    mask = mask_ref[...].astype(F32)
    added = []
    for h in range(2):
        cols = slice(h * LANES, (h + 1) * LANES)
        here = heat[h * ROWS : (h + 1) * ROWS]
        heat_out[:, cols] = here
        added.append(mask[:, cols] * here)
        top_out[:, cols] = top_ref[:, cols] + added[h]
    first = iota((ROWS, LANES), 1) == 0
    west = west_ref[...] + jnp.where(first, added[0], 0.0)
    east = east_ref[...] + jnp.where(first, roll(added[1], 1, 1), 0.0)
    own_out[...] = west
    odd = is_odd("lon")
    lon_a_ref[...] = jnp.where(odd, west, east)
    lon_b_ref[...] = jnp.where(odd, east, west)
    south = jnp.concatenate([top_out[0:1, :], south_ref[1:, :]], axis=0)
    north = jnp.concatenate([top_out[ROWS - 1 : ROWS, :], north_ref[1:, :]], axis=0)
    send_rows(south, north, lat_a_ref, lat_b_ref)
    move.wait()


def add_heat(s1, top, west, east, south, north, mask, back, codes):
    field = pltpu.VMEM((LEVELS, ROWS, 2 * LANES), F32)
    return pl.pallas_call(
        heat_kernel,
        out_shape=(
            field,
            pltpu.VMEM((ROWS, 2 * LANES), F32),
            pltpu.VMEM((ROWS, 2 * LANES), F32),
            pltpu.VMEM((ROWS, LANES), F32),
            pltpu.VMEM((ROWS, LANES), F32),
            pltpu.VMEM((32, 2 * LANES), F32),
            pltpu.VMEM((32, 2 * LANES), F32),
            pltpu.VMEM((ROWS, LANES), F32),
        ),
        in_specs=[VM] * 5 + [ANY] * 2 + [VM] * 2,
        out_specs=(VM,) * 8,
        scratch_shapes=[
            pltpu.VMEM((ROWS, 2 * LANES), jnp.int32),
            pltpu.SemaphoreType.DMA((2,)),
        ],
        compiler_params=pltpu.CompilerParams(vmem_limit_bytes=LIMIT),
        cost_estimate=pl.CostEstimate(flops=10**9, bytes_accessed=2**20, transcendentals=0),
        name="heat",
    )(*[in_vmem(x) for x in (top, west, east, south, north)], in_hbm(mask), in_hbm(s1), in_vmem(back), in_vmem(codes))


def second_kernel(t_ref, s_ref, u_hbm, v_hbm, k_hbm, mask_hbm, top_ref, heat_ref, own_ref,
                  lon_a, lon_b, lat_a, lat_b, c_lon_a, c_lon_b, c_lat_a, c_lat_b,
                  t_out, s_out, rho_out,
                  carry_ref, side_ref, north_ref,
                  u_ref, v_ref, k_ref, t_buf, s_buf, rho_buf, mask_ref, in_sems, sems):
    sources = (u_hbm, v_hbm, k_hbm)
    held = (u_ref, v_ref, k_ref)

    def copy_in(t, index):
        rows = pl.ds(pl.multiple_of(index * 8, 8), 8)
        return pltpu.make_async_copy(sources[t].at[:, rows, :], held[t].at[:, rows, :], in_sems.at[t, index])

    def start(index, carry):
        for f in range(3):
            copy_in(f, index).start()
        return carry

    mask_copy = pltpu.make_async_copy(mask_hbm, mask_ref, in_sems.at[3, 0])
    start(0, 0)
    mask_copy.start()
    lax.fori_loop(1, STRIPS, start, 0)
    load, load_row = pair_loader((t_ref, s_ref), top_ref)
    halo_setup(is_odd("lon"), is_odd("lat"), (lon_a, lon_b, lat_a, lat_b), (c_lon_a, c_lon_b, c_lat_a, c_lat_b),
               own_ref, load_row, carry_ref, side_ref, north_ref)
    mask_copy.wait()
    bufs = (t_buf, s_buf, rho_buf)
    outs = (t_out, s_out, rho_out)

    def emit(k, strip, new):
        for h in range(2):
            at = (k, pl.ds(strip, 8), slice(h * LANES, (h + 1) * LANES))
            for t in range(2):
                bufs[t][at] = new[t][h]
            rho_buf[at] = density_of(new[0][h], new[1][h])

    def copies(index):
        rows = pl.ds(pl.multiple_of(index * 16, 16), 16)
        return [
            pltpu.make_async_copy(bufs[n].at[:, rows, :], outs[n].at[:, rows, :], sems.at[n, index])
            for n in range(3)
        ]

    def body(strip, last):
        index = STRIPS - 1 if last else strip // 8
        for f in range(3):
            copy_in(f, index).wait()
        step_strip(strip, last, load, u_ref, v_ref, k_ref, mask_ref, side_ref, north_ref, carry_ref, emit, heat_ref)

        def send():
            for copy in copies(index // 2):
                copy.start()

        if last:
            send()
        else:
            pl.when(lax.rem(index, 2) == 1)(send)

    strips(body)

    def finish(index, carry):
        for copy in copies(index):
            copy.wait()
        return carry

    lax.fori_loop(0, STRIPS // 2, finish, 0)


def second_step(t, s, fields, mask, top, heat, own, got, coefs):
    shape = jax.ShapeDtypeStruct((LEVELS, ROWS, 2 * LANES), F32)
    buf = pltpu.VMEM((LEVELS, ROWS, 2 * LANES), F32)
    return pl.pallas_call(
        second_kernel,
        out_shape=(shape, shape, shape),
        in_specs=[VM] * 2 + [ANY] * 4 + [VM] * 11,
        out_specs=(ANY, ANY, ANY),
        scratch_shapes=STEP_SCRATCH
        + [buf] * 6
        + [pltpu.VMEM((ROWS, 2 * LANES), jnp.int32), pltpu.SemaphoreType.DMA((4, STRIPS)), pltpu.SemaphoreType.DMA((3, STRIPS // 2))],
        compiler_params=pltpu.CompilerParams(vmem_limit_bytes=LIMIT),
        cost_estimate=STEP_COST,
        name="second_step",
    )(in_vmem(t), in_vmem(s), *[in_hbm(x) for x in fields], in_hbm(mask), in_vmem(top), in_vmem(heat), in_vmem(own), *[in_vmem(g) for g in got], *coefs)


def body(
    temp,
    salt,
    east_face_velocity,
    v_face,
    kappa,
    land_mask,
    margin_owner_device,
    margin_cell,
    margin_weight,
    air_temp,
    wind_speed,
):
    def lists(x):
        return jnp.transpose(x.reshape(256, 2))

    fields = (temp, salt, east_face_velocity, v_face, kappa)
    request, codes = make_request(
        lists(margin_owner_device), lists(margin_cell), lists(margin_weight), temp
    )
    request = request.reshape(128, 1, GROUP * LANES)
    got = lax.all_to_all(request, AXES, split_axis=0, concat_axis=0, tiled=True)
    got = got.reshape(128 * GROUP, LANES)
    *sent, own = make_edges(fields, codes)
    halos = [in_vmem(g) for g in exchange(*sent)]
    answer = make_answer(
        got, air_temp.reshape(256, LANES), wind_speed.reshape(256, LANES), halos
    )
    back = lax.all_to_all(answer, AXES, split_axis=0, concat_axis=0, tiled=True)
    t1, s1, *edges = first_step(fields, land_mask, in_vmem(own), halos)
    s1, heat, top, *sent, own = add_heat(s1, *edges, land_mask, back, codes)
    later = exchange(*sent)
    return second_step(t1, s1, fields[2:], land_mask, top, heat, own, later, halos)


def solution(mesh):
    grid = P(None, "lat", "lon")
    lists = P("lat", "lon", None, None)
    owned = P("lon", "lat", None, None)
    in_specs = (grid,) * 5 + (P("lat", "lon"),) + (lists,) * 3 + (owned,) * 2
    return jax.shard_map(body, mesh=mesh, in_specs=in_specs, out_specs=(grid,) * 3, check_vma=False)
```

```python
import jax
import jax.numpy as jnp
from jax import lax
from jax.experimental import pallas as pl
from jax.experimental.pallas import tpu as pltpu
from jax.sharding import PartitionSpec as P

F32 = jnp.float32
BF16 = jnp.bfloat16
AXES = ("lon", "lat")
BULK = 0.1
SLOTS = 8
GROUP = SLOTS + 1
LEVELS = 16
ROWS = 128
LANES = 128
STRIPS = ROWS // 8
LIMIT = 24 * 1024 * 1024

VM = pl.BlockSpec(memory_space=pltpu.VMEM)
ANY = pl.BlockSpec(memory_space=pl.ANY)


def in_vmem(x):
    return pltpu.with_memory_space_constraint(x, pltpu.VMEM)


def dot(a, b):
    return jnp.dot(a, b, preferred_element_type=F32)


def dot_nt(a, b):
    return lax.dot_general(a, b, (((1,), (1,)), ((), ())), preferred_element_type=F32)


def pieces(x):
    high = x.astype(BF16)
    rest = x - high.astype(F32)
    middle = rest.astype(BF16)
    low = (rest - middle.astype(F32)).astype(BF16)
    return high, middle, low


def pick(onehot, x):
    high, middle, low = pieces(x)
    return dot(onehot, high) + (dot(onehot, middle) + dot(onehot, low))


def iota(shape, dim):
    return lax.broadcasted_iota(jnp.int32, shape, dim)


def roll(x, steps, axis):
    steps = steps % x.shape[axis]
    return x if steps == 0 else pltpu.roll(x, steps, axis)


def as_bf16(flag):
    return flag.astype(F32).astype(BF16)


def make_lists(owner_ref, cell_ref, weight_ref):
    w = weight_ref[...]
    share = w / (w[0:1] + w[1:2])
    before = iota((256, 256), 0)
    after = iota((256, 256), 1)
    perm = as_bf16(before == (after % ROWS) * 2 + after // ROWS)
    lists = jnp.concatenate([owner_ref[...].astype(F32), cell_ref[...].astype(F32)], axis=0)
    lists = dot(lists.astype(BF16), perm)
    share = pick_left(share, perm)
    owner = [lists[m : m + 1].astype(jnp.int32) for m in range(2)]
    cell = [lists[2 + m : 3 + m] for m in range(2)]
    return owner, cell, share


def write_request(owner, cell, share, surface, out_ref, codes_ref):
    device = iota((128, 256), 0)
    named = [as_bf16(device == owner[m]) for m in range(2)]
    earlier = as_bf16(iota((256, 256), 0) < iota((256, 256), 1))
    ones = jnp.ones((256, 256), BF16)
    ahead = [dot(named[0], earlier), dot(named[1], earlier) + dot(named[0], ones)]
    rank = [
        jnp.sum(named[m].astype(F32) * ahead[m], axis=0, keepdims=True).astype(jnp.int32)
        for m in range(2)
    ]
    slot = iota((128, 256), 0)
    ids = sum(
        dot_nt(named[m], jnp.where(slot == rank[m], cell[m], 0.0).astype(BF16)) for m in range(2)
    )
    total = 128 * GROUP
    line = iota((total, 256), 0)
    place = as_bf16(
        (line == owner[0] * GROUP + rank[0]) | (line == owner[1] * GROUP + rank[1])
    )
    id_place = as_bf16(iota((total, 128), 0) == iota((total, 128), 1) * GROUP + SLOTS)
    blocks = jnp.concatenate([surface[:, :LANES], surface[:, LANES:]], axis=0)
    out_ref[...] = pick(place, blocks) + dot(id_place, ids.astype(BF16))
    table = jnp.concatenate(
        [(owner[m] * SLOTS + rank[m]).astype(F32) for m in range(2)]
        + [share, jnp.zeros((124, 256), F32)],
        axis=0,
    )
    codes_ref[...] = jnp.transpose(table)


def request_kernel(owner_ref, cell_ref, weight_ref, surface_ref, out_ref, codes_ref):
    owner, cell, share = make_lists(owner_ref, cell_ref, weight_ref)
    write_request(owner, cell, share, surface_ref[...], out_ref, codes_ref)


def in_hbm(x):
    return pltpu.with_memory_space_constraint(x, pltpu.HBM)


def make_request(owner, cell, weight, temp):
    return pl.pallas_call(
        request_kernel,
        out_shape=(pltpu.VMEM((128 * GROUP, LANES), F32), pltpu.VMEM((256, LANES), F32)),
        grid=(1,),
        in_specs=[pl.BlockSpec((2, 256), lambda i: (0, 0))] * 3
        + [pl.BlockSpec((None, ROWS, 2 * LANES), lambda i: (0, 0, 0))],
        out_specs=(VM,) * 2,
        compiler_params=pltpu.CompilerParams(vmem_limit_bytes=LIMIT),
        cost_estimate=pl.CostEstimate(flops=5 * 10**8, bytes_accessed=2**20, transcendentals=0),
        name="request",
    )(*[in_hbm(x) for x in (owner, cell, weight, temp)])


def pick_left(x, onehot):
    high, middle, low = pieces(x)
    return dot(high, onehot) + (dot(middle, onehot) + dot(low, onehot))


def edges_kernel(t_ref, s_ref, u_ref, v_ref, k_ref, _,
                 lon_a_ref, lon_b_ref, lat_a_ref, lat_b_ref, west_ref,
                 t_buf, s_buf, u_buf, k_buf, v_row, k_row, sems, more_sems):
    last = pl.ds(ROWS - 8, 8)
    rows = [
        pltpu.make_async_copy(v_ref.at[:, last, :], v_row, more_sems.at[0]),
        pltpu.make_async_copy(k_ref.at[:, last, :], k_row, more_sems.at[1]),
    ]
    eastern = pl.ds(LANES, LANES)

    copies = [
        pltpu.make_async_copy(t_ref, t_buf, sems.at[0]),
        pltpu.make_async_copy(s_ref, s_buf, sems.at[1]),
        pltpu.make_async_copy(u_ref.at[:, :, eastern], u_buf, sems.at[2]),
        pltpu.make_async_copy(k_ref.at[:, :, eastern], k_buf, sems.at[3]),
    ]
    for copy in copies + rows:
        copy.start()
    odd = is_odd("lon")
    columns = Columns(ROWS)
    for t, ref in enumerate((t_buf, s_buf)):
        copies[t].wait()
        for k in range(LEVELS):
            columns.add_west(LEVELS * t + k, ref[k, :, :LANES])
        for k in range(LEVELS):
            columns.add_east(LEVELS * t + k, ref[k, :, LANES:])
    for f, ref in enumerate((u_buf, k_buf)):
        copies[2 + f].wait()
        for k in range(LEVELS):
            columns.add_east(64 + LEVELS * f + k, ref[k])
    west, east = columns.west, with_faces(columns)
    west_ref[...] = west
    lon_a_ref[...] = jnp.where(odd, west, east)
    lon_b_ref[...] = jnp.where(odd, east, west)
    for copy in rows:
        copy.wait()
    south = jnp.concatenate(
        [ref[k, 0:1, :] for ref in (t_buf, s_buf) for k in range(LEVELS)], axis=0
    )
    north = jnp.concatenate(
        [ref[k, ROWS - 1 : ROWS, :] for ref in (t_buf, s_buf) for k in range(LEVELS)], axis=0
    )
    faces = jnp.concatenate(
        [ref[k, 7:8, :] for ref in (v_row, k_row) for k in range(LEVELS)], axis=0
    )
    send_rows(south, north, lat_a_ref, lat_b_ref)
    lat_a_ref[32:64, :] = faces
    lat_b_ref[32:64, :] = faces


def send_rows(south, north, lat_a_ref, lat_b_ref):
    odd = is_odd("lat")
    top = lax.axis_index("lat") == lax.axis_size("lat") - 1
    lat_a_ref[0:32, :] = jnp.where(odd, south, north)
    lat_b_ref[0:32, :] = jnp.where(odd, jnp.where(top, flipped(north), north), south)


def make_edges(fields, after):
    field = pltpu.VMEM((LEVELS, ROWS, 2 * LANES), F32)
    half = pltpu.VMEM((LEVELS, ROWS, LANES), F32)
    row = pltpu.VMEM((LEVELS, 8, 2 * LANES), F32)
    return pl.pallas_call(
        edges_kernel,
        out_shape=(
            pltpu.VMEM((ROWS, LANES), F32),
            pltpu.VMEM((ROWS, LANES), F32),
            pltpu.VMEM((64, 2 * LANES), F32),
            pltpu.VMEM((64, 2 * LANES), F32),
            pltpu.VMEM((ROWS, LANES), F32),
        ),
        in_specs=[ANY] * 6,
        out_specs=(VM,) * 5,
        scratch_shapes=[
            field, field, half, half, row, row,
            pltpu.SemaphoreType.DMA((4,)),
            pltpu.SemaphoreType.DMA((2,)),
        ],
        compiler_params=pltpu.CompilerParams(vmem_limit_bytes=LIMIT),
        cost_estimate=pl.CostEstimate(flops=10**8, bytes_accessed=8 * 2**20, transcendentals=0),
        name="edges",
    )(*[in_hbm(x) for x in fields], after)


def answer_kernel(got_ref, air_ref, wind_ref, *rest):
    out_ref = rest[-1]
    ids = got_ref[pl.ds(SLOTS, 128, stride=GROUP), :].astype(BF16)
    patches = jnp.concatenate([air_ref[...], wind_ref[...]], axis=1)
    high, middle, low = pieces(patches)
    spread = jnp.ones((128, 256), BF16)
    chunk = 512
    for part in range(2):
        line = iota((chunk, 128), 0) + part * chunk
        lane = iota((chunk, 128), 1)
        rows = dot(as_bf16(line // SLOTS == lane), ids)
        rows = jnp.where(lane == line % SLOTS, rows, 0.0)
        wanted = dot(rows.astype(BF16), spread).astype(jnp.int32)
        onehot = as_bf16(wanted == iota((chunk, 256), 1))
        found = dot(onehot, high) + (dot(onehot, middle) + dot(onehot, low))
        for s in range(chunk // SLOTS):
            source = part * (chunk // SLOTS) + s
            cells = got_ref[source * GROUP : source * GROUP + SLOTS, :]
            here = found[s * SLOTS : (s + 1) * SLOTS]
            out_ref[source * SLOTS : (source + 1) * SLOTS, :] = (
                BULK * here[:, LANES:] * (here[:, :LANES] - cells)
            )


def make_answer(got, air, wind, after):
    return pl.pallas_call(
        answer_kernel,
        out_shape=pltpu.VMEM((128 * SLOTS, LANES), F32),
        in_specs=[VM] * 3 + [ANY] * len(after),
        out_specs=VM,
        compiler_params=pltpu.CompilerParams(vmem_limit_bytes=LIMIT),
        cost_estimate=pl.CostEstimate(flops=2 * 10**9, bytes_accessed=2**20, transcendentals=0),
        name="answer",
    )(in_vmem(got), air, wind, *after)


def is_odd(axis):
    return lax.rem(lax.axis_index(axis), 2) == 1


def flipped(x):
    back = as_bf16(iota((256, 256), 0) + iota((256, 256), 1) == 255)
    return pick_left(x, back)


class Columns:
    def __init__(self, rows):
        self.lane = iota((rows, LANES), 1)
        self.west = jnp.zeros((rows, LANES), F32)
        self.east = jnp.zeros((rows, LANES), F32)

    def add_west(self, at, x):
        self.west = jnp.where(self.lane == at, roll(x, at, 1), self.west)

    def add_east(self, at, x):
        self.east = jnp.where(self.lane == at, roll(x, at - 127, 1), self.east)


def with_faces(columns):
    faces = jnp.where(columns.lane >= 64, columns.east, 0.0)
    tracers_east = jnp.where(columns.lane < 64, columns.east, 0.0)
    u = jnp.where(columns.lane < 80, faces, 0.0)
    d = faces - u
    u = roll(u, -32, 1)
    d = roll(d, -16, 1)
    east = tracers_east + (u + roll(u, 16, 1)) + (d + roll(d, 16, 1))
    return east


def swap_pairs(first, count):
    route = []
    for low in range(first, count - 1, 2):
        route += [(low, low + 1), (low + 1, low)]
    return route


def exchange(lon_a, lon_b, lat_a, lat_b):
    n_lon, n_lat = lax.axis_size("lon"), lax.axis_size("lat")
    ring = swap_pairs(1, n_lon) + [(n_lon - 1, 0), (0, n_lon - 1)]
    got_lon_a = lax.ppermute(lon_a, "lon", swap_pairs(0, n_lon))
    got_lon_b = lax.ppermute(lon_b, "lon", ring)
    got_lat_a = lax.ppermute(lat_a, "lat", swap_pairs(0, n_lat))
    route = [
        (i * n_lat + low, i * n_lat + high) for i in range(n_lon) for low, high in swap_pairs(1, n_lat)
    ]
    route += [(i * n_lat + n_lat - 1, (n_lon - 1 - i) * n_lat + n_lat - 1) for i in range(n_lon)]
    got_lat_b = lax.ppermute(lat_b, AXES, route)
    return got_lon_a, got_lon_b, got_lat_a, got_lat_b


def density_of(t, s):
    return t * (-0.25 - 0.04 * t + 0.03 * s) + 0.8 * s


def twice_density(t, s):
    return t * (-0.5 - 0.08 * t + 0.06 * s) + 1.6 * s


def step_strip(strip, last, load, u_ref, v_ref, k_ref, mask_ref, side_ref, north_ref, carry_ref, emit, heat_ref=None):
    rows = pl.ds(strip, 8)
    lane = iota((8, LANES), 1)
    sub = iota((8, LANES), 0)
    first_lane, last_lane = lane == 0, lane == LANES - 1
    row0, row7 = sub == 0, sub == 7
    halves = (slice(0, LANES), slice(LANES, 2 * LANES))
    mask = [mask_ref[rows, h].astype(F32) for h in halves]
    x = [load(t, 0, strip) for t in range(2)]
    rho = [twice_density(x[0][h], x[1][h]) for h in range(2)]
    below = None
    for k in range(LEVELS):
        if k < LEVELS - 1:
            x_next = [load(t, k + 1, strip) for t in range(2)]
            rho_next = [twice_density(x_next[0][h], x_next[1][h]) for h in range(2)]
            mixing = [0.06 + 0.05 * jnp.tanh(rho[h] - rho_next[h]) for h in range(2)]
        u = [u_ref[k, rows, h] for h in halves]
        v = [v_ref[k, rows, h] for h in halves]
        d = [k_ref[k, rows, h] for h in halves]
        pe = [jnp.maximum(u[h], 0.0) + d[h] for h in range(2)]
        ne = [jnp.minimum(u[h], 0.0) - d[h] for h in range(2)]
        pn = [jnp.maximum(v[h], 0.0) + d[h] for h in range(2)]
        nn = [jnp.minimum(v[h], 0.0) - d[h] for h in range(2)]
        above = [None, None]
        new = [None, None]
        for t in range(2):
            at = LEVELS * t + k
            xt = x[t]
            side = side_ref[at, rows, :]
            y = [roll(xt[h], -1, 1) for h in range(2)]
            xe = [
                jnp.where(last_lane, y[1], y[0]),
                jnp.where(last_lane, side, y[1]),
            ]
            east = [pe[h] * xt[h] + ne[h] * xe[h] for h in range(2)]
            z = [roll(east[h], 1, 1) for h in range(2)]
            west = [
                jnp.where(first_lane, side, z[0]),
                jnp.where(first_lane, z[0], z[1]),
            ]
            if last:
                ahead = [jnp.broadcast_to(north_ref[at : at + 1, h], (8, LANES)) for h in halves]
            else:
                ahead = load(t, k, strip + 8)
            xn = [roll(jnp.where(row0, ahead[h], xt[h]), -1, 0) for h in range(2)]
            north = [pn[h] * xt[h] + nn[h] * xn[h] for h in range(2)]
            south = [
                roll(jnp.where(row7, carry_ref[at, :, halves[h]], north[h]), 1, 0) for h in range(2)
            ]
            if not last:
                for h in range(2):
                    carry_ref[at, :, halves[h]] = north[h]
            tend = [(west[h] - east[h]) + (south[h] - north[h]) for h in range(2)]
            if k < LEVELS - 1:
                above[t] = [mixing[h] * (x_next[t][h] - xt[h]) for h in range(2)]
                tend = [tend[h] + above[t][h] for h in range(2)]
            if k > 0:
                tend = [tend[h] - below[t][h] for h in range(2)]
            if heat_ref is not None and t == 0 and k == 0:
                tend = [tend[h] + heat_ref[rows, halves[h]] for h in range(2)]
            new[t] = [xt[h] + mask[h] * tend[h] for h in range(2)]
        emit(k, strip, new)
        below = above
        if k < LEVELS - 1:
            x, rho = x_next, rho_next


def west_fluxes(west, coef, own):
    u = roll(coef, -32, 1)
    d = roll(coef, -64, 1)
    return (jnp.maximum(u, 0.0) + d) * west + (jnp.minimum(u, 0.0) - d) * own


def first_carry(south, faces, load_row, carry_ref):
    for k in range(LEVELS):
        v, d = faces(k), faces(LEVELS + k)
        pn = jnp.maximum(v, 0.0) + d
        nn = jnp.minimum(v, 0.0) - d
        for t in range(2):
            at = LEVELS * t + k
            flux = pn * south(at) + nn * load_row(t, k)
            carry_ref[at] = jnp.broadcast_to(flux, (8, 2 * LANES))


def halo_setup(odd_lon, odd_lat, got, coefs, own_ref, load_row, carry_ref, side_ref, north_ref):
    lon_a, lon_b, lat_a, lat_b = got
    c_lon_a, c_lon_b, c_lat_a, c_lat_b = coefs
    west = jnp.where(odd_lon, lon_a[...], lon_b[...])
    coef = jnp.where(odd_lon, c_lon_a[...], c_lon_b[...])
    flux = west_fluxes(west, coef, own_ref[...])
    east = jnp.where(odd_lon, lon_b[...], lon_a[...])
    last_lane = iota((ROWS, LANES), 1) == LANES - 1
    for at in range(2 * LEVELS):
        side_ref[at] = jnp.where(last_lane, roll(east, 127 - at, 1), roll(flux, -at, 1))
    north_ref[...] = jnp.where(odd_lat, lat_b[0:32, :], lat_a[0:32, :])

    def south(at):
        return jnp.where(odd_lat, lat_a[at : at + 1, :], lat_b[at : at + 1, :])

    def faces(at):
        return jnp.where(odd_lat, c_lat_a[32 + at : 33 + at, :], c_lat_b[32 + at : 33 + at, :])

    first_carry(south, faces, load_row, carry_ref)


def pair_loader(refs, top_ref=None):
    def load(t, k, strip):
        rows = pl.ds(strip, 8)
        if t == 0 and k == 0 and top_ref is not None:
            return [top_ref[rows, :LANES], top_ref[rows, LANES:]]
        return [refs[t][k, rows, :LANES], refs[t][k, rows, LANES:]]

    def load_row(t, k):
        if t == 0 and k == 0 and top_ref is not None:
            return top_ref[0:1, :]
        return refs[t][k, 0:1, :]

    return load, load_row


def strips(body):
    def one(i, carry):
        body(pl.multiple_of(i * 8, 8), False)
        return carry

    lax.fori_loop(0, ROWS // 8 - 1, one, 0)
    body(ROWS - 8, True)


def first_kernel(t_hbm, s_hbm, u_hbm, v_hbm, k_hbm, mask_hbm, own_ref, lon_a, lon_b, lat_a, lat_b,
                 t_new, s_out, top_out, west_out, east_out, south_out, north_out,
                 carry_ref, side_ref, north_ref,
                 t_ref, s_ref, u_ref, v_ref, k_ref, s_new, mask_ref, sems, out_sems):
    sources = (t_hbm, s_hbm, u_hbm, v_hbm, k_hbm)
    bufs = (t_ref, s_ref, u_ref, v_ref, k_ref)
    new_bufs = (t_new, s_new)

    def copy_in(f, index):
        rows = pl.ds(pl.multiple_of(index * 8, 8), 8)
        return pltpu.make_async_copy(sources[f].at[:, rows, :], bufs[f].at[:, rows, :], sems.at[f, index])

    def copy_out(index):
        rows = pl.ds(pl.multiple_of(index * 8, 8), 8)
        return pltpu.make_async_copy(s_new.at[:, rows, :], s_out.at[:, rows, :], out_sems.at[index])

    def start(index, carry):
        for f in range(5):
            copy_in(f, index).start()
        return carry

    mask_copy = pltpu.make_async_copy(mask_hbm, mask_ref, sems.at[5, 0])
    start(0, 0)
    mask_copy.start()
    lax.fori_loop(1, STRIPS, start, 0)
    copy_in(0, 0).wait()
    copy_in(1, 0).wait()
    load, load_row = pair_loader((t_ref, s_ref))
    got = (lon_a, lon_b, lat_a, lat_b)
    halo_setup(is_odd("lon"), is_odd("lat"), got, got, own_ref, load_row, carry_ref, side_ref, north_ref)
    mask_copy.wait()

    def body(strip, last):
        index = STRIPS - 1 if last else strip // 8
        for f in range(2, 5):
            copy_in(f, index).wait()
        if not last:
            for f in range(2):
                copy_in(f, index + 1).wait()
        columns = Columns(8)

        def emit(k, strip, new):
            rows = pl.ds(strip, 8)
            for t in range(2):
                for h in range(2):
                    new_bufs[t][k, rows, h * LANES : (h + 1) * LANES] = new[t][h]
                    if t == 0 and k == 0:
                        top_out[rows, h * LANES : (h + 1) * LANES] = new[t][h]
                columns.add_west(LEVELS * t + k, new[t][0])
                columns.add_east(LEVELS * t + k, new[t][1])

        step_strip(strip, last, load, u_ref, v_ref, k_ref, mask_ref, side_ref, north_ref, carry_ref, emit)
        west_out[pl.ds(strip, 8), :] = columns.west
        east_out[pl.ds(strip, 8), :] = columns.east
        copy_out(index).start()

    strips(body)
    south_out[...] = jnp.concatenate([ref[k, 0:1, :] for ref in new_bufs for k in range(LEVELS)], axis=0)
    north_out[...] = jnp.concatenate(
        [ref[k, ROWS - 1 : ROWS, :] for ref in new_bufs for k in range(LEVELS)], axis=0
    )

    def finish(index, carry):
        copy_out(index).wait()
        return carry

    lax.fori_loop(0, STRIPS, finish, 0)


STEP_SCRATCH = [
    pltpu.VMEM((2 * LEVELS, 8, 2 * LANES), F32),
    pltpu.VMEM((2 * LEVELS, ROWS, LANES), F32),
    pltpu.VMEM((2 * LEVELS, 2 * LANES), F32),
]
STEP_COST = pl.CostEstimate(flops=7 * 10**7, bytes_accessed=25 * 2**20, transcendentals=10**6)


def first_step(fields, mask, own, got):
    shape = pltpu.HBM((LEVELS, ROWS, 2 * LANES), F32)
    buf = pltpu.VMEM((LEVELS, ROWS, 2 * LANES), F32)
    return pl.pallas_call(
        first_kernel,
        out_shape=(
            buf,
            shape,
            pltpu.VMEM((ROWS, 2 * LANES), F32),
            pltpu.VMEM((ROWS, LANES), F32),
            pltpu.VMEM((ROWS, LANES), F32),
            pltpu.VMEM((2 * LEVELS, 2 * LANES), F32),
            pltpu.VMEM((2 * LEVELS, 2 * LANES), F32),
        ),
        in_specs=[ANY] * 6 + [VM] * 5,
        out_specs=(VM, ANY) + (VM,) * 5,
        scratch_shapes=STEP_SCRATCH
        + [buf] * 6
        + [pltpu.VMEM((ROWS, 2 * LANES), jnp.int32), pltpu.SemaphoreType.DMA((6, STRIPS)), pltpu.SemaphoreType.DMA((STRIPS,))],
        compiler_params=pltpu.CompilerParams(vmem_limit_bytes=LIMIT),
        cost_estimate=STEP_COST,
        name="first_step",
    )(*[in_hbm(x) for x in fields], in_hbm(mask), own, *got)


def heat_kernel(top_ref, west_ref, east_ref, south_ref, north_ref, mask_hbm, s1_hbm, back_ref, codes_ref,
                s1_out, heat_out, top_out, lon_a_ref, lon_b_ref, lat_a_ref, lat_b_ref, own_out, mask_ref, sems):
    mask_copy = pltpu.make_async_copy(mask_hbm, mask_ref, sems.at[0])
    mask_copy.start()
    move = pltpu.make_async_copy(s1_hbm, s1_out, sems.at[1])
    move.start()
    high, middle, low = pieces(back_ref[...])
    codes = codes_ref[...]
    lane = iota((256, 1024), 1)
    onehot = jnp.concatenate(
        [as_bf16(codes[:, m : m + 1].astype(jnp.int32) == lane) for m in range(2)], axis=0
    )
    upper = dot(onehot, jnp.concatenate([high, middle], axis=1))
    flux = upper[:, :LANES] + (upper[:, LANES:] + dot(onehot, low))
    heat = codes[:, 2:3] * flux[:256] + codes[:, 3:4] * flux[256:]
    mask_copy.wait()
    mask = mask_ref[...].astype(F32)
    added = []
    for h in range(2):
        cols = slice(h * LANES, (h + 1) * LANES)
        here = heat[h * ROWS : (h + 1) * ROWS]
        heat_out[:, cols] = here
        added.append(mask[:, cols] * here)
        top_out[:, cols] = top_ref[:, cols] + added[h]
    first = iota((ROWS, LANES), 1) == 0
    west = west_ref[...] + jnp.where(first, added[0], 0.0)
    east = east_ref[...] + jnp.where(first, roll(added[1], 1, 1), 0.0)
    own_out[...] = west
    odd = is_odd("lon")
    lon_a_ref[...] = jnp.where(odd, west, east)
    lon_b_ref[...] = jnp.where(odd, east, west)
    south = jnp.concatenate([top_out[0:1, :], south_ref[1:, :]], axis=0)
    north = jnp.concatenate([top_out[ROWS - 1 : ROWS, :], north_ref[1:, :]], axis=0)
    send_rows(south, north, lat_a_ref, lat_b_ref)
    move.wait()


def add_heat(s1, top, west, east, south, north, mask, back, codes):
    field = pltpu.VMEM((LEVELS, ROWS, 2 * LANES), F32)
    return pl.pallas_call(
        heat_kernel,
        out_shape=(
            field,
            pltpu.VMEM((ROWS, 2 * LANES), F32),
            pltpu.VMEM((ROWS, 2 * LANES), F32),
            pltpu.VMEM((ROWS, LANES), F32),
            pltpu.VMEM((ROWS, LANES), F32),
            pltpu.VMEM((32, 2 * LANES), F32),
            pltpu.VMEM((32, 2 * LANES), F32),
            pltpu.VMEM((ROWS, LANES), F32),
        ),
        in_specs=[VM] * 5 + [ANY] * 2 + [VM] * 2,
        out_specs=(VM,) * 8,
        scratch_shapes=[
            pltpu.VMEM((ROWS, 2 * LANES), jnp.int32),
            pltpu.SemaphoreType.DMA((2,)),
        ],
        compiler_params=pltpu.CompilerParams(vmem_limit_bytes=LIMIT),
        cost_estimate=pl.CostEstimate(flops=10**9, bytes_accessed=2**20, transcendentals=0),
        name="heat",
    )(*[in_vmem(x) for x in (top, west, east, south, north)], in_hbm(mask), in_hbm(s1), in_vmem(back), in_vmem(codes))


def second_kernel(t_ref, s_ref, u_hbm, v_hbm, k_hbm, mask_hbm, top_ref, heat_ref, own_ref,
                  lon_a, lon_b, lat_a, lat_b, c_lon_a, c_lon_b, c_lat_a, c_lat_b,
                  t_out, s_out, rho_out,
                  carry_ref, side_ref, north_ref,
                  u_ref, v_ref, k_ref, t_buf, s_buf, rho_buf, mask_ref, in_sems, sems):
    sources = (u_hbm, v_hbm, k_hbm)
    held = (u_ref, v_ref, k_ref)

    def copy_in(t, index):
        rows = pl.ds(pl.multiple_of(index * 8, 8), 8)
        return pltpu.make_async_copy(sources[t].at[:, rows, :], held[t].at[:, rows, :], in_sems.at[t, index])

    def start(index, carry):
        for f in range(3):
            copy_in(f, index).start()
        return carry

    mask_copy = pltpu.make_async_copy(mask_hbm, mask_ref, in_sems.at[3, 0])
    start(0, 0)
    mask_copy.start()
    lax.fori_loop(1, STRIPS, start, 0)
    load, load_row = pair_loader((t_ref, s_ref), top_ref)
    halo_setup(is_odd("lon"), is_odd("lat"), (lon_a, lon_b, lat_a, lat_b), (c_lon_a, c_lon_b, c_lat_a, c_lat_b),
               own_ref, load_row, carry_ref, side_ref, north_ref)
    mask_copy.wait()
    bufs = (t_buf, s_buf, rho_buf)
    outs = (t_out, s_out, rho_out)

    def emit(k, strip, new):
        for h in range(2):
            at = (k, pl.ds(strip, 8), slice(h * LANES, (h + 1) * LANES))
            for t in range(2):
                bufs[t][at] = new[t][h]
            rho_buf[at] = density_of(new[0][h], new[1][h])

    def copies(index):
        rows = pl.ds(pl.multiple_of(index * 16, 16), 16)
        return [
            pltpu.make_async_copy(bufs[n].at[:, rows, :], outs[n].at[:, rows, :], sems.at[n, index])
            for n in range(3)
        ]

    def body(strip, last):
        index = STRIPS - 1 if last else strip // 8
        for f in range(3):
            copy_in(f, index).wait()
        step_strip(strip, last, load, u_ref, v_ref, k_ref, mask_ref, side_ref, north_ref, carry_ref, emit, heat_ref)

        def send():
            for copy in copies(index // 2):
                copy.start(priority=1)

        if last:
            send()
        else:
            pl.when(lax.rem(index, 2) == 1)(send)

    strips(body)

    def finish(index, carry):
        for copy in copies(index):
            copy.wait()
        return carry

    lax.fori_loop(0, STRIPS // 2, finish, 0)


def second_step(t, s, fields, mask, top, heat, own, got, coefs):
    shape = jax.ShapeDtypeStruct((LEVELS, ROWS, 2 * LANES), F32)
    buf = pltpu.VMEM((LEVELS, ROWS, 2 * LANES), F32)
    return pl.pallas_call(
        second_kernel,
        out_shape=(shape, shape, shape),
        in_specs=[VM] * 2 + [ANY] * 4 + [VM] * 11,
        out_specs=(ANY, ANY, ANY),
        scratch_shapes=STEP_SCRATCH
        + [buf] * 6
        + [pltpu.VMEM((ROWS, 2 * LANES), jnp.int32), pltpu.SemaphoreType.DMA((4, STRIPS)), pltpu.SemaphoreType.DMA((3, STRIPS // 2))],
        compiler_params=pltpu.CompilerParams(vmem_limit_bytes=LIMIT),
        cost_estimate=STEP_COST,
        name="second_step",
    )(in_vmem(t), in_vmem(s), *[in_hbm(x) for x in fields], in_hbm(mask), in_vmem(top), in_vmem(heat), in_vmem(own), *[in_vmem(g) for g in got], *coefs)


def body(
    temp,
    salt,
    east_face_velocity,
    v_face,
    kappa,
    land_mask,
    margin_owner_device,
    margin_cell,
    margin_weight,
    air_temp,
    wind_speed,
):
    def lists(x):
        return jnp.transpose(x.reshape(256, 2))

    fields = (temp, salt, east_face_velocity, v_face, kappa)
    request, codes = make_request(
        lists(margin_owner_device), lists(margin_cell), lists(margin_weight), temp
    )
    request = request.reshape(128, 1, GROUP * LANES)
    got = lax.all_to_all(request, AXES, split_axis=0, concat_axis=0, tiled=True)
    got = got.reshape(128 * GROUP, LANES)
    *sent, own = make_edges(fields, codes)
    halos = [in_vmem(g) for g in exchange(*sent)]
    answer = make_answer(
        got, air_temp.reshape(256, LANES), wind_speed.reshape(256, LANES), halos
    )
    back = lax.all_to_all(answer, AXES, split_axis=0, concat_axis=0, tiled=True)
    t1, s1, *edges = first_step(fields, land_mask, in_vmem(own), halos)
    s1, heat, top, *sent, own = add_heat(s1, *edges, land_mask, back, codes)
    later = exchange(*sent)
    return second_step(t1, s1, fields[2:], land_mask, top, heat, own, later, halos)


def solution(mesh):
    grid = P(None, "lat", "lon")
    lists = P("lat", "lon", None, None)
    owned = P("lon", "lat", None, None)
    in_specs = (grid,) * 5 + (P("lat", "lon"),) + (lists,) * 3 + (owned,) * 2
    return jax.shard_map(body, mesh=mesh, in_specs=in_specs, out_specs=(grid,) * 3, check_vma=False)
```
